512 devices in a mesh: dp: 64 (over x_lo, z, core), mp: 8 (over x_hi, y).
Axes of the slice: x: 4 (x_hi: 2, x_lo: 2; x = x_hi * 2 + x_lo), y: 4, z: 16, core: 2. Of those that a mesh axis runs over, the one named last changes fastest.
Arguments:
- grads: bfloat16 [32, 8192, 512], P('mp', 'dp'), may hold values from -400 to 400
- block_owner: int32 [8, 4], P('mp'), may hold values from 0 to 63, as said below
- owner_counts: int32 [8, 64], P('mp', 'dp'), may hold values from 0 to 3, as said below
Outputs:
- preconditioned: bfloat16 [32, 8192, 512], P('mp', 'dp')
- owned_factors: bfloat16 [8, 192, 512, 512], P('mp', 'dp')
The draws below stay inside these ranges and needn't reach their ends.
Inputs may be any that keep to these rules, and one draw needn't show every extreme that they name: `block_owner`: for each mp index at most 3 of its 4 blocks share an owner, and in every draw some owner holds exactly 3 blocks of one mp index. owner_counts[m, o] is the number of j with block_owner[m, j] = o.
All inputs are finite; a program needn't handle non-finite values.
Results may differ from the reference program's by a relative error of at most 0.002.
The reference program's roundings to bfloat16 on the way (of `normal` and `factors`) count: a program that leaves them out, or rounds other values in their place, can miss the bound.
Values may be sent and summed in bfloat16 or wider, within the bound.
No kernel may reach another device: no remote copies, remote signals or barrier semaphores. Data moves between devices by JAX's collectives and lax.ppermute only.
A program may use at most 64 MiB of HBM per device.

```python
import jax
import jax.numpy as jnp
from jax import lax

BLK = 512
LAYERS = 2
BPL = 2
NB = 4
CAP = 3
ITERS = 3
ROWS_DEV = 128
ROWS_ALL = 8192
N_DP = 64
N_MP = 8


def permute_blocks(one_key):
    return jax.random.permutation(one_key, NB)


def place_top(one_key, target):
    order = jax.random.permutation(one_key, N_DP).astype(jnp.int32)
    held = order[target]
    order = jnp.where(order == N_DP - 1, held, order)
    order = jnp.where(jnp.arange(N_DP) == target, N_DP - 1, order)
    return order[:NB]


def ownership(key):
    subkeys = jax.random.split(key, 4)
    heavy_counts = jax.random.randint(subkeys[0], (N_MP,), 1, CAP + 1)
    forced = jax.random.randint(subkeys[1], (), 0, N_MP)
    heavy_counts = jnp.where(jnp.arange(N_MP) == forced, CAP, heavy_counts)
    orders = jax.vmap(permute_blocks)(jax.random.split(subkeys[2], N_MP))
    last_used = NB - heavy_counts
    chosen_owners = jax.vmap(place_top)(jax.random.split(subkeys[3], N_MP), last_used)
    position = jnp.arange(NB)
    pick_index = jnp.where(position[None, :] < heavy_counts[:, None], 0, position[None, :] - heavy_counts[:, None] + 1)
    values = jnp.take_along_axis(chosen_owners, pick_index, axis=1)
    result = jnp.zeros((N_MP, NB), jnp.int32).at[jnp.arange(N_MP)[:, None], orders].set(values)
    return result.astype(jnp.int32)


def draw_block_owner(key, part):
    owners_drawn = ownership(key)
    return owners_drawn


def draw_owner_counts(key, part):
    owners_drawn = ownership(key)
    matching = owners_drawn[:, :, None] == jnp.arange(N_DP, dtype=jnp.int32)[None, None, :]
    return jnp.sum(matching.astype(jnp.int32), axis=1)


def draw_grads(key, part):
    key = jax.random.fold_in(key, 11)
    subkeys = jax.random.split(key, 6)
    blocks_all = NB * N_MP
    rows_all = ROWS_DEV * N_DP
    base_noise = jax.random.normal(subkeys[0], (blocks_all, rows_all, BLK), jnp.float32)
    common_weight = 0.6
    column_spread = 1.15
    common_part = jax.random.normal(subkeys[1], (blocks_all, rows_all, 1), jnp.float32)
    row_scale = jnp.exp(jax.random.uniform(subkeys[2], (blocks_all, rows_all, 1), jnp.float32, -0.7, 0.7))
    device_scale = jnp.exp(jax.random.uniform(subkeys[3], (blocks_all, N_DP, 1, 1), jnp.float32, -0.8, 0.8))
    column_scale = jnp.exp(jax.random.uniform(subkeys[4], (blocks_all, 1, BLK), jnp.float32, -column_spread, column_spread))
    block_scale = jnp.exp(jax.random.uniform(subkeys[5], (blocks_all, 1, 1), jnp.float32, -0.7, 0.7))
    values = (base_noise + common_weight * common_part) * row_scale * column_scale * block_scale
    values = (values.reshape(blocks_all, N_DP, ROWS_DEV, BLK) * device_scale).reshape(blocks_all, rows_all, BLK)
    return values.astype(jnp.bfloat16)


def setup_inputs(seed: int = 0) -> dict:
    key_of = jax.random.split(jax.random.key(seed), 4)
    grads = draw_grads(jax.random.fold_in(key_of[3], 71), 0)
    block_owner = draw_block_owner(jax.random.fold_in(key_of[3], 71), 0)
    owner_counts = draw_owner_counts(jax.random.fold_in(key_of[3], 71), 0)
    return dict(grads=grads, block_owner=block_owner, owner_counts=owner_counts)


eps_rel = 0.1

def newton_root(normal, norm_scale):
    identity = jnp.eye(normal.shape[0], dtype=jnp.float32)
    current = lax.optimization_barrier(normal)
    factor = normal
    for iteration in range(ITERS):
        step_matrix = lax.optimization_barrier(((5.0 * identity - current.astype(jnp.float32)) * 0.25).astype(jnp.bfloat16))
        if iteration == 0:
            factor = (norm_scale ** (-0.25) * step_matrix.astype(jnp.float32)).astype(jnp.bfloat16)
        else:
            factor = jnp.dot(factor, step_matrix, preferred_element_type=jnp.float32).astype(jnp.bfloat16)
        if iteration + 1 < ITERS:
            square = jnp.dot(step_matrix, step_matrix, preferred_element_type=jnp.float32).astype(jnp.bfloat16)
            fourth = jnp.dot(square, square, preferred_element_type=jnp.float32).astype(jnp.bfloat16)
            current = lax.optimization_barrier(jnp.dot(fourth, current, preferred_element_type=jnp.float32).astype(jnp.bfloat16))
    return factor

def block_gram(gradient):
    return jnp.dot(gradient.T, gradient, preferred_element_type=jnp.float32) / ROWS_ALL

def apply_factor(operands):
    return jnp.dot(operands[0], operands[1], preferred_element_type=jnp.float32).astype(jnp.bfloat16)

def root_pair(operands):
    return newton_root(operands[0], operands[1])

def slot_fill(operands):
    return jnp.einsum('osj,jxy->osxy', operands[0], operands[1].astype(jnp.float32)).astype(jnp.bfloat16)

def reference(grads, block_owner, owner_counts):
    gram_sums = lax.map(block_gram, grads)
    traces = jnp.trace(gram_sums, axis1=1, axis2=2)
    layer_sums = lax.optimization_barrier(jnp.sum(traces.reshape(N_MP, LAYERS, BPL), axis=(0, 2)))
    layer_damping = eps_rel * layer_sums / (N_MP * BPL * BLK)
    block_damping = jnp.tile(jnp.repeat(layer_damping, BPL), N_MP)
    identity = jnp.eye(BLK, dtype=jnp.float32)
    shifted = gram_sums + block_damping[:, None, None] * identity
    norm_scale = jnp.sqrt(lax.optimization_barrier(jnp.sum(shifted * shifted, axis=(1, 2))))
    normal = (shifted / norm_scale[:, None, None]).astype(jnp.bfloat16)
    factors = lax.map(root_pair, (normal, norm_scale))
    preconditioned = lax.map(apply_factor, (grads, factors))
    position = jnp.arange(NB, dtype=jnp.int32)
    matching = block_owner[:, :, None] == block_owner[:, None, :]
    earlier = position[None, None, :] < position[None, :, None]
    slot_of = lax.optimization_barrier(jnp.sum((matching & earlier).astype(jnp.int32), axis=2))
    owner_range = jnp.arange(N_DP, dtype=jnp.int32)
    slot_range = jnp.arange(CAP, dtype=jnp.int32)
    selection = (block_owner[:, None, None, :] == owner_range[None, :, None, None]) & (slot_of[:, None, None, :] == slot_range[None, None, :, None]) & (slot_range[None, None, :, None] < owner_counts[:, :, None, None])
    weights = selection.astype(jnp.float32)
    column_factors = factors.reshape(N_MP, NB, BLK, BLK)
    owned_stack = lax.map(slot_fill, (weights, column_factors))
    owned_factors = owned_stack.reshape(N_MP, N_DP * CAP, BLK, BLK)
    return (preconditioned, owned_factors)
```

```python
import jax
import jax.numpy as jnp
from jax import lax
from jax.experimental import pallas as pl
from jax.experimental.pallas import tpu as pltpu
from jax.sharding import Mesh
from jax.sharding import PartitionSpec as P

LAYERS = 2
BPL = 2
CAP = 3
ITERS = 3
NB = 4
TILE = 128
CHUNKS = 16
HALF = 64
SENT_ROWS = 80
SUM_ROWS = 72

eps_rel = 0.1

QUAD = ("x", "c")
VMEM = pl.BlockSpec(memory_space=pltpu.VMEM)
SMEM = pl.BlockSpec(memory_space=pltpu.SMEM)
PARAMS = pltpu.CompilerParams(vmem_limit_bytes=40 * 1024 * 1024)
OFF_TILES = ((0, 1), (0, 2), (0, 3), (1, 2), (1, 3), (2, 3))


def row_col():
    rows = lax.broadcasted_iota(jnp.int32, (TILE, TILE), 0)
    cols = lax.broadcasted_iota(jnp.int32, (TILE, TILE), 1)
    return rows, cols


def gram_kernel(a_ref, b_ref, c_ref, d_ref, out_ref):
    gram = None
    for ref in (a_ref, b_ref, c_ref, d_ref):
        rows = ref[...]
        term = lax.dot_general(
            rows, rows, (((0,), (0,)), ((), ())), preferred_element_type=jnp.float32
        )
        gram = term if gram is None else gram + term
    rows, cols = row_col()

    def tile(i, j):
        return gram[i * TILE : (i + 1) * TILE, j * TILE : (j + 1) * TILE]

    tiles = [tile(i, j) for i, j in OFF_TILES]
    for i in (0, 2):
        tiles.append(jnp.where(rows < cols, tile(i, i), tile(i + 1, i + 1)))
    row16 = lax.broadcasted_iota(jnp.int32, (16, TILE), 0)
    extras = []
    for i in range(4):
        diagonal = jnp.sum(jnp.where(rows == cols, tile(i, i), 0.0), axis=0, keepdims=True)
        high = diagonal.astype(jnp.bfloat16).astype(jnp.float32)
        middle = (diagonal - high).astype(jnp.bfloat16).astype(jnp.float32)
        low = diagonal - high - middle
        extras.append(
            jnp.where(row16 == 0, high, jnp.where(row16 == 1, middle, jnp.where(row16 == 2, low, 0.0)))
        )
    for k in range(CHUNKS):
        half = tiles[k // 2][(k % 2) * HALF : (k % 2 + 1) * HALF]
        out_ref[k, :HALF] = half.astype(jnp.bfloat16)
        out_ref[k, HALF:] = extras[k % 4].astype(jnp.bfloat16)


def sum_kernel(parts_ref, squares_ref, out_ref):
    total = parts_ref[0].astype(jnp.float32)
    for k in range(1, CHUNKS):
        total = total + parts_ref[k].astype(jnp.float32)
    diagonal = jnp.sum(total[HALF : HALF + 8], axis=0, keepdims=True)
    squares = jnp.sum(squares_ref[...], axis=0)
    row8 = lax.broadcasted_iota(jnp.int32, (8, TILE), 0)
    out_ref[:HALF] = total[:HALF]
    out_ref[HALF:] = jnp.where(row8 == 7, diagonal, squares)


def root_kernel(total_rows, layer_blocks, chunks_ref, factor_ref, shifted_ref):
    width = factor_ref.shape[0]
    rows, cols = row_col()
    scale = 1.0 / total_rows
    squares = chunks_ref[0, HALF:SUM_ROWS]
    for k in range(1, CHUNKS):
        squares = squares + chunks_ref[k, HALF:SUM_ROWS]
    layer_sums = jnp.sum(squares, axis=1, keepdims=True) * scale
    damping = jnp.where(lax.axis_index("x") == 0, layer_sums[0:1], layer_sums[1:2]) * (
        eps_rel / (layer_blocks * width)
    )

    def stored(t):
        return jnp.concatenate([chunks_ref[2 * t, :HALF], chunks_ref[2 * t + 1, :HALF]], axis=0) * scale

    for t, (i, j) in enumerate(OFF_TILES):
        value = stored(t)
        shifted_ref[i * TILE : (i + 1) * TILE, j * TILE : (j + 1) * TILE] = value
        shifted_ref[j * TILE : (j + 1) * TILE, i * TILE : (i + 1) * TILE] = value.T
    for i in range(4):
        value = stored(6 + i // 2)
        value = jnp.where(rows < cols if i % 2 == 0 else rows > cols, value, 0.0)
        diagonal = chunks_ref[i, SUM_ROWS - 1 : SUM_ROWS] * scale + damping
        value = jnp.where(rows == cols, diagonal, value + value.T)
        shifted_ref[i * TILE : (i + 1) * TILE, i * TILE : (i + 1) * TILE] = value
    shifted = shifted_ref[...]
    square_sum = jnp.sum(jnp.sum(shifted * shifted, axis=0, keepdims=True), axis=1, keepdims=True)
    norm_scale = jnp.sqrt(square_sum)
    current = (shifted / norm_scale).astype(jnp.bfloat16)
    root_scale = 1.0 / jnp.sqrt(jnp.sqrt(norm_scale))
    eye_rows = lax.broadcasted_iota(jnp.int32, (width, width), 0)
    eye_cols = lax.broadcasted_iota(jnp.int32, (width, width), 1)
    five = jnp.where(eye_rows == eye_cols, 5.0, 0.0)

    def mm(a, b):
        return jnp.dot(a, b, preferred_element_type=jnp.float32).astype(jnp.bfloat16)

    factor = None
    for iteration in range(ITERS):
        step = ((five - current.astype(jnp.float32)) * 0.25).astype(jnp.bfloat16)
        if iteration == 0:
            factor = (root_scale * step.astype(jnp.float32)).astype(jnp.bfloat16)
        else:
            factor = mm(factor, step)
        if iteration + 1 < ITERS:
            square = mm(step, step)
            fourth = mm(square, square)
            current = mm(fourth, current)
    factor_ref[...] = factor


def apply_kernel(owner_ref, count_ref, grads_ref, f0_ref, f1_ref, f2_ref, f3_ref, pre_ref, own_ref):
    quad = lax.axis_index("x") * 2 + lax.axis_index("c")
    mine = (lax.axis_index("x") * lax.axis_size("z") + lax.axis_index("z")) * 2 + lax.axis_index("c")
    factors = (f0_ref, f1_ref, f2_ref, f3_ref)
    for k, ref in enumerate(factors):
        block = quad ^ k
        pre_ref[block] = jnp.dot(
            grads_ref[block], ref[...], preferred_element_type=jnp.float32
        ).astype(jnp.bfloat16)
    owners = [owner_ref[0, j] for j in range(NB)]
    slots = []
    for j in range(NB):
        slot = jnp.int32(0)
        for i in range(j):
            slot = slot + (owners[i] == owners[j]).astype(jnp.int32)
        slots.append(slot)
    for s in range(CAP):
        chosen = jnp.int32(-1)
        for j in range(NB):
            held = (owners[j] == mine) & (slots[j] == s) & (s < count_ref[0, 0])
            chosen = jnp.where(held, j ^ quad, chosen)

        @pl.when(chosen < 0)
        def _():
            own_ref[0, s] = jnp.zeros_like(own_ref[0, s])

        for k, ref in enumerate(factors):

            @pl.when(chosen == k)
            def _():
                own_ref[0, s] = ref[...]


def quad_swap(value, k):
    pairs = [(i, i ^ k) for i in range(4)]
    return lax.ppermute(value, QUAD, pairs)


def per_device(grads, block_owner, owner_counts):
    block_count, row_count, block_width = grads.shape
    z_size = lax.axis_size("z")
    total_rows = row_count * lax.axis_size("x") * z_size * lax.axis_size("c")
    quad = lax.axis_index("x") * 2 + lax.axis_index("c")
    outgoing = [lax.dynamic_index_in_dim(grads, quad ^ k, keepdims=False) for k in range(4)]
    held = [outgoing[0]] + [quad_swap(outgoing[k], k) for k in range(1, 4)]
    wide = grads.astype(jnp.float32).reshape(LAYERS, BPL * row_count, block_width // TILE, TILE)
    squares = jnp.sum(wide * wide, axis=(1, 2))
    squares = jnp.pad(squares, ((0, 6), (0, 0)))
    members = 4 * lax.axis_size("m")
    squares = lax.all_to_all(
        jnp.broadcast_to(squares, (members, 8, TILE)), ("x", "c", "m"), 0, 0, tiled=True
    )
    packed = pl.pallas_call(
        gram_kernel,
        out_shape=jax.ShapeDtypeStruct((CHUNKS, SENT_ROWS, TILE), jnp.bfloat16),
        in_specs=[VMEM] * 4,
        out_specs=VMEM,
        compiler_params=PARAMS,
        name="gram",
    )(*held)
    parts = lax.all_to_all(packed, "z", 0, 0, tiled=True)
    chunk = pl.pallas_call(
        sum_kernel,
        out_shape=jax.ShapeDtypeStruct((SUM_ROWS, TILE), jnp.float32),
        in_specs=[VMEM] * 2,
        out_specs=VMEM,
        compiler_params=PARAMS,
        name="sum",
    )(parts, squares)
    chunks = lax.all_gather(chunk, "z")
    factor = pl.pallas_call(
        lambda *refs: root_kernel(total_rows, lax.axis_size("m") * BPL, *refs),
        out_shape=jax.ShapeDtypeStruct((block_width, block_width), jnp.bfloat16),
        in_specs=[VMEM],
        out_specs=VMEM,
        scratch_shapes=[pltpu.VMEM((block_width, block_width), jnp.float32)],
        compiler_params=PARAMS,
        name="root",
    )(chunks)
    across = lax.ppermute(factor, "x", [(0, 1), (1, 0)])
    beside = lax.ppermute(factor, "c", [(0, 1), (1, 0)])
    both = lax.ppermute(across, "c", [(0, 1), (1, 0)])
    preconditioned, owned = pl.pallas_call(
        apply_kernel,
        out_shape=(
            jax.ShapeDtypeStruct((block_count, row_count, block_width), jnp.bfloat16),
            jax.ShapeDtypeStruct((1, CAP, block_width, block_width), jnp.bfloat16),
        ),
        in_specs=[SMEM, SMEM] + [VMEM] * 5,
        out_specs=(VMEM, VMEM),
        compiler_params=PARAMS,
        name="apply",
    )(block_owner, owner_counts, grads, factor, beside, across, both)
    return preconditioned, owned


def solution(mesh):
    fine = Mesh(mesh.devices.reshape(2, 16, 2, 8), ("x", "z", "c", "m"))
    dp = ("x", "z", "c")
    return jax.shard_map(
        per_device,
        mesh=fine,
        in_specs=(P("m", dp, None), P("m", None), P("m", dp)),
        out_specs=(P("m", dp, None), P("m", dp, None, None)),
        check_vma=False,
    )
```

```python
import jax
import jax.numpy as jnp
from jax import lax
from jax.experimental import pallas as pl
from jax.experimental.pallas import tpu as pltpu
from jax.sharding import Mesh
from jax.sharding import PartitionSpec as P

LAYERS = 2
BPL = 2
CAP = 3
ITERS = 3
NB = 4
TILE = 128
CHUNKS = 16
HALF = 64
SENT_ROWS = 80
SUM_ROWS = 72

eps_rel = 0.1

QUAD = ("x", "c")
VMEM = pl.BlockSpec(memory_space=pltpu.VMEM)
SMEM = pl.BlockSpec(memory_space=pltpu.SMEM)
PARAMS = pltpu.CompilerParams(vmem_limit_bytes=40 * 1024 * 1024)
OFF_TILES = ((0, 1), (0, 2), (0, 3), (1, 2), (1, 3), (2, 3))


def row_col():
    rows = lax.broadcasted_iota(jnp.int32, (TILE, TILE), 0)
    cols = lax.broadcasted_iota(jnp.int32, (TILE, TILE), 1)
    return rows, cols


def pieces(value):
    high = value.astype(jnp.bfloat16).astype(jnp.float32)
    middle = (value - high).astype(jnp.bfloat16).astype(jnp.float32)
    return [high, middle, value - high - middle]


def spread_scale(source):
    rows = lax.broadcasted_iota(jnp.int32, (HALF, TILE), 0)
    return 1.0 + ((rows * 37 + source * 11) & (HALF - 1)).astype(jnp.float32) / HALF


def gram_kernel(a_ref, b_ref, c_ref, d_ref, out_ref):
    gram = None
    scale = spread_scale(lax.axis_index("z"))
    for ref in (a_ref, b_ref, c_ref, d_ref):
        rows = ref[...]
        term = lax.dot_general(
            rows, rows, (((0,), (0,)), ((), ())), preferred_element_type=jnp.float32
        )
        gram = term if gram is None else gram + term
    rows, cols = row_col()

    def tile(i, j):
        return gram[i * TILE : (i + 1) * TILE, j * TILE : (j + 1) * TILE]

    tiles = [tile(i, j) for i, j in OFF_TILES]
    for i in (0, 2):
        tiles.append(jnp.where(rows < cols, tile(i, i), tile(i + 1, i + 1)))
    diagonals = [
        jnp.sum(jnp.where(rows == cols, tile(i, i), 0.0), axis=0, keepdims=True) for i in range(4)
    ]
    trace = pieces(diagonals[0] + diagonals[1] + diagonals[2] + diagonals[3])
    row16 = lax.broadcasted_iota(jnp.int32, (16, TILE), 0)
    extras = []
    for i in range(4):
        extra = jnp.zeros((16, TILE), jnp.float32)
        for row, piece in enumerate(pieces(diagonals[i]) + trace):
            extra = jnp.where(row16 == row, piece, extra)
        extras.append(extra.astype(jnp.bfloat16))
    for k in range(CHUNKS):
        half = tiles[k // 2][(k % 2) * HALF : (k % 2 + 1) * HALF]
        out_ref[k, :HALF] = (half * scale).astype(jnp.bfloat16)
        out_ref[k, HALF:] = extras[k % 4]


def sum_kernel(parts_ref, out_ref, trace_ref):
    total = jnp.zeros((HALF, TILE), jnp.float32)
    extras = jnp.zeros((16, TILE), jnp.float32)
    for k in range(CHUNKS):
        total = total + parts_ref[k, :HALF].astype(jnp.float32) / spread_scale(k)
        extras = extras + parts_ref[k, HALF:].astype(jnp.float32)
    row16 = lax.broadcasted_iota(jnp.int32, (16, TILE), 0)
    diagonal = jnp.sum(jnp.where(row16 < 3, extras, 0.0), axis=0, keepdims=True)
    trace = jnp.sum(jnp.where(row16 < 3, 0.0, extras), axis=0, keepdims=True)
    out_ref[:HALF] = total
    out_ref[HALF:] = jnp.broadcast_to(diagonal, (8, TILE))
    for k in range(trace_ref.shape[0]):
        trace_ref[k] = jnp.broadcast_to(trace, (8, TILE))


def root_kernel(total_rows, layer_blocks, chunks_ref, traces_ref, factor_ref, shifted_ref):
    width = factor_ref.shape[0]
    rows, cols = row_col()
    scale = 1.0 / total_rows
    traces = jnp.sum(traces_ref[...], axis=0)[0:1]
    layer_sum = jnp.sum(traces, axis=1, keepdims=True) * scale
    damping = layer_sum * (eps_rel / (layer_blocks * width))

    def stored(t):
        return jnp.concatenate([chunks_ref[2 * t, :HALF], chunks_ref[2 * t + 1, :HALF]], axis=0) * scale

    for t, (i, j) in enumerate(OFF_TILES):
        value = stored(t)
        shifted_ref[i * TILE : (i + 1) * TILE, j * TILE : (j + 1) * TILE] = value
        shifted_ref[j * TILE : (j + 1) * TILE, i * TILE : (i + 1) * TILE] = value.T
    for i in range(4):
        value = stored(6 + i // 2)
        value = jnp.where(rows < cols if i % 2 == 0 else rows > cols, value, 0.0)
        diagonal = chunks_ref[i, SUM_ROWS - 1 : SUM_ROWS] * scale + damping
        value = jnp.where(rows == cols, diagonal, value + value.T)
        shifted_ref[i * TILE : (i + 1) * TILE, i * TILE : (i + 1) * TILE] = value
    shifted = shifted_ref[...]
    square_sum = jnp.sum(jnp.sum(shifted * shifted, axis=0, keepdims=True), axis=1, keepdims=True)
    norm_scale = jnp.sqrt(square_sum)
    current = (shifted / norm_scale).astype(jnp.bfloat16)
    root_scale = 1.0 / jnp.sqrt(jnp.sqrt(norm_scale))
    eye_rows = lax.broadcasted_iota(jnp.int32, (width, width), 0)
    eye_cols = lax.broadcasted_iota(jnp.int32, (width, width), 1)
    five = jnp.where(eye_rows == eye_cols, 5.0, 0.0)

    def mm(a, b):
        return jnp.dot(a, b, preferred_element_type=jnp.float32).astype(jnp.bfloat16)

    factor = None
    for iteration in range(ITERS):
        step = ((five - current.astype(jnp.float32)) * 0.25).astype(jnp.bfloat16)
        if iteration == 0:
            factor = (root_scale * step.astype(jnp.float32)).astype(jnp.bfloat16)
        else:
            factor = mm(factor, step)
        if iteration + 1 < ITERS:
            square = mm(step, step)
            fourth = mm(square, square)
            current = mm(fourth, current)
    factor_ref[...] = factor


def apply_kernel(owner_ref, count_ref, grads_ref, f0_ref, f1_ref, f2_ref, f3_ref, pre_ref, own_ref):
    quad = lax.axis_index("x") * 2 + lax.axis_index("c")
    mine = (lax.axis_index("x") * lax.axis_size("z") + lax.axis_index("z")) * 2 + lax.axis_index("c")
    factors = (f0_ref, f1_ref, f2_ref, f3_ref)
    for k, ref in enumerate(factors):
        block = quad ^ k
        pre_ref[block] = jnp.dot(
            grads_ref[block], ref[...], preferred_element_type=jnp.float32
        ).astype(jnp.bfloat16)
    owners = [owner_ref[0, j] for j in range(NB)]
    slots = []
    for j in range(NB):
        slot = jnp.int32(0)
        for i in range(j):
            slot = slot + (owners[i] == owners[j]).astype(jnp.int32)
        slots.append(slot)
    for s in range(CAP):
        chosen = jnp.int32(-1)
        for j in range(NB):
            held = (owners[j] == mine) & (slots[j] == s) & (s < count_ref[0, 0])
            chosen = jnp.where(held, j ^ quad, chosen)

        @pl.when(chosen < 0)
        def _():
            own_ref[0, s] = jnp.zeros_like(own_ref[0, s])

        for k, ref in enumerate(factors):

            @pl.when(chosen == k)
            def _():
                own_ref[0, s] = ref[...]


def quad_swap(value, k):
    pairs = [(i, i ^ k) for i in range(4)]
    return lax.ppermute(value, QUAD, pairs)


def per_device(grads, block_owner, owner_counts):
    block_count, row_count, block_width = grads.shape
    z_size = lax.axis_size("z")
    total_rows = row_count * lax.axis_size("x") * z_size * lax.axis_size("c")
    quad = lax.axis_index("x") * 2 + lax.axis_index("c")
    outgoing = [lax.dynamic_index_in_dim(grads, quad ^ k, keepdims=False) for k in range(4)]
    held = [outgoing[0]] + [quad_swap(outgoing[k], k) for k in range(1, 4)]
    packed = pl.pallas_call(
        gram_kernel,
        out_shape=jax.ShapeDtypeStruct((CHUNKS, SENT_ROWS, TILE), jnp.bfloat16),
        in_specs=[VMEM] * 4,
        out_specs=VMEM,
        compiler_params=PARAMS,
        name="gram",
    )(*held)
    parts = lax.all_to_all(packed, "z", 0, 0, tiled=True)
    peers = lax.axis_size("c") * lax.axis_size("m")
    chunk, trace = pl.pallas_call(
        sum_kernel,
        out_shape=(
            jax.ShapeDtypeStruct((SUM_ROWS, TILE), jnp.float32),
            jax.ShapeDtypeStruct((peers, 8, TILE), jnp.float32),
        ),
        in_specs=[VMEM],
        out_specs=(VMEM, VMEM),
        compiler_params=PARAMS,
        name="sum",
    )(parts)
    traces = lax.all_to_all(trace, ("c", "m"), 0, 0, tiled=True)
    chunks = lax.all_gather(chunk, "z")
    factor = pl.pallas_call(
        lambda *refs: root_kernel(total_rows, lax.axis_size("m") * BPL, *refs),
        out_shape=jax.ShapeDtypeStruct((block_width, block_width), jnp.bfloat16),
        in_specs=[VMEM] * 2,
        out_specs=VMEM,
        scratch_shapes=[pltpu.VMEM((block_width, block_width), jnp.float32)],
        compiler_params=PARAMS,
        name="root",
    )(chunks, traces)
    across = lax.ppermute(factor, "x", [(0, 1), (1, 0)])
    beside = lax.ppermute(factor, "c", [(0, 1), (1, 0)])
    both = lax.ppermute(across, "c", [(0, 1), (1, 0)])
    preconditioned, owned = pl.pallas_call(
        apply_kernel,
        out_shape=(
            jax.ShapeDtypeStruct((block_count, row_count, block_width), jnp.bfloat16),
            jax.ShapeDtypeStruct((1, CAP, block_width, block_width), jnp.bfloat16),
        ),
        in_specs=[SMEM, SMEM] + [VMEM] * 5,
        out_specs=(VMEM, VMEM),
        compiler_params=PARAMS,
        name="apply",
    )(block_owner, owner_counts, grads, factor, beside, across, both)
    return preconditioned, owned


def solution(mesh):
    fine = Mesh(mesh.devices.reshape(2, 16, 2, 8), ("x", "z", "c", "m"))
    dp = ("x", "z", "c")
    return jax.shard_map(
        per_device,
        mesh=fine,
        in_specs=(P("m", dp, None), P("m", None), P("m", dp)),
        out_specs=(P("m", dp, None), P("m", dp, None, None)),
        check_vma=False,
    )
```

```python
import jax
import jax.numpy as jnp
from jax import lax
from jax.experimental import pallas as pl
from jax.experimental.pallas import tpu as pltpu
from jax.sharding import Mesh
from jax.sharding import PartitionSpec as P

LAYERS = 2
BPL = 2
CAP = 3
ITERS = 3
NB = 4
TILE = 128
CHUNKS = 16
HALF = 64
SENT_ROWS = 80
SUM_ROWS = 72
TILES = 8
PACKED_ROWS = TILES * TILE + 16

eps_rel = 0.1

QUAD = ("x", "c")
VMEM = pl.BlockSpec(memory_space=pltpu.VMEM)
SMEM = pl.BlockSpec(memory_space=pltpu.SMEM)
HBM = pl.BlockSpec(memory_space=pl.ANY)
PARAMS = pltpu.CompilerParams(vmem_limit_bytes=40 * 1024 * 1024)
OFF_TILES = ((0, 1), (0, 2), (0, 3), (1, 2), (1, 3), (2, 3))


def row_col():
    rows = lax.broadcasted_iota(jnp.int32, (TILE, TILE), 0)
    cols = lax.broadcasted_iota(jnp.int32, (TILE, TILE), 1)
    return rows, cols


def pieces(value):
    high = value.astype(jnp.bfloat16).astype(jnp.float32)
    middle = (value - high).astype(jnp.bfloat16).astype(jnp.float32)
    return [high, middle, value - high - middle]


def spread_scale(source):
    rows = lax.broadcasted_iota(jnp.int32, (HALF, TILE), 0)
    return 1.0 + ((rows * 37 + source * 11) & (HALF - 1)).astype(jnp.float32) / HALF


def gram_kernel(a_ref, b_ref, c_ref, d_ref, out_ref):
    gram = None
    scale = spread_scale(lax.axis_index("z"))
    for ref in (a_ref, b_ref, c_ref, d_ref):
        rows = ref[...]
        term = lax.dot_general(
            rows, rows, (((0,), (0,)), ((), ())), preferred_element_type=jnp.float32
        )
        gram = term if gram is None else gram + term
    rows, cols = row_col()

    def tile(i, j):
        return gram[i * TILE : (i + 1) * TILE, j * TILE : (j + 1) * TILE]

    tiles = [tile(i, j) for i, j in OFF_TILES]
    for i in (0, 2):
        tiles.append(jnp.where(rows < cols, tile(i, i), tile(i + 1, i + 1)))
    diagonals = [
        jnp.sum(jnp.where(rows == cols, tile(i, i), 0.0), axis=0, keepdims=True) for i in range(4)
    ]
    trace = pieces(diagonals[0] + diagonals[1] + diagonals[2] + diagonals[3])
    row16 = lax.broadcasted_iota(jnp.int32, (16, TILE), 0)
    extras = []
    for i in range(4):
        extra = jnp.zeros((16, TILE), jnp.float32)
        for row, piece in enumerate(pieces(diagonals[i]) + trace):
            extra = jnp.where(row16 == row, piece, extra)
        extras.append(extra.astype(jnp.bfloat16))
    for k in range(CHUNKS):
        half = tiles[k // 2][(k % 2) * HALF : (k % 2 + 1) * HALF]
        out_ref[k, :HALF] = (half * scale).astype(jnp.bfloat16)
        out_ref[k, HALF:] = extras[k % 4]


def sum_kernel(parts_ref, out_ref, trace_ref):
    total = jnp.zeros((HALF, TILE), jnp.float32)
    extras = jnp.zeros((16, TILE), jnp.float32)
    for k in range(CHUNKS):
        total = total + parts_ref[k, :HALF].astype(jnp.float32) / spread_scale(k)
        extras = extras + parts_ref[k, HALF:].astype(jnp.float32)
    row16 = lax.broadcasted_iota(jnp.int32, (16, TILE), 0)
    diagonal = jnp.sum(jnp.where(row16 < 3, extras, 0.0), axis=0, keepdims=True)
    trace = jnp.sum(jnp.where(row16 < 3, 0.0, extras), axis=0, keepdims=True)
    out_ref[:HALF] = total
    out_ref[HALF:] = jnp.broadcast_to(diagonal, (8, TILE))
    for k in range(trace_ref.shape[0]):
        trace_ref[k] = jnp.broadcast_to(trace, (8, TILE))


def normal_kernel(total_rows, layer_blocks, chunks_ref, traces_ref, out_ref):
    width = 4 * TILE
    rows, cols = row_col()
    scale = 1.0 / total_rows
    traces = jnp.sum(traces_ref[...], axis=0)[0:1]
    layer_sum = jnp.sum(traces, axis=1, keepdims=True) * scale
    damping = layer_sum * (eps_rel / (layer_blocks * width))
    tiles = []
    square_sum = jnp.zeros((TILE, TILE), jnp.float32)
    for t in range(TILES):
        tile = jnp.concatenate([chunks_ref[2 * t, :HALF], chunks_ref[2 * t + 1, :HALF]], axis=0) * scale
        if t >= len(OFF_TILES):
            tile = jnp.where(rows == cols, 0.0, tile)
        tiles.append(tile)
        square_sum = square_sum + tile * tile
    diagonals = [chunks_ref[i, SUM_ROWS - 1 : SUM_ROWS] * scale + damping for i in range(4)]
    by_lane = 2.0 * jnp.sum(square_sum, axis=0, keepdims=True)
    for diagonal in diagonals:
        by_lane = by_lane + diagonal * diagonal
    norm_scale = jnp.sqrt(jnp.sum(by_lane, axis=1, keepdims=True))
    root_scale = 1.0 / jnp.sqrt(jnp.sqrt(norm_scale))
    for t in range(TILES):
        out_ref[t * TILE : (t + 1) * TILE] = (tiles[t] / norm_scale).astype(jnp.bfloat16)
    row16 = lax.broadcasted_iota(jnp.int32, (16, TILE), 0)
    extra = jnp.zeros((16, TILE), jnp.float32)
    for row, value in enumerate([diagonal / norm_scale for diagonal in diagonals] + pieces(root_scale)):
        extra = jnp.where(row16 == row, value, extra)
    out_ref[TILES * TILE :] = extra.astype(jnp.bfloat16)


def root_kernel(packed_ref, factor_ref, normal_ref):
    width = factor_ref.shape[0]
    rows, cols = row_col()
    extra = packed_ref[TILES * TILE :].astype(jnp.float32)
    root_scale = (extra[4:5] + extra[5:6] + extra[6:7])[:, 0:1]

    def stored(t):
        return packed_ref[t * TILE : (t + 1) * TILE].astype(jnp.float32)

    for t, (i, j) in enumerate(OFF_TILES):
        value = stored(t)
        normal_ref[i * TILE : (i + 1) * TILE, j * TILE : (j + 1) * TILE] = value
        normal_ref[j * TILE : (j + 1) * TILE, i * TILE : (i + 1) * TILE] = value.T
    for i in range(4):
        value = stored(len(OFF_TILES) + i // 2)
        value = jnp.where(rows < cols if i % 2 == 0 else rows > cols, value, 0.0)
        value = jnp.where(rows == cols, extra[i : i + 1], value + value.T)
        normal_ref[i * TILE : (i + 1) * TILE, i * TILE : (i + 1) * TILE] = value
    eye_rows = lax.broadcasted_iota(jnp.int32, (width, width), 0)
    eye_cols = lax.broadcasted_iota(jnp.int32, (width, width), 1)
    five = jnp.where(eye_rows == eye_cols, 5.0, 0.0)

    def mm(a, b):
        return jnp.dot(a, b, preferred_element_type=jnp.float32).astype(jnp.bfloat16)

    current = normal_ref[...].astype(jnp.bfloat16)
    factor = None
    for iteration in range(ITERS):
        step = ((five - current.astype(jnp.float32)) * 0.25).astype(jnp.bfloat16)
        if iteration == 0:
            factor = (root_scale * step.astype(jnp.float32)).astype(jnp.bfloat16)
        else:
            factor = mm(factor, step)
        if iteration + 1 < ITERS:
            square = mm(step, step)
            fourth = mm(square, square)
            current = mm(fourth, current)
    factor_ref[...] = factor


def root(packed, width):
    return pl.pallas_call(
        root_kernel,
        out_shape=jax.ShapeDtypeStruct((width, width), jnp.bfloat16),
        in_specs=[VMEM],
        out_specs=VMEM,
        scratch_shapes=[pltpu.VMEM((width, width), jnp.float32)],
        compiler_params=PARAMS,
        cost_estimate=pl.CostEstimate(flops=16 * width**3, bytes_accessed=4 * width * width, transcendentals=0),
        name="root",
    )(packed)


def apply_kernel(
    owner_ref,
    count_ref,
    grads_ref,
    f0_ref,
    f1_ref,
    f2_ref,
    f3_ref,
    pre_ref,
    own_ref,
    rows_ref,
    zero_ref,
    pre_sem,
    own_sem,
):
    quad = lax.axis_index("x") * 2 + lax.axis_index("c")
    mine = (lax.axis_index("x") * lax.axis_size("z") + lax.axis_index("z")) * 2 + lax.axis_index("c")
    factors = (f0_ref, f1_ref, f2_ref, f3_ref)
    owners = [owner_ref[0, j] for j in range(NB)]
    slots = []
    for j in range(NB):
        slot = jnp.int32(0)
        for i in range(j):
            slot = slot + (owners[i] == owners[j]).astype(jnp.int32)
        slots.append(slot)
    zero_ref[...] = jnp.zeros_like(zero_ref)

    def slot_copy(source, s):
        return pltpu.make_async_copy(source, own_ref.at[0, s], own_sem.at[s])

    for s in range(CAP):
        chosen = jnp.int32(-1)
        for j in range(NB):
            held = (owners[j] == mine) & (slots[j] == s) & (s < count_ref[0, 0])
            chosen = jnp.where(held, j ^ quad, chosen)
        for k, ref in ((-1, zero_ref),) + tuple(enumerate(factors)):

            @pl.when(chosen == k)
            def _():
                slot_copy(ref, s).start()

    copies = []
    for k, ref in enumerate(factors):
        block = quad ^ k
        rows_ref[k] = jnp.dot(
            grads_ref[block], ref[...], preferred_element_type=jnp.float32
        ).astype(jnp.bfloat16)
        copies.append(pltpu.make_async_copy(rows_ref.at[k], pre_ref.at[block], pre_sem.at[k]))
        copies[-1].start()
    for copy in copies:
        copy.wait()
    for s in range(CAP):
        slot_copy(zero_ref, s).wait()


def quad_swap(value, k):
    pairs = [(i, i ^ k) for i in range(4)]
    return lax.ppermute(value, QUAD, pairs)


def per_device(grads, block_owner, owner_counts):
    block_count, row_count, block_width = grads.shape
    z_size = lax.axis_size("z")
    total_rows = row_count * lax.axis_size("x") * z_size * lax.axis_size("c")
    quad = lax.axis_index("x") * 2 + lax.axis_index("c")
    outgoing = [lax.dynamic_index_in_dim(grads, quad ^ k, keepdims=False) for k in range(4)]
    held = [outgoing[0]] + [quad_swap(outgoing[k], k) for k in range(1, 4)]
    packed = pl.pallas_call(
        gram_kernel,
        out_shape=jax.ShapeDtypeStruct((CHUNKS, SENT_ROWS, TILE), jnp.bfloat16),
        in_specs=[VMEM] * 4,
        out_specs=VMEM,
        compiler_params=PARAMS,
        name="gram",
    )(*held)
    parts = lax.all_to_all(packed, "z", 0, 0, tiled=True)
    peers = lax.axis_size("c") * lax.axis_size("m")
    chunk, trace = pl.pallas_call(
        sum_kernel,
        out_shape=(
            jax.ShapeDtypeStruct((SUM_ROWS, TILE), jnp.float32),
            jax.ShapeDtypeStruct((peers, 8, TILE), jnp.float32),
        ),
        in_specs=[VMEM],
        out_specs=(VMEM, VMEM),
        compiler_params=PARAMS,
        name="sum",
    )(parts)
    traces = lax.all_to_all(trace, ("c", "m"), 0, 0, tiled=True)
    chunks = lax.all_gather(chunk, "z")
    packed_normal = pl.pallas_call(
        lambda *refs: normal_kernel(total_rows, lax.axis_size("m") * BPL, *refs),
        out_shape=jax.ShapeDtypeStruct((PACKED_ROWS, TILE), jnp.bfloat16),
        in_specs=[VMEM] * 2,
        out_specs=VMEM,
        compiler_params=PARAMS,
        name="normal",
    )(chunks, traces)
    swap = [(0, 1), (1, 0)]
    packed_across = lax.ppermute(packed_normal, "x", swap)
    factor = root(packed_normal, block_width)
    beside = lax.ppermute(factor, "c", swap)
    across = root(packed_across, block_width)
    both = lax.ppermute(across, "c", swap)
    preconditioned, owned = pl.pallas_call(
        apply_kernel,
        out_shape=(
            jax.ShapeDtypeStruct((block_count, row_count, block_width), jnp.bfloat16),
            jax.ShapeDtypeStruct((1, CAP, block_width, block_width), jnp.bfloat16),
        ),
        in_specs=[SMEM, SMEM] + [VMEM] * 5,
        out_specs=(HBM, HBM),
        scratch_shapes=[
            pltpu.VMEM((block_count, row_count, block_width), jnp.bfloat16),
            pltpu.VMEM((block_width, block_width), jnp.bfloat16),
            pltpu.SemaphoreType.DMA((block_count,)),
            pltpu.SemaphoreType.DMA((CAP,)),
        ],
        compiler_params=PARAMS,
        name="apply",
    )(block_owner, owner_counts, grads, factor, beside, across, both)
    return preconditioned, owned


def solution(mesh):
    fine = Mesh(mesh.devices.reshape(2, 16, 2, 8), ("x", "z", "c", "m"))
    dp = ("x", "z", "c")
    return jax.shard_map(
        per_device,
        mesh=fine,
        in_specs=(P("m", dp, None), P("m", None), P("m", dp)),
        out_specs=(P("m", dp, None), P("m", dp, None, None)),
        check_vma=False,
    )
```

```python
import jax
import jax.numpy as jnp
from jax import lax
from jax.experimental import pallas as pl
from jax.experimental.pallas import tpu as pltpu
from jax.sharding import Mesh
from jax.sharding import PartitionSpec as P

LAYERS = 2
BPL = 2
CAP = 3
ITERS = 3
NB = 4
TILE = 128
CHUNKS = 16
HALF = 64
SENT_ROWS = 80
SUM_ROWS = 72
TILES = 8
PACKED_ROWS = TILES * TILE + 16

eps_rel = 0.1

QUAD = ("x", "c")
VMEM = pl.BlockSpec(memory_space=pltpu.VMEM)
SMEM = pl.BlockSpec(memory_space=pltpu.SMEM)
HBM = pl.BlockSpec(memory_space=pl.ANY)
PARAMS = pltpu.CompilerParams(vmem_limit_bytes=40 * 1024 * 1024)
OFF_TILES = ((0, 1), (0, 2), (0, 3), (1, 2), (1, 3), (2, 3))


def row_col():
    rows = lax.broadcasted_iota(jnp.int32, (TILE, TILE), 0)
    cols = lax.broadcasted_iota(jnp.int32, (TILE, TILE), 1)
    return rows, cols


def pieces(value):
    high = value.astype(jnp.bfloat16).astype(jnp.float32)
    middle = (value - high).astype(jnp.bfloat16).astype(jnp.float32)
    return [high, middle, value - high - middle]


def spread_scale(source):
    rows = lax.broadcasted_iota(jnp.int32, (HALF, TILE), 0)
    return 1.0 + ((rows * 37 + source * 11) & (HALF - 1)).astype(jnp.float32) / HALF


def gram_kernel(grads_ref, out_ref):
    gram = None
    scale = spread_scale(lax.axis_index("z"))
    for k in range(grads_ref.shape[0]):
        rows = grads_ref[k]
        term = lax.dot_general(
            rows, rows, (((0,), (0,)), ((), ())), preferred_element_type=jnp.float32
        )
        gram = term if gram is None else gram + term
    rows, cols = row_col()

    def tile(i, j):
        return gram[i * TILE : (i + 1) * TILE, j * TILE : (j + 1) * TILE]

    tiles = [tile(i, j) for i, j in OFF_TILES]
    for i in (0, 2):
        tiles.append(jnp.where(rows < cols, tile(i, i), tile(i + 1, i + 1)))
    diagonals = [
        jnp.sum(jnp.where(rows == cols, tile(i, i), 0.0), axis=0, keepdims=True) for i in range(4)
    ]
    trace = pieces(diagonals[0] + diagonals[1] + diagonals[2] + diagonals[3])
    row16 = lax.broadcasted_iota(jnp.int32, (16, TILE), 0)
    extras = []
    for i in range(4):
        extra = jnp.zeros((16, TILE), jnp.float32)
        for row, piece in enumerate(pieces(diagonals[i]) + trace):
            extra = jnp.where(row16 == row, piece, extra)
        extras.append(extra.astype(jnp.bfloat16))
    for k in range(CHUNKS):
        half = tiles[k // 2][(k % 2) * HALF : (k % 2 + 1) * HALF]
        out_ref[k, :HALF] = (half * scale).astype(jnp.bfloat16)
        out_ref[k, HALF:] = extras[k % 4]


def sum_kernel(parts_ref, out_ref, trace_ref):
    total = jnp.zeros((HALF, TILE), jnp.float32)
    extras = jnp.zeros((16, TILE), jnp.float32)
    for k in range(CHUNKS):
        total = total + parts_ref[k, :HALF].astype(jnp.float32) / spread_scale(k)
        extras = extras + parts_ref[k, HALF:].astype(jnp.float32)
    row16 = lax.broadcasted_iota(jnp.int32, (16, TILE), 0)
    diagonal = jnp.sum(jnp.where(row16 < 3, extras, 0.0), axis=0, keepdims=True)
    trace = jnp.sum(jnp.where(row16 < 3, 0.0, extras), axis=0, keepdims=True)
    out_ref[:HALF] = total
    out_ref[HALF:] = jnp.broadcast_to(diagonal, (8, TILE))
    for k in range(trace_ref.shape[0]):
        trace_ref[k] = jnp.broadcast_to(trace, (8, TILE))


def normal_kernel(total_rows, layer_blocks, chunks_ref, traces_ref, out_ref):
    width = 4 * TILE
    rows, cols = row_col()
    scale = 1.0 / total_rows
    traces = jnp.sum(traces_ref[...], axis=0)[0:1]
    layer_sum = jnp.sum(traces, axis=1, keepdims=True) * scale
    damping = layer_sum * (eps_rel / (layer_blocks * width))
    tiles = []
    square_sum = jnp.zeros((TILE, TILE), jnp.float32)
    for t in range(TILES):
        tile = jnp.concatenate([chunks_ref[2 * t, :HALF], chunks_ref[2 * t + 1, :HALF]], axis=0) * scale
        if t >= len(OFF_TILES):
            tile = jnp.where(rows == cols, 0.0, tile)
        tiles.append(tile)
        square_sum = square_sum + tile * tile
    diagonals = [chunks_ref[i, SUM_ROWS - 1 : SUM_ROWS] * scale + damping for i in range(4)]
    by_lane = 2.0 * jnp.sum(square_sum, axis=0, keepdims=True)
    for diagonal in diagonals:
        by_lane = by_lane + diagonal * diagonal
    norm_scale = jnp.sqrt(jnp.sum(by_lane, axis=1, keepdims=True))
    root_scale = 1.0 / jnp.sqrt(jnp.sqrt(norm_scale))
    for t in range(TILES):
        out_ref[t * TILE : (t + 1) * TILE] = (tiles[t] / norm_scale).astype(jnp.bfloat16)
    row16 = lax.broadcasted_iota(jnp.int32, (16, TILE), 0)
    extra = jnp.zeros((16, TILE), jnp.float32)
    for row, value in enumerate([diagonal / norm_scale for diagonal in diagonals] + pieces(root_scale)):
        extra = jnp.where(row16 == row, value, extra)
    out_ref[TILES * TILE :] = extra.astype(jnp.bfloat16)


def root_kernel(packed_ref, factor_ref, normal_ref):
    width = factor_ref.shape[0]
    rows, cols = row_col()
    extra = packed_ref[TILES * TILE :].astype(jnp.float32)
    root_scale = (extra[4:5] + extra[5:6] + extra[6:7])[:, 0:1]

    def stored(t):
        return packed_ref[t * TILE : (t + 1) * TILE].astype(jnp.float32)

    for t, (i, j) in enumerate(OFF_TILES):
        value = stored(t)
        normal_ref[i * TILE : (i + 1) * TILE, j * TILE : (j + 1) * TILE] = value
        normal_ref[j * TILE : (j + 1) * TILE, i * TILE : (i + 1) * TILE] = value.T
    for i in range(4):
        value = stored(len(OFF_TILES) + i // 2)
        value = jnp.where(rows < cols if i % 2 == 0 else rows > cols, value, 0.0)
        value = jnp.where(rows == cols, extra[i : i + 1], value + value.T)
        normal_ref[i * TILE : (i + 1) * TILE, i * TILE : (i + 1) * TILE] = value
    eye_rows = lax.broadcasted_iota(jnp.int32, (width, width), 0)
    eye_cols = lax.broadcasted_iota(jnp.int32, (width, width), 1)
    five = jnp.where(eye_rows == eye_cols, 5.0, 0.0)

    def mm(a, b):
        return jnp.dot(a, b, preferred_element_type=jnp.float32).astype(jnp.bfloat16)

    current = normal_ref[...].astype(jnp.bfloat16)
    factor = None
    for iteration in range(ITERS):
        step = ((five - current.astype(jnp.float32)) * 0.25).astype(jnp.bfloat16)
        if iteration == 0:
            factor = (root_scale * step.astype(jnp.float32)).astype(jnp.bfloat16)
        else:
            factor = mm(factor, step)
        if iteration + 1 < ITERS:
            square = mm(step, step)
            fourth = mm(square, square)
            current = mm(fourth, current)
    factor_ref[...] = factor


def root(packed, width):
    return pl.pallas_call(
        root_kernel,
        out_shape=jax.ShapeDtypeStruct((width, width), jnp.bfloat16),
        in_specs=[VMEM],
        out_specs=VMEM,
        scratch_shapes=[pltpu.VMEM((width, width), jnp.float32)],
        compiler_params=PARAMS,
        cost_estimate=pl.CostEstimate(flops=16 * width**3, bytes_accessed=4 * width * width, transcendentals=0),
        name="root",
    )(packed)


def apply_kernel(
    owner_ref,
    count_ref,
    grads_ref,
    f0_ref,
    f1_ref,
    f2_ref,
    f3_ref,
    pre_ref,
    own_ref,
    rows_ref,
    zero_ref,
    pre_sem,
    own_sem,
):
    quad = lax.axis_index("x") * 2 + lax.axis_index("c")
    mine = (lax.axis_index("x") * lax.axis_size("z") + lax.axis_index("z")) * 2 + lax.axis_index("c")
    factors = (f0_ref, f1_ref, f2_ref, f3_ref)
    owners = [owner_ref[0, j] for j in range(NB)]
    slots = []
    for j in range(NB):
        slot = jnp.int32(0)
        for i in range(j):
            slot = slot + (owners[i] == owners[j]).astype(jnp.int32)
        slots.append(slot)
    zero_ref[...] = jnp.zeros_like(zero_ref)

    def slot_copy(source, s):
        return pltpu.make_async_copy(source, own_ref.at[0, s], own_sem.at[s])

    for s in range(CAP):
        chosen = jnp.int32(-1)
        for j in range(NB):
            held = (owners[j] == mine) & (slots[j] == s) & (s < count_ref[0, 0])
            chosen = jnp.where(held, j ^ quad, chosen)
        for k, ref in ((-1, zero_ref),) + tuple(enumerate(factors)):

            @pl.when(chosen == k)
            def _():
                slot_copy(ref, s).start()

    copies = []
    for k, ref in enumerate(factors):
        block = quad ^ k
        rows_ref[k] = jnp.dot(
            grads_ref[block], ref[...], preferred_element_type=jnp.float32
        ).astype(jnp.bfloat16)
        copies.append(pltpu.make_async_copy(rows_ref.at[k], pre_ref.at[block], pre_sem.at[k]))
        copies[-1].start()
    for copy in copies:
        copy.wait()
    for s in range(CAP):
        slot_copy(zero_ref, s).wait()


def per_device(grads, block_owner, owner_counts):
    block_count, row_count, block_width = grads.shape
    z_size = lax.axis_size("z")
    total_rows = row_count * lax.axis_size("x") * z_size * lax.axis_size("c")
    held = lax.all_to_all(grads, QUAD, 0, 0, tiled=True)
    packed = pl.pallas_call(
        gram_kernel,
        out_shape=jax.ShapeDtypeStruct((CHUNKS, SENT_ROWS, TILE), jnp.bfloat16),
        in_specs=[VMEM],
        out_specs=VMEM,
        compiler_params=PARAMS,
        name="gram",
    )(held)
    parts = lax.all_to_all(packed, "z", 0, 0, tiled=True)
    peers = lax.axis_size("c") * lax.axis_size("m")
    chunk, trace = pl.pallas_call(
        sum_kernel,
        out_shape=(
            jax.ShapeDtypeStruct((SUM_ROWS, TILE), jnp.float32),
            jax.ShapeDtypeStruct((peers, 8, TILE), jnp.float32),
        ),
        in_specs=[VMEM],
        out_specs=(VMEM, VMEM),
        compiler_params=PARAMS,
        name="sum",
    )(parts)
    traces = lax.all_to_all(trace, ("c", "m"), 0, 0, tiled=True)
    chunks = lax.all_gather(chunk, "z")
    packed_normal = pl.pallas_call(
        lambda *refs: normal_kernel(total_rows, lax.axis_size("m") * BPL, *refs),
        out_shape=jax.ShapeDtypeStruct((PACKED_ROWS, TILE), jnp.bfloat16),
        in_specs=[VMEM] * 2,
        out_specs=VMEM,
        compiler_params=PARAMS,
        name="normal",
    )(chunks, traces)
    swap = [(0, 1), (1, 0)]
    packed_across = lax.ppermute(packed_normal, "x", swap)
    factor = root(packed_normal, block_width)
    beside = lax.ppermute(factor, "c", swap)
    across = root(packed_across, block_width)
    both = lax.ppermute(across, "c", swap)
    preconditioned, owned = pl.pallas_call(
        apply_kernel,
        out_shape=(
            jax.ShapeDtypeStruct((block_count, row_count, block_width), jnp.bfloat16),
            jax.ShapeDtypeStruct((1, CAP, block_width, block_width), jnp.bfloat16),
        ),
        in_specs=[SMEM, SMEM] + [VMEM] * 5,
        out_specs=(HBM, HBM),
        scratch_shapes=[
            pltpu.VMEM((block_count, row_count, block_width), jnp.bfloat16),
            pltpu.VMEM((block_width, block_width), jnp.bfloat16),
            pltpu.SemaphoreType.DMA((block_count,)),
            pltpu.SemaphoreType.DMA((CAP,)),
        ],
        compiler_params=PARAMS,
        name="apply",
    )(block_owner, owner_counts, grads, factor, beside, across, both)
    return preconditioned, owned


def solution(mesh):
    fine = Mesh(mesh.devices.reshape(2, 16, 2, 8), ("x", "z", "c", "m"))
    dp = ("x", "z", "c")
    return jax.shard_map(
        per_device,
        mesh=fine,
        in_specs=(P("m", dp, None), P("m", None), P("m", dp)),
        out_specs=(P("m", dp, None), P("m", dp, None, None)),
        check_vma=False,
    )
```

```python
import jax
import jax.numpy as jnp
from jax import lax
from jax.experimental import pallas as pl
from jax.experimental.pallas import tpu as pltpu
from jax.sharding import Mesh
from jax.sharding import PartitionSpec as P

LAYERS = 2
BPL = 2
CAP = 3
ITERS = 3
NB = 4
TILE = 128
CHUNKS = 16
HALF = 64
SENT_ROWS = 80
TILES = 8
PACKED_ROWS = TILES * TILE + 16

eps_rel = 0.1

QUAD = ("x", "c")
VMEM = pl.BlockSpec(memory_space=pltpu.VMEM)
SMEM = pl.BlockSpec(memory_space=pltpu.SMEM)
HBM = pl.BlockSpec(memory_space=pl.ANY)
PARAMS = pltpu.CompilerParams(vmem_limit_bytes=40 * 1024 * 1024)
OFF_TILES = ((0, 1), (0, 2), (0, 3), (1, 2), (1, 3), (2, 3))


def row_col():
    rows = lax.broadcasted_iota(jnp.int32, (TILE, TILE), 0)
    cols = lax.broadcasted_iota(jnp.int32, (TILE, TILE), 1)
    return rows, cols


def pieces(value):
    high = value.astype(jnp.bfloat16).astype(jnp.float32)
    middle = (value - high).astype(jnp.bfloat16).astype(jnp.float32)
    return [high, middle, value - high - middle]


def spread_scale(source):
    rows = lax.broadcasted_iota(jnp.int32, (HALF, TILE), 0)
    return 1.0 + ((rows * 37 + source * 11) & (HALF - 1)).astype(jnp.float32) / HALF


def extra_rows(diagonal, trace):
    rows = lax.broadcasted_iota(jnp.int32, (16, TILE), 0)
    extra = jnp.zeros((16, TILE), jnp.float32)
    for row, piece in enumerate(pieces(diagonal) + pieces(trace)):
        extra = jnp.where(rows == row, piece, extra)
    return extra.astype(jnp.bfloat16)


def gram_kernel(grads_ref, out_ref):
    gram = None
    scale = spread_scale(lax.axis_index("z"))
    for k in range(grads_ref.shape[0]):
        rows = grads_ref[k]
        term = lax.dot_general(
            rows, rows, (((0,), (0,)), ((), ())), preferred_element_type=jnp.float32
        )
        gram = term if gram is None else gram + term
    rows, cols = row_col()

    def tile(i, j):
        return gram[i * TILE : (i + 1) * TILE, j * TILE : (j + 1) * TILE]

    tiles = [tile(i, j) for i, j in OFF_TILES]
    for i in (0, 2):
        tiles.append(jnp.where(rows < cols, tile(i, i), tile(i + 1, i + 1)))
    diagonals = [
        jnp.sum(jnp.where(rows == cols, tile(i, i), 0.0), axis=0, keepdims=True) for i in range(4)
    ]
    trace = diagonals[0] + diagonals[1] + diagonals[2] + diagonals[3]
    for k in range(CHUNKS):
        half = tiles[k // 2][(k % 2) * HALF : (k % 2 + 1) * HALF]
        out_ref[k, :HALF] = (half * scale).astype(jnp.bfloat16)
        out_ref[k, HALF:] = extra_rows(diagonals[k % 4], trace)


def read_extra(extra, first):
    rows = lax.broadcasted_iota(jnp.int32, (16, TILE), 0)
    chosen = jnp.where((rows >= first) & (rows < first + 3), extra.astype(jnp.float32), 0.0)
    return jnp.sum(chosen, axis=0, keepdims=True)


def trace_kernel(parts_ref, trace_ref):
    trace = jnp.zeros((1, TILE), jnp.float32)
    for k in range(CHUNKS):
        trace = trace + read_extra(parts_ref[k, HALF:], 3)
    trace_ref[...] = jnp.broadcast_to(trace, (8, TILE))


def sum_kernel(parts_ref, trace_ref, out_ref):
    total = jnp.zeros((HALF, TILE), jnp.float32)
    diagonal = jnp.zeros((1, TILE), jnp.float32)
    for k in range(CHUNKS):
        total = total + parts_ref[k, :HALF].astype(jnp.float32) / spread_scale(k)
        diagonal = diagonal + read_extra(parts_ref[k, HALF:], 0)
    total = (total * spread_scale(CHUNKS)).astype(jnp.bfloat16)
    extra = extra_rows(diagonal, trace_ref[0:1])
    for k in range(CHUNKS):
        out_ref[k, :HALF] = total
        out_ref[k, HALF:] = extra


def normal_kernel(total_rows, layer_blocks, chunks_ref, out_ref):
    width = 4 * TILE
    rows, cols = row_col()
    scale = 1.0 / total_rows
    traces = jnp.zeros((1, TILE), jnp.float32)
    for k in range(CHUNKS):
        traces = traces + read_extra(chunks_ref[k, HALF:], 3)
    layer_sum = jnp.sum(traces, axis=1, keepdims=True) * scale
    factor = scale / spread_scale(CHUNKS)
    damping = layer_sum * (eps_rel / (layer_blocks * width))
    tiles = []
    square_sum = jnp.zeros((TILE, TILE), jnp.float32)
    for t in range(TILES):
        halves = [chunks_ref[2 * t + h, :HALF].astype(jnp.float32) * factor for h in range(2)]
        tile = jnp.concatenate(halves, axis=0)
        if t >= len(OFF_TILES):
            tile = jnp.where(rows == cols, 0.0, tile)
        tiles.append(tile)
        square_sum = square_sum + tile * tile
    diagonals = [read_extra(chunks_ref[i, HALF:], 0) * scale + damping for i in range(4)]
    by_lane = 2.0 * jnp.sum(square_sum, axis=0, keepdims=True)
    for diagonal in diagonals:
        by_lane = by_lane + diagonal * diagonal
    norm_scale = jnp.sqrt(jnp.sum(by_lane, axis=1, keepdims=True))
    root_scale = 1.0 / jnp.sqrt(jnp.sqrt(norm_scale))
    for t in range(TILES):
        out_ref[t * TILE : (t + 1) * TILE] = (tiles[t] / norm_scale).astype(jnp.bfloat16)
    row16 = lax.broadcasted_iota(jnp.int32, (16, TILE), 0)
    extra = jnp.zeros((16, TILE), jnp.float32)
    for row, value in enumerate([diagonal / norm_scale for diagonal in diagonals] + pieces(root_scale)):
        extra = jnp.where(row16 == row, value, extra)
    out_ref[TILES * TILE :] = extra.astype(jnp.bfloat16)


def root_kernel(packed_ref, factor_ref, normal_ref):
    width = factor_ref.shape[0]
    rows, cols = row_col()
    extra = packed_ref[TILES * TILE :].astype(jnp.float32)
    root_scale = (extra[4:5] + extra[5:6] + extra[6:7])[:, 0:1]

    def stored(t):
        return packed_ref[t * TILE : (t + 1) * TILE].astype(jnp.float32)

    for t, (i, j) in enumerate(OFF_TILES):
        value = stored(t)
        normal_ref[i * TILE : (i + 1) * TILE, j * TILE : (j + 1) * TILE] = value
        normal_ref[j * TILE : (j + 1) * TILE, i * TILE : (i + 1) * TILE] = value.T
    for i in range(4):
        value = stored(len(OFF_TILES) + i // 2)
        value = jnp.where(rows < cols if i % 2 == 0 else rows > cols, value, 0.0)
        value = jnp.where(rows == cols, extra[i : i + 1], value + value.T)
        normal_ref[i * TILE : (i + 1) * TILE, i * TILE : (i + 1) * TILE] = value
    eye_rows = lax.broadcasted_iota(jnp.int32, (width, width), 0)
    eye_cols = lax.broadcasted_iota(jnp.int32, (width, width), 1)
    five = jnp.where(eye_rows == eye_cols, 5.0, 0.0)

    def mm(a, b):
        return jnp.dot(a, b, preferred_element_type=jnp.float32).astype(jnp.bfloat16)

    current = normal_ref[...].astype(jnp.bfloat16)
    factor = None
    for iteration in range(ITERS):
        step = ((five - current.astype(jnp.float32)) * 0.25).astype(jnp.bfloat16)
        if iteration == 0:
            factor = (root_scale * step.astype(jnp.float32)).astype(jnp.bfloat16)
        else:
            factor = mm(factor, step)
        if iteration + 1 < ITERS:
            square = mm(step, step)
            fourth = mm(square, square)
            current = mm(fourth, current)
    factor_ref[...] = factor


def root(packed, width):
    return pl.pallas_call(
        root_kernel,
        out_shape=jax.ShapeDtypeStruct((width, width), jnp.bfloat16),
        in_specs=[VMEM],
        out_specs=VMEM,
        scratch_shapes=[pltpu.VMEM((width, width), jnp.float32)],
        compiler_params=PARAMS,
        cost_estimate=pl.CostEstimate(flops=16 * width**3, bytes_accessed=4 * width * width, transcendentals=0),
        name="root",
    )(packed)


def apply_kernel(
    owner_ref,
    count_ref,
    grads_ref,
    f0_ref,
    f1_ref,
    f2_ref,
    f3_ref,
    pre_ref,
    own_ref,
    rows_ref,
    zero_ref,
    pre_sem,
    own_sem,
):
    quad = lax.axis_index("x") * 2 + lax.axis_index("c")
    mine = (lax.axis_index("x") * lax.axis_size("z") + lax.axis_index("z")) * 2 + lax.axis_index("c")
    factors = (f0_ref, f1_ref, f2_ref, f3_ref)
    owners = [owner_ref[0, j] for j in range(NB)]
    slots = []
    for j in range(NB):
        slot = jnp.int32(0)
        for i in range(j):
            slot = slot + (owners[i] == owners[j]).astype(jnp.int32)
        slots.append(slot)
    zero_ref[...] = jnp.zeros_like(zero_ref)

    def slot_copy(source, s):
        return pltpu.make_async_copy(source, own_ref.at[0, s], own_sem.at[s])

    for s in range(CAP):
        chosen = jnp.int32(-1)
        for j in range(NB):
            held = (owners[j] == mine) & (slots[j] == s) & (s < count_ref[0, 0])
            chosen = jnp.where(held, j ^ quad, chosen)
        for k, ref in ((-1, zero_ref),) + tuple(enumerate(factors)):

            @pl.when(chosen == k)
            def _():
                slot_copy(ref, s).start()

    copies = []
    for k, ref in enumerate(factors):
        block = quad ^ k
        rows_ref[k] = jnp.dot(
            grads_ref[block], ref[...], preferred_element_type=jnp.float32
        ).astype(jnp.bfloat16)
        copies.append(pltpu.make_async_copy(rows_ref.at[k], pre_ref.at[block], pre_sem.at[k]))
        copies[-1].start()
    for copy in copies:
        copy.wait()
    for s in range(CAP):
        slot_copy(zero_ref, s).wait()


def per_device(grads, block_owner, owner_counts):
    block_count, row_count, block_width = grads.shape
    z_size = lax.axis_size("z")
    total_rows = row_count * lax.axis_size("x") * z_size * lax.axis_size("c")
    held = lax.all_to_all(grads, QUAD, 0, 0, tiled=True)
    packed = pl.pallas_call(
        gram_kernel,
        out_shape=jax.ShapeDtypeStruct((CHUNKS, SENT_ROWS, TILE), jnp.bfloat16),
        in_specs=[VMEM],
        out_specs=VMEM,
        compiler_params=PARAMS,
        name="gram",
    )(held)
    parts = lax.all_to_all(packed, "z", 0, 0, tiled=True)
    trace = pl.pallas_call(
        trace_kernel,
        out_shape=jax.ShapeDtypeStruct((8, TILE), jnp.float32),
        in_specs=[VMEM],
        out_specs=VMEM,
        compiler_params=PARAMS,
        name="trace",
    )(parts)
    peers = lax.axis_size(("c", "m"))
    pairs = [(z * peers + p, z * peers + (p ^ z)) for z in range(peers) for p in range(peers)]
    passed = lax.ppermute(trace, ("z", "c", "m"), pairs)
    copies = pl.pallas_call(
        sum_kernel,
        out_shape=jax.ShapeDtypeStruct((CHUNKS, SENT_ROWS, TILE), jnp.bfloat16),
        in_specs=[VMEM] * 2,
        out_specs=VMEM,
        compiler_params=PARAMS,
        name="sum",
    )(parts, passed)
    chunks = lax.all_to_all(copies, "z", 0, 0, tiled=True)
    packed_normal = pl.pallas_call(
        lambda *refs: normal_kernel(total_rows, lax.axis_size("m") * BPL, *refs),
        out_shape=jax.ShapeDtypeStruct((PACKED_ROWS, TILE), jnp.bfloat16),
        in_specs=[VMEM],
        out_specs=VMEM,
        compiler_params=PARAMS,
        name="normal",
    )(chunks)
    swap = [(0, 1), (1, 0)]
    packed_across = lax.ppermute(packed_normal, "x", swap)
    factor = root(packed_normal, block_width)
    beside = lax.ppermute(factor, "c", swap)
    across = root(packed_across, block_width)
    both = lax.ppermute(across, "c", swap)
    preconditioned, owned = pl.pallas_call(
        apply_kernel,
        out_shape=(
            jax.ShapeDtypeStruct((block_count, row_count, block_width), jnp.bfloat16),
            jax.ShapeDtypeStruct((1, CAP, block_width, block_width), jnp.bfloat16),
        ),
        in_specs=[SMEM, SMEM] + [VMEM] * 5,
        out_specs=(HBM, HBM),
        scratch_shapes=[
            pltpu.VMEM((block_count, row_count, block_width), jnp.bfloat16),
            pltpu.VMEM((block_width, block_width), jnp.bfloat16),
            pltpu.SemaphoreType.DMA((block_count,)),
            pltpu.SemaphoreType.DMA((CAP,)),
        ],
        compiler_params=PARAMS,
        name="apply",
    )(block_owner, owner_counts, grads, factor, beside, across, both)
    return preconditioned, owned


def solution(mesh):
    fine = Mesh(mesh.devices.reshape(2, 16, 2, 8), ("x", "z", "c", "m"))
    dp = ("x", "z", "c")
    return jax.shard_map(
        per_device,
        mesh=fine,
        in_specs=(P("m", dp, None), P("m", None), P("m", dp)),
        out_specs=(P("m", dp, None), P("m", dp, None, None)),
        check_vma=False,
    )
```

```python
import jax
import jax.numpy as jnp
from jax import lax
from jax.experimental import pallas as pl
from jax.experimental.pallas import tpu as pltpu
from jax.sharding import Mesh
from jax.sharding import PartitionSpec as P

LAYERS = 2
BPL = 2
CAP = 3
ITERS = 3
NB = 4
TILE = 128
CHUNKS = 16
HALF = 64
SENT_ROWS = 72
TILES = 8
PACKED_ROWS = TILES * TILE + 16

eps_rel = 0.1

QUAD = ("x", "c")
VMEM = pl.BlockSpec(memory_space=pltpu.VMEM)
SMEM = pl.BlockSpec(memory_space=pltpu.SMEM)
HBM = pl.BlockSpec(memory_space=pl.ANY)
PARAMS = pltpu.CompilerParams(vmem_limit_bytes=40 * 1024 * 1024)
OFF_TILES = ((0, 1), (0, 2), (0, 3), (1, 2), (1, 3), (2, 3))


def row_col():
    rows = lax.broadcasted_iota(jnp.int32, (TILE, TILE), 0)
    cols = lax.broadcasted_iota(jnp.int32, (TILE, TILE), 1)
    return rows, cols


def pieces(value):
    high = value.astype(jnp.bfloat16).astype(jnp.float32)
    middle = (value - high).astype(jnp.bfloat16).astype(jnp.float32)
    return [high, middle, value - high - middle]


def spread_scale(source):
    rows = lax.broadcasted_iota(jnp.int32, (HALF, TILE), 0)
    return 1.0 + ((rows * 37 + source * 11) & (HALF - 1)).astype(jnp.float32) / HALF


def extra_rows(diagonal, trace):
    rows = lax.broadcasted_iota(jnp.int32, (8, TILE), 0)
    extra = jnp.zeros((8, TILE), jnp.float32)
    for row, piece in enumerate(pieces(diagonal) + pieces(trace)):
        extra = jnp.where(rows == row, piece, extra)
    return extra


def gram_kernel(grads_ref, out_ref):
    gram = None
    scale = spread_scale(lax.axis_index("z"))
    for k in range(grads_ref.shape[0]):
        rows = grads_ref[k]
        term = lax.dot_general(
            rows, rows, (((0,), (0,)), ((), ())), preferred_element_type=jnp.float32
        )
        gram = term if gram is None else gram + term
    rows, cols = row_col()

    def tile(i, j):
        return gram[i * TILE : (i + 1) * TILE, j * TILE : (j + 1) * TILE]

    tiles = [tile(i, j) for i, j in OFF_TILES]
    for i in (0, 2):
        tiles.append(jnp.where(rows < cols, tile(i, i), tile(i + 1, i + 1)))
    diagonals = [
        jnp.sum(jnp.where(rows == cols, tile(i, i), 0.0), axis=0, keepdims=True) for i in range(4)
    ]
    trace = diagonals[0] + diagonals[1] + diagonals[2] + diagonals[3]
    for k in range(CHUNKS):
        half = tiles[k // 2][(k % 2) * HALF : (k % 2 + 1) * HALF]
        extra = extra_rows(diagonals[k % 4], trace)
        out_ref[k] = jnp.concatenate([half * scale, extra], axis=0).astype(jnp.bfloat16)


def read_extra(chunk, first):
    rows = lax.broadcasted_iota(jnp.int32, (8, TILE), 0)
    chosen = jnp.where((rows >= first) & (rows < first + 3), chunk[HALF:], 0.0)
    return jnp.sum(chosen, axis=0, keepdims=True)


def trace_kernel(parts_ref, trace_ref):
    trace = jnp.zeros((1, TILE), jnp.float32)
    for k in range(CHUNKS):
        trace = trace + read_extra(parts_ref[k].astype(jnp.float32), 3)
    trace_ref[...] = jnp.broadcast_to(trace, (8, TILE))


def sum_kernel(parts_ref, trace_ref, out_ref):
    total = jnp.zeros((HALF, TILE), jnp.float32)
    diagonal = jnp.zeros((1, TILE), jnp.float32)
    for k in range(CHUNKS):
        chunk = parts_ref[k].astype(jnp.float32)
        total = total + chunk[:HALF] / spread_scale(k)
        diagonal = diagonal + read_extra(chunk, 0)
    extra = extra_rows(diagonal, trace_ref[0:1])
    total = jnp.concatenate([total * spread_scale(CHUNKS), extra], axis=0).astype(jnp.bfloat16)
    for k in range(CHUNKS):
        out_ref[k] = total


def normal_kernel(total_rows, layer_blocks, chunks_ref, out_ref):
    width = 4 * TILE
    rows, cols = row_col()
    scale = 1.0 / total_rows
    chunks = [chunks_ref[k].astype(jnp.float32) for k in range(CHUNKS)]
    traces = jnp.zeros((1, TILE), jnp.float32)
    for k in range(CHUNKS):
        traces = traces + read_extra(chunks[k], 3)
    layer_sum = jnp.sum(traces, axis=1, keepdims=True) * scale
    factor = scale / spread_scale(CHUNKS)
    damping = layer_sum * (eps_rel / (layer_blocks * width))
    tiles = []
    square_sum = jnp.zeros((TILE, TILE), jnp.float32)
    for t in range(TILES):
        halves = [chunks[2 * t + h][:HALF] * factor for h in range(2)]
        tile = jnp.concatenate(halves, axis=0)
        if t >= len(OFF_TILES):
            tile = jnp.where(rows == cols, 0.0, tile)
        tiles.append(tile)
        square_sum = square_sum + tile * tile
    diagonals = [read_extra(chunks[i], 0) * scale + damping for i in range(4)]
    by_lane = 2.0 * jnp.sum(square_sum, axis=0, keepdims=True)
    for diagonal in diagonals:
        by_lane = by_lane + diagonal * diagonal
    norm_scale = jnp.sqrt(jnp.sum(by_lane, axis=1, keepdims=True))
    root_scale = 1.0 / jnp.sqrt(jnp.sqrt(norm_scale))
    for t in range(TILES):
        out_ref[t * TILE : (t + 1) * TILE] = (tiles[t] / norm_scale).astype(jnp.bfloat16)
    row16 = lax.broadcasted_iota(jnp.int32, (16, TILE), 0)
    extra = jnp.zeros((16, TILE), jnp.float32)
    for row, value in enumerate([diagonal / norm_scale for diagonal in diagonals] + pieces(root_scale)):
        extra = jnp.where(row16 == row, value, extra)
    out_ref[TILES * TILE :] = extra.astype(jnp.bfloat16)


def root_kernel(packed_ref, factor_ref, normal_ref):
    width = factor_ref.shape[0]
    rows, cols = row_col()
    extra = packed_ref[TILES * TILE :].astype(jnp.float32)
    root_scale = (extra[4:5] + extra[5:6] + extra[6:7])[:, 0:1]

    def stored(t):
        return packed_ref[t * TILE : (t + 1) * TILE].astype(jnp.float32)

    for t, (i, j) in enumerate(OFF_TILES):
        value = stored(t)
        normal_ref[i * TILE : (i + 1) * TILE, j * TILE : (j + 1) * TILE] = value
        normal_ref[j * TILE : (j + 1) * TILE, i * TILE : (i + 1) * TILE] = value.T
    for i in range(4):
        value = stored(len(OFF_TILES) + i // 2)
        value = jnp.where(rows < cols if i % 2 == 0 else rows > cols, value, 0.0)
        value = jnp.where(rows == cols, extra[i : i + 1], value + value.T)
        normal_ref[i * TILE : (i + 1) * TILE, i * TILE : (i + 1) * TILE] = value
    eye_rows = lax.broadcasted_iota(jnp.int32, (width, width), 0)
    eye_cols = lax.broadcasted_iota(jnp.int32, (width, width), 1)
    five = jnp.where(eye_rows == eye_cols, 5.0, 0.0)

    def mm(a, b):
        return jnp.dot(a, b, preferred_element_type=jnp.float32).astype(jnp.bfloat16)

    current = normal_ref[...].astype(jnp.bfloat16)
    factor = None
    for iteration in range(ITERS):
        step = ((five - current.astype(jnp.float32)) * 0.25).astype(jnp.bfloat16)
        if iteration == 0:
            factor = (root_scale * step.astype(jnp.float32)).astype(jnp.bfloat16)
        else:
            factor = mm(factor, step)
        if iteration + 1 < ITERS:
            square = mm(step, step)
            fourth = mm(square, square)
            current = mm(fourth, current)
    factor_ref[...] = factor


def root(packed, width):
    return pl.pallas_call(
        root_kernel,
        out_shape=jax.ShapeDtypeStruct((width, width), jnp.bfloat16),
        in_specs=[VMEM],
        out_specs=VMEM,
        scratch_shapes=[pltpu.VMEM((width, width), jnp.float32)],
        compiler_params=PARAMS,
        cost_estimate=pl.CostEstimate(flops=16 * width**3, bytes_accessed=4 * width * width, transcendentals=0),
        name="root",
    )(packed)


def apply_kernel(
    owner_ref,
    count_ref,
    grads_ref,
    f0_ref,
    f1_ref,
    f2_ref,
    f3_ref,
    pre_ref,
    own_ref,
    rows_ref,
    zero_ref,
    pre_sem,
    own_sem,
):
    quad = lax.axis_index("x") * 2 + lax.axis_index("c")
    mine = (lax.axis_index("x") * lax.axis_size("z") + lax.axis_index("z")) * 2 + lax.axis_index("c")
    factors = (f0_ref, f1_ref, f2_ref, f3_ref)
    owners = [owner_ref[0, j] for j in range(NB)]
    slots = []
    for j in range(NB):
        slot = jnp.int32(0)
        for i in range(j):
            slot = slot + (owners[i] == owners[j]).astype(jnp.int32)
        slots.append(slot)
    zero_ref[...] = jnp.zeros_like(zero_ref)

    def slot_copy(source, s):
        return pltpu.make_async_copy(source, own_ref.at[0, s], own_sem.at[s])

    for s in range(CAP):
        chosen = jnp.int32(-1)
        for j in range(NB):
            held = (owners[j] == mine) & (slots[j] == s) & (s < count_ref[0, 0])
            chosen = jnp.where(held, j ^ quad, chosen)
        for k, ref in ((-1, zero_ref),) + tuple(enumerate(factors)):

            @pl.when(chosen == k)
            def _():
                slot_copy(ref, s).start()

    copies = []
    for k, ref in enumerate(factors):
        block = quad ^ k
        rows_ref[k] = jnp.dot(
            grads_ref[block], ref[...], preferred_element_type=jnp.float32
        ).astype(jnp.bfloat16)
        copies.append(pltpu.make_async_copy(rows_ref.at[k], pre_ref.at[block], pre_sem.at[k]))
        copies[-1].start()
    for copy in copies:
        copy.wait()
    for s in range(CAP):
        slot_copy(zero_ref, s).wait()


def per_device(grads, block_owner, owner_counts):
    block_count, row_count, block_width = grads.shape
    z_size = lax.axis_size("z")
    total_rows = row_count * lax.axis_size("x") * z_size * lax.axis_size("c")
    held = lax.all_to_all(grads, QUAD, 0, 0, tiled=True)
    packed = pl.pallas_call(
        gram_kernel,
        out_shape=jax.ShapeDtypeStruct((CHUNKS, SENT_ROWS, TILE), jnp.bfloat16),
        in_specs=[VMEM],
        out_specs=VMEM,
        compiler_params=PARAMS,
        name="gram",
    )(held)
    parts = lax.all_to_all(packed, "z", 0, 0, tiled=True)
    trace = pl.pallas_call(
        trace_kernel,
        out_shape=jax.ShapeDtypeStruct((8, TILE), jnp.float32),
        in_specs=[VMEM],
        out_specs=VMEM,
        compiler_params=PARAMS,
        name="trace",
    )(parts)
    peers = lax.axis_size(("c", "m"))
    pairs = [(z * peers + p, z * peers + (p ^ z)) for z in range(peers) for p in range(peers)]
    passed = lax.ppermute(trace, ("z", "c", "m"), pairs)
    copies = pl.pallas_call(
        sum_kernel,
        out_shape=jax.ShapeDtypeStruct((CHUNKS, SENT_ROWS, TILE), jnp.bfloat16),
        in_specs=[VMEM] * 2,
        out_specs=VMEM,
        compiler_params=PARAMS,
        name="sum",
    )(parts, passed)
    chunks = lax.all_to_all(copies, "z", 0, 0, tiled=True)
    packed_normal = pl.pallas_call(
        lambda *refs: normal_kernel(total_rows, lax.axis_size("m") * BPL, *refs),
        out_shape=jax.ShapeDtypeStruct((PACKED_ROWS, TILE), jnp.bfloat16),
        in_specs=[VMEM],
        out_specs=VMEM,
        compiler_params=PARAMS,
        name="normal",
    )(chunks)
    swap = [(0, 1), (1, 0)]
    packed_across = lax.ppermute(packed_normal, "x", swap)
    factor = root(packed_normal, block_width)
    beside = lax.ppermute(factor, "c", swap)
    across = root(packed_across, block_width)
    both = lax.ppermute(across, "c", swap)
    preconditioned, owned = pl.pallas_call(
        apply_kernel,
        out_shape=(
            jax.ShapeDtypeStruct((block_count, row_count, block_width), jnp.bfloat16),
            jax.ShapeDtypeStruct((1, CAP, block_width, block_width), jnp.bfloat16),
        ),
        in_specs=[SMEM, SMEM] + [VMEM] * 5,
        out_specs=(HBM, HBM),
        scratch_shapes=[
            pltpu.VMEM((block_count, row_count, block_width), jnp.bfloat16),
            pltpu.VMEM((block_width, block_width), jnp.bfloat16),
            pltpu.SemaphoreType.DMA((block_count,)),
            pltpu.SemaphoreType.DMA((CAP,)),
        ],
        compiler_params=PARAMS,
        name="apply",
    )(block_owner, owner_counts, grads, factor, beside, across, both)
    return preconditioned, owned


def solution(mesh):
    fine = Mesh(mesh.devices.reshape(2, 16, 2, 8), ("x", "z", "c", "m"))
    dp = ("x", "z", "c")
    return jax.shard_map(
        per_device,
        mesh=fine,
        in_specs=(P("m", dp, None), P("m", None), P("m", dp)),
        out_specs=(P("m", dp, None), P("m", dp, None, None)),
        check_vma=False,
    )
```

```python
import jax
import jax.numpy as jnp
from jax import lax
from jax.experimental import pallas as pl
from jax.experimental.pallas import tpu as pltpu
from jax.sharding import Mesh
from jax.sharding import PartitionSpec as P

LAYERS = 2
BPL = 2
CAP = 3
ITERS = 3
NB = 4
TILE = 128
CHUNKS = 16
HALF = 64
SENT_ROWS = 72
TILES = 8
PACKED_ROWS = TILES * TILE + 16

eps_rel = 0.1

QUAD = ("x", "c")
VMEM = pl.BlockSpec(memory_space=pltpu.VMEM)
SMEM = pl.BlockSpec(memory_space=pltpu.SMEM)
HBM = pl.BlockSpec(memory_space=pl.ANY)
PARAMS = pltpu.CompilerParams(vmem_limit_bytes=40 * 1024 * 1024)
OFF_TILES = ((0, 1), (0, 2), (0, 3), (1, 2), (1, 3), (2, 3))


def row_col():
    rows = lax.broadcasted_iota(jnp.int32, (TILE, TILE), 0)
    cols = lax.broadcasted_iota(jnp.int32, (TILE, TILE), 1)
    return rows, cols


def pieces(value):
    high = value.astype(jnp.bfloat16).astype(jnp.float32)
    middle = (value - high).astype(jnp.bfloat16).astype(jnp.float32)
    return [high, middle, value - high - middle]


def spread_scale(source):
    rows = lax.broadcasted_iota(jnp.int32, (HALF, TILE), 0)
    return 1.0 + ((rows * 37 + source * 11) & (HALF - 1)).astype(jnp.float32) / HALF


def extra_rows(diagonal, trace):
    rows = lax.broadcasted_iota(jnp.int32, (8, TILE), 0)
    extra = jnp.zeros((8, TILE), jnp.float32)
    for row, piece in enumerate(pieces(diagonal) + pieces(trace)):
        extra = jnp.where(rows == row, piece, extra)
    return extra


def gram_kernel(grads_ref, out_ref):
    gram = None
    scale = spread_scale(lax.axis_index("z"))
    for k in range(grads_ref.shape[0]):
        rows = grads_ref[k]
        term = lax.dot_general(
            rows, rows, (((0,), (0,)), ((), ())), preferred_element_type=jnp.float32
        )
        gram = term if gram is None else gram + term
    rows, cols = row_col()

    def tile(i, j):
        return gram[i * TILE : (i + 1) * TILE, j * TILE : (j + 1) * TILE]

    tiles = [tile(i, j) for i, j in OFF_TILES]
    for i in (0, 2):
        tiles.append(jnp.where(rows < cols, tile(i, i), tile(i + 1, i + 1)))
    diagonals = [
        jnp.sum(jnp.where(rows == cols, tile(i, i), 0.0), axis=0, keepdims=True) for i in range(4)
    ]
    trace = diagonals[0] + diagonals[1] + diagonals[2] + diagonals[3]
    for k in range(CHUNKS):
        half = tiles[k // 2][(k % 2) * HALF : (k % 2 + 1) * HALF]
        extra = extra_rows(diagonals[k % 4], trace)
        out_ref[k] = jnp.concatenate([half * scale, extra], axis=0).astype(jnp.bfloat16)


def read_extra(chunk, first):
    rows = lax.broadcasted_iota(jnp.int32, (8, TILE), 0)
    chosen = jnp.where((rows >= first) & (rows < first + 3), chunk[HALF:], 0.0)
    return jnp.sum(chosen, axis=0, keepdims=True)


def trace_kernel(parts_ref, trace_ref):
    trace = jnp.zeros((1, TILE), jnp.float32)
    for k in range(CHUNKS):
        trace = trace + read_extra(parts_ref[k].astype(jnp.float32), 3)
    trace_ref[...] = jnp.broadcast_to(trace, (8, TILE))


def sum_kernel(parts_ref, trace_ref, out_ref):
    total = jnp.zeros((HALF, TILE), jnp.float32)
    diagonal = jnp.zeros((1, TILE), jnp.float32)
    for k in range(CHUNKS):
        chunk = parts_ref[k].astype(jnp.float32)
        total = total + chunk[:HALF] / spread_scale(k)
        diagonal = diagonal + read_extra(chunk, 0)
    extra = extra_rows(diagonal, trace_ref[0:1])
    total = jnp.concatenate([total * spread_scale(CHUNKS), extra], axis=0).astype(jnp.bfloat16)
    for k in range(CHUNKS):
        out_ref[k] = total


def normal_kernel(total_rows, layer_blocks, chunks_ref, out_ref):
    width = 4 * TILE
    rows, cols = row_col()
    scale = 1.0 / total_rows
    chunks = [chunks_ref[k].astype(jnp.float32) for k in range(CHUNKS)]
    traces = jnp.zeros((1, TILE), jnp.float32)
    for k in range(CHUNKS):
        traces = traces + read_extra(chunks[k], 3)
    layer_sum = jnp.sum(traces, axis=1, keepdims=True) * scale
    factor = scale / spread_scale(CHUNKS)
    damping = layer_sum * (eps_rel / (layer_blocks * width))
    tiles = []
    square_sum = jnp.zeros((TILE, TILE), jnp.float32)
    for t in range(TILES):
        halves = [chunks[2 * t + h][:HALF] * factor for h in range(2)]
        tile = jnp.concatenate(halves, axis=0)
        if t >= len(OFF_TILES):
            tile = jnp.where(rows == cols, 0.0, tile)
        tiles.append(tile)
        square_sum = square_sum + tile * tile
    diagonals = [read_extra(chunks[i], 0) * scale + damping for i in range(4)]
    by_lane = 2.0 * jnp.sum(square_sum, axis=0, keepdims=True)
    for diagonal in diagonals:
        by_lane = by_lane + diagonal * diagonal
    norm_scale = jnp.sqrt(jnp.sum(by_lane, axis=1, keepdims=True))
    root_scale = 1.0 / jnp.sqrt(jnp.sqrt(norm_scale))
    for t in range(TILES):
        out_ref[t * TILE : (t + 1) * TILE] = (tiles[t] / norm_scale).astype(jnp.bfloat16)
    row16 = lax.broadcasted_iota(jnp.int32, (16, TILE), 0)
    extra = jnp.zeros((16, TILE), jnp.float32)
    for row, value in enumerate([diagonal / norm_scale for diagonal in diagonals] + pieces(root_scale)):
        extra = jnp.where(row16 == row, value, extra)
    out_ref[TILES * TILE :] = extra.astype(jnp.bfloat16)


def root_kernel(packed_ref, factor_ref, normal_ref):
    width = factor_ref.shape[0]
    rows, cols = row_col()
    extra = packed_ref[TILES * TILE :].astype(jnp.float32)
    root_scale = (extra[4:5] + extra[5:6] + extra[6:7])[:, 0:1]

    def stored(t):
        return packed_ref[t * TILE : (t + 1) * TILE].astype(jnp.float32)

    for t, (i, j) in enumerate(OFF_TILES):
        value = stored(t)
        normal_ref[i * TILE : (i + 1) * TILE, j * TILE : (j + 1) * TILE] = value
        normal_ref[j * TILE : (j + 1) * TILE, i * TILE : (i + 1) * TILE] = value.T
    for i in range(4):
        value = stored(len(OFF_TILES) + i // 2)
        value = jnp.where(rows < cols if i % 2 == 0 else rows > cols, value, 0.0)
        value = jnp.where(rows == cols, extra[i : i + 1], value + value.T)
        normal_ref[i * TILE : (i + 1) * TILE, i * TILE : (i + 1) * TILE] = value
    eye_rows = lax.broadcasted_iota(jnp.int32, (width, width), 0)
    eye_cols = lax.broadcasted_iota(jnp.int32, (width, width), 1)
    five = jnp.where(eye_rows == eye_cols, 5.0, 0.0)

    def mm(a, b):
        return jnp.dot(a, b, preferred_element_type=jnp.float32).astype(jnp.bfloat16)

    current = normal_ref[...].astype(jnp.bfloat16)
    factor = None
    for iteration in range(ITERS):
        step = ((five - current.astype(jnp.float32)) * 0.25).astype(jnp.bfloat16)
        if iteration == 0:
            factor = (root_scale * step.astype(jnp.float32)).astype(jnp.bfloat16)
        else:
            factor = mm(factor, step)
        if iteration + 1 < ITERS:
            square = mm(step, step)
            fourth = mm(square, square)
            current = mm(fourth, current)
    factor_ref[...] = factor


def root(packed, width):
    return pl.pallas_call(
        root_kernel,
        out_shape=jax.ShapeDtypeStruct((width, width), jnp.bfloat16),
        in_specs=[VMEM],
        out_specs=VMEM,
        scratch_shapes=[pltpu.VMEM((width, width), jnp.float32)],
        compiler_params=PARAMS,
        cost_estimate=pl.CostEstimate(flops=16 * width**3, bytes_accessed=4 * width * width, transcendentals=0),
        name="root",
    )(packed)


def slot_choice(owner_ref, count_ref, quad):
    mine = (lax.axis_index("x") * lax.axis_size("z") + lax.axis_index("z")) * 2 + lax.axis_index("c")
    owners = [owner_ref[0, j] for j in range(NB)]
    slots = []
    for j in range(NB):
        slot = jnp.int32(0)
        for i in range(j):
            slot = slot + (owners[i] == owners[j]).astype(jnp.int32)
        slots.append(slot)
    choice = []
    for s in range(CAP):
        chosen = jnp.int32(-1)
        for j in range(NB):
            held = (owners[j] == mine) & (slots[j] == s) & (s < count_ref[0, 0])
            chosen = jnp.where(held, j ^ quad, chosen)
        choice.append(chosen)
    return choice


def apply_blocks(first, choice, sources, quad, grads_ref, pre_ref, own_ref, rows_ref, pre_sem, own_sem):
    for s in range(CAP):
        for k, ref in sources:

            @pl.when(choice[s] == k)
            def _():
                pltpu.make_async_copy(ref, own_ref.at[0, s], own_sem.at[s]).start()

    copies = []
    for k, ref in sources:
        if k < 0:
            continue
        block = quad ^ k
        rows_ref[k - first] = jnp.dot(
            grads_ref[block], ref[...], preferred_element_type=jnp.float32
        ).astype(jnp.bfloat16)
        copies.append(
            pltpu.make_async_copy(rows_ref.at[k - first], pre_ref.at[block], pre_sem.at[k - first])
        )
        copies[-1].start()
    for copy in copies:
        copy.wait()
    for s in range(CAP):
        for k, ref in sources:

            @pl.when(choice[s] == k)
            def _():
                pltpu.make_async_copy(ref, own_ref.at[0, s], own_sem.at[s]).wait()


def apply_first(
    owner_ref, count_ref, grads_ref, f0_ref, f1_ref, f2_ref, pre_ref, own_ref, rows_ref, zero_ref, pre_sem, own_sem
):
    quad = lax.axis_index("x") * 2 + lax.axis_index("c")
    choice = slot_choice(owner_ref, count_ref, quad)
    zero_ref[...] = jnp.zeros_like(zero_ref)
    sources = [(-1, zero_ref), (0, f0_ref), (1, f1_ref), (2, f2_ref)]
    apply_blocks(0, choice, sources, quad, grads_ref, pre_ref, own_ref, rows_ref, pre_sem, own_sem)


def apply_last(
    owner_ref, count_ref, grads_ref, f3_ref, pre_in, own_in, pre_ref, own_ref, rows_ref, pre_sem, own_sem
):
    quad = lax.axis_index("x") * 2 + lax.axis_index("c")
    choice = slot_choice(owner_ref, count_ref, quad)
    sources = [(3, f3_ref)]
    apply_blocks(3, choice, sources, quad, grads_ref, pre_ref, own_ref, rows_ref, pre_sem, own_sem)


def per_device(grads, block_owner, owner_counts):
    block_count, row_count, block_width = grads.shape
    z_size = lax.axis_size("z")
    total_rows = row_count * lax.axis_size("x") * z_size * lax.axis_size("c")
    held = lax.all_to_all(grads, QUAD, 0, 0, tiled=True)
    packed = pl.pallas_call(
        gram_kernel,
        out_shape=jax.ShapeDtypeStruct((CHUNKS, SENT_ROWS, TILE), jnp.bfloat16),
        in_specs=[VMEM],
        out_specs=VMEM,
        compiler_params=PARAMS,
        name="gram",
    )(held)
    parts = lax.all_to_all(packed, "z", 0, 0, tiled=True)
    trace = pl.pallas_call(
        trace_kernel,
        out_shape=jax.ShapeDtypeStruct((8, TILE), jnp.float32),
        in_specs=[VMEM],
        out_specs=VMEM,
        compiler_params=PARAMS,
        name="trace",
    )(parts)
    peers = lax.axis_size(("c", "m"))
    pairs = [(z * peers + p, z * peers + (p ^ z)) for z in range(peers) for p in range(peers)]
    passed = lax.ppermute(trace, ("z", "c", "m"), pairs)
    copies = pl.pallas_call(
        sum_kernel,
        out_shape=jax.ShapeDtypeStruct((CHUNKS, SENT_ROWS, TILE), jnp.bfloat16),
        in_specs=[VMEM] * 2,
        out_specs=VMEM,
        compiler_params=PARAMS,
        name="sum",
    )(parts, passed)
    chunks = lax.all_to_all(copies, "z", 0, 0, tiled=True)
    packed_normal = pl.pallas_call(
        lambda *refs: normal_kernel(total_rows, lax.axis_size("m") * BPL, *refs),
        out_shape=jax.ShapeDtypeStruct((PACKED_ROWS, TILE), jnp.bfloat16),
        in_specs=[VMEM],
        out_specs=VMEM,
        compiler_params=PARAMS,
        name="normal",
    )(chunks)
    swap = [(0, 1), (1, 0)]
    packed_across = lax.ppermute(packed_normal, "x", swap)
    factor = root(packed_normal, block_width)
    beside = lax.ppermute(factor, "c", swap)
    across = root(packed_across, block_width)
    both = lax.ppermute(across, "c", swap)
    outs = (
        jax.ShapeDtypeStruct((block_count, row_count, block_width), jnp.bfloat16),
        jax.ShapeDtypeStruct((1, CAP, block_width, block_width), jnp.bfloat16),
    )

    def scratch(count):
        return [
            pltpu.VMEM((count, row_count, block_width), jnp.bfloat16),
            pltpu.SemaphoreType.DMA((count,)),
            pltpu.SemaphoreType.DMA((CAP,)),
        ]

    zero = pltpu.VMEM((block_width, block_width), jnp.bfloat16)
    three = scratch(3)
    preconditioned, owned = pl.pallas_call(
        apply_first,
        out_shape=outs,
        in_specs=[SMEM, SMEM] + [VMEM] * 4,
        out_specs=(HBM, HBM),
        scratch_shapes=[three[0], zero] + three[1:],
        compiler_params=PARAMS,
        cost_estimate=pl.CostEstimate(flops=10**9, bytes_accessed=4 * 10**6, transcendentals=0),
        name="apply_first",
    )(block_owner, owner_counts, grads, factor, beside, across)
    return pl.pallas_call(
        apply_last,
        out_shape=outs,
        in_specs=[SMEM, SMEM, VMEM, VMEM, HBM, HBM],
        out_specs=(HBM, HBM),
        scratch_shapes=scratch(1),
        input_output_aliases={4: 0, 5: 1},
        compiler_params=PARAMS,
        name="apply_last",
    )(block_owner, owner_counts, grads, both, preconditioned, owned)


def solution(mesh):
    fine = Mesh(mesh.devices.reshape(2, 16, 2, 8), ("x", "z", "c", "m"))
    dp = ("x", "z", "c")
    return jax.shard_map(
        per_device,
        mesh=fine,
        in_specs=(P("m", dp, None), P("m", None), P("m", dp)),
        out_specs=(P("m", dp, None), P("m", dp, None, None)),
        check_vma=False,
    )
```

```python
import jax
import jax.numpy as jnp
from jax import lax
from jax.experimental import pallas as pl
from jax.experimental.pallas import tpu as pltpu
from jax.sharding import Mesh
from jax.sharding import PartitionSpec as P

LAYERS = 2
BPL = 2
CAP = 3
ITERS = 3
NB = 4
TILE = 128
CHUNKS = 16
HALF = 64
SENT_ROWS = 72
TILES = 8
PACKED_ROWS = TILES * TILE + 16

eps_rel = 0.1

QUAD = ("x", "c")
VMEM = pl.BlockSpec(memory_space=pltpu.VMEM)
SMEM = pl.BlockSpec(memory_space=pltpu.SMEM)
HBM = pl.BlockSpec(memory_space=pl.ANY)
PARAMS = pltpu.CompilerParams(vmem_limit_bytes=40 * 1024 * 1024)
OFF_TILES = ((0, 1), (0, 2), (0, 3), (1, 2), (1, 3), (2, 3))
PAIRS = OFF_TILES + ((0, 1), (2, 3))
DIAGONAL_CHUNK = (0, 1, 2, 4)


def row_col():
    rows = lax.broadcasted_iota(jnp.int32, (TILE, TILE), 0)
    cols = lax.broadcasted_iota(jnp.int32, (TILE, TILE), 1)
    return rows, cols


def pieces(value):
    high = value.astype(jnp.bfloat16).astype(jnp.float32)
    middle = (value - high).astype(jnp.bfloat16).astype(jnp.float32)
    return [high, middle, value - high - middle]


def spread_scale(source):
    rows = lax.broadcasted_iota(jnp.int32, (HALF, TILE), 0)
    return 1.0 + ((rows * 37 + source * 11) & (HALF - 1)).astype(jnp.float32) / HALF


def extra_rows(values):
    rows = lax.broadcasted_iota(jnp.int32, (8, TILE), 0)
    extra = jnp.zeros((8, TILE), jnp.float32)
    for row, value in enumerate(values):
        extra = jnp.where(rows == row, value, extra)
    return extra


def read_extra(chunk, first, count):
    rows = lax.broadcasted_iota(jnp.int32, (8, TILE), 0)
    chosen = jnp.where((rows >= first) & (rows < first + count), chunk[HALF:], 0.0)
    return jnp.sum(chosen, axis=0, keepdims=True)


def down(row):
    return jnp.broadcast_to(row, (TILE, TILE)).T


def gram_kernel(grads_ref, out_ref):
    gram = None
    scale = spread_scale(lax.axis_index("z"))
    for k in range(grads_ref.shape[0]):
        rows = grads_ref[k]
        term = lax.dot_general(
            rows, rows, (((0,), (0,)), ((), ())), preferred_element_type=jnp.float32
        )
        gram = term if gram is None else gram + term
    rows, cols = row_col()

    def tile(i, j):
        return gram[i * TILE : (i + 1) * TILE, j * TILE : (j + 1) * TILE]

    tiles = [tile(i, j) for i, j in OFF_TILES]
    for i in (0, 2):
        tiles.append(jnp.where(rows < cols, tile(i, i), tile(i + 1, i + 1)))
    diagonals = [
        jnp.sum(jnp.where(rows == cols, tile(i, i), 0.0), axis=0, keepdims=True) for i in range(4)
    ]
    trace = diagonals[0] + diagonals[1] + diagonals[2] + diagonals[3]
    for k in range(CHUNKS):
        half = tiles[k // 2][(k % 2) * HALF : (k % 2 + 1) * HALF]
        first, second = PAIRS[k // 2]
        extra = extra_rows(pieces(diagonals[first]) + pieces(diagonals[second]) + pieces(trace)[:2])
        out_ref[k] = jnp.concatenate([half * scale, extra], axis=0).astype(jnp.bfloat16)


def trace_kernel(parts_ref, trace_ref):
    trace = jnp.zeros((1, TILE), jnp.float32)
    for k in range(CHUNKS):
        trace = trace + read_extra(parts_ref[k].astype(jnp.float32), 6, 2)
    trace_ref[...] = jnp.broadcast_to(trace, (8, TILE))


def sum_kernel(parts_ref, trace_ref, out_ref):
    total = jnp.zeros((HALF, TILE), jnp.float32)
    first = jnp.zeros((1, TILE), jnp.float32)
    second = jnp.zeros((1, TILE), jnp.float32)
    for k in range(CHUNKS):
        chunk = parts_ref[k].astype(jnp.float32)
        total = total + chunk[:HALF] / spread_scale(k)
        first = first + read_extra(chunk, 0, 3)
        second = second + read_extra(chunk, 3, 3)
    z = lax.axis_index("z")
    merged = z >= 2 * len(OFF_TILES)
    lower_half = (z & 1) == 1
    cols = lax.broadcasted_iota(jnp.int32, (HALF, TILE), 1)
    rows = lax.broadcasted_iota(jnp.int32, (HALF, TILE), 0) + HALF * (z & 1)
    first_root, second_root = jnp.sqrt(first), jnp.sqrt(second)

    def half_down(row):
        tile = down(row)
        return jnp.where(lower_half, tile[HALF:], tile[:HALF])

    first_down, second_down = half_down(first_root), half_down(second_root)
    outer = jnp.where(
        merged,
        jnp.where(rows < cols, first_down * first_root, second_down * second_root),
        first_down * second_root,
    )
    valid = jnp.where(merged & (rows == cols), 0.0, outer)

    def sum_all(value):
        return jnp.sum(jnp.sum(value, axis=0, keepdims=True), axis=1, keepdims=True)

    alpha = sum_all(total * valid) / jnp.maximum(sum_all(valid * valid), 1e-30)
    alpha = pieces(jnp.broadcast_to(alpha, (1, TILE)))[:2]
    rest = (total - (alpha[0] + alpha[1]) * outer) * spread_scale(CHUNKS)
    diagonal = jnp.where(z == DIAGONAL_CHUNK[0], first, second)
    extra = extra_rows(pieces(diagonal) + pieces(trace_ref[0:1])[:2] + alpha)
    rest = jnp.concatenate([rest, extra], axis=0).astype(jnp.bfloat16)
    for k in range(CHUNKS):
        out_ref[k] = rest


def normal_kernel(total_rows, layer_blocks, chunks_ref, out_ref):
    width = 4 * TILE
    rows, cols = row_col()
    scale = 1.0 / total_rows
    chunks = [chunks_ref[k].astype(jnp.float32) for k in range(CHUNKS)]
    traces = jnp.zeros((1, TILE), jnp.float32)
    for k in range(CHUNKS):
        traces = traces + read_extra(chunks[k], 3, 2)
    layer_sum = jnp.sum(traces, axis=1, keepdims=True) * scale
    spread = spread_scale(CHUNKS)
    diagonals = [read_extra(chunks[DIAGONAL_CHUNK[i]], 0, 3) for i in range(4)]
    roots = [jnp.sqrt(diagonal) for diagonal in diagonals]
    roots_down = [down(root) for root in roots]
    damping = layer_sum * (eps_rel / (layer_blocks * width))
    tiles = []
    square_sum = jnp.zeros((TILE, TILE), jnp.float32)
    for t in range(TILES):
        first, second = PAIRS[t]
        if t < len(OFF_TILES):
            outer = roots_down[first] * roots[second]
        else:
            outer = jnp.where(
                rows < cols, roots_down[first] * roots[first], roots_down[second] * roots[second]
            )
        halves = []
        for h in range(2):
            chunk = chunks[2 * t + h]
            alpha = read_extra(chunk, 5, 2)
            halves.append((chunk[:HALF] / spread + alpha * outer[h * HALF : (h + 1) * HALF]) * scale)
        tile = jnp.concatenate(halves, axis=0)
        if t >= len(OFF_TILES):
            tile = jnp.where(rows == cols, 0.0, tile)
        tiles.append(tile)
        square_sum = square_sum + tile * tile
    diagonals = [diagonal * scale + damping for diagonal in diagonals]
    by_lane = 2.0 * jnp.sum(square_sum, axis=0, keepdims=True)
    for diagonal in diagonals:
        by_lane = by_lane + diagonal * diagonal
    norm_scale = jnp.sqrt(jnp.sum(by_lane, axis=1, keepdims=True))
    root_scale = 1.0 / jnp.sqrt(jnp.sqrt(norm_scale))
    for t in range(TILES):
        out_ref[t * TILE : (t + 1) * TILE] = (tiles[t] / norm_scale).astype(jnp.bfloat16)
    row16 = lax.broadcasted_iota(jnp.int32, (16, TILE), 0)
    extra = jnp.zeros((16, TILE), jnp.float32)
    for row, value in enumerate([diagonal / norm_scale for diagonal in diagonals] + pieces(root_scale)):
        extra = jnp.where(row16 == row, value, extra)
    out_ref[TILES * TILE :] = extra.astype(jnp.bfloat16)


def root_kernel(packed_ref, factor_ref, normal_ref):
    width = factor_ref.shape[0]
    rows, cols = row_col()
    extra = packed_ref[TILES * TILE :].astype(jnp.float32)
    root_scale = (extra[4:5] + extra[5:6] + extra[6:7])[:, 0:1]

    def stored(t):
        return packed_ref[t * TILE : (t + 1) * TILE].astype(jnp.float32)

    for t, (i, j) in enumerate(OFF_TILES):
        value = stored(t)
        normal_ref[i * TILE : (i + 1) * TILE, j * TILE : (j + 1) * TILE] = value
        normal_ref[j * TILE : (j + 1) * TILE, i * TILE : (i + 1) * TILE] = value.T
    for i in range(4):
        value = stored(len(OFF_TILES) + i // 2)
        value = jnp.where(rows < cols if i % 2 == 0 else rows > cols, value, 0.0)
        value = jnp.where(rows == cols, extra[i : i + 1], value + value.T)
        normal_ref[i * TILE : (i + 1) * TILE, i * TILE : (i + 1) * TILE] = value
    eye_rows = lax.broadcasted_iota(jnp.int32, (width, width), 0)
    eye_cols = lax.broadcasted_iota(jnp.int32, (width, width), 1)
    five = jnp.where(eye_rows == eye_cols, 5.0, 0.0)

    def mm(a, b):
        return jnp.dot(a, b, preferred_element_type=jnp.float32).astype(jnp.bfloat16)

    current = normal_ref[...].astype(jnp.bfloat16)
    factor = None
    for iteration in range(ITERS):
        step = ((five - current.astype(jnp.float32)) * 0.25).astype(jnp.bfloat16)
        if iteration == 0:
            factor = (root_scale * step.astype(jnp.float32)).astype(jnp.bfloat16)
        else:
            factor = mm(factor, step)
        if iteration + 1 < ITERS:
            square = mm(step, step)
            fourth = mm(square, square)
            current = mm(fourth, current)
    factor_ref[...] = factor


def root(packed, width):
    return pl.pallas_call(
        root_kernel,
        out_shape=jax.ShapeDtypeStruct((width, width), jnp.bfloat16),
        in_specs=[VMEM],
        out_specs=VMEM,
        scratch_shapes=[pltpu.VMEM((width, width), jnp.float32)],
        compiler_params=PARAMS,
        cost_estimate=pl.CostEstimate(flops=16 * width**3, bytes_accessed=4 * width * width, transcendentals=0),
        name="root",
    )(packed)


def apply_kernel(
    owner_ref,
    count_ref,
    grads_ref,
    f0_ref,
    f1_ref,
    f2_ref,
    f3_ref,
    pre_ref,
    own_ref,
    rows_ref,
    zero_ref,
    pre_sem,
    own_sem,
):
    quad = lax.axis_index("x") * 2 + lax.axis_index("c")
    mine = (lax.axis_index("x") * lax.axis_size("z") + lax.axis_index("z")) * 2 + lax.axis_index("c")
    factors = (f0_ref, f1_ref, f2_ref, f3_ref)
    owners = [owner_ref[0, j] for j in range(NB)]
    slots = []
    for j in range(NB):
        slot = jnp.int32(0)
        for i in range(j):
            slot = slot + (owners[i] == owners[j]).astype(jnp.int32)
        slots.append(slot)
    zero_ref[...] = jnp.zeros_like(zero_ref)

    def slot_copy(source, s):
        return pltpu.make_async_copy(source, own_ref.at[0, s], own_sem.at[s])

    for s in range(CAP):
        chosen = jnp.int32(-1)
        for j in range(NB):
            held = (owners[j] == mine) & (slots[j] == s) & (s < count_ref[0, 0])
            chosen = jnp.where(held, j ^ quad, chosen)
        for k, ref in ((-1, zero_ref),) + tuple(enumerate(factors)):

            @pl.when(chosen == k)
            def _():
                slot_copy(ref, s).start()

    copies = []
    for k, ref in enumerate(factors):
        block = quad ^ k
        rows_ref[k] = jnp.dot(
            grads_ref[block], ref[...], preferred_element_type=jnp.float32
        ).astype(jnp.bfloat16)
        copies.append(pltpu.make_async_copy(rows_ref.at[k], pre_ref.at[block], pre_sem.at[k]))
        copies[-1].start()
    for copy in copies:
        copy.wait()
    for s in range(CAP):
        slot_copy(zero_ref, s).wait()


def per_device(grads, block_owner, owner_counts):
    block_count, row_count, block_width = grads.shape
    z_size = lax.axis_size("z")
    total_rows = row_count * lax.axis_size("x") * z_size * lax.axis_size("c")
    held = lax.all_to_all(grads, QUAD, 0, 0, tiled=True)
    packed = pl.pallas_call(
        gram_kernel,
        out_shape=jax.ShapeDtypeStruct((CHUNKS, SENT_ROWS, TILE), jnp.bfloat16),
        in_specs=[VMEM],
        out_specs=VMEM,
        compiler_params=PARAMS,
        name="gram",
    )(held)
    parts = lax.all_to_all(packed, "z", 0, 0, tiled=True)
    trace = pl.pallas_call(
        trace_kernel,
        out_shape=jax.ShapeDtypeStruct((8, TILE), jnp.float32),
        in_specs=[VMEM],
        out_specs=VMEM,
        compiler_params=PARAMS,
        name="trace",
    )(parts)
    peers = lax.axis_size(("c", "m"))
    pairs = [(z * peers + p, z * peers + (p ^ z)) for z in range(peers) for p in range(peers)]
    passed = lax.ppermute(trace, ("z", "c", "m"), pairs)
    copies = pl.pallas_call(
        sum_kernel,
        out_shape=jax.ShapeDtypeStruct((CHUNKS, SENT_ROWS, TILE), jnp.bfloat16),
        in_specs=[VMEM] * 2,
        out_specs=VMEM,
        compiler_params=PARAMS,
        name="sum",
    )(parts, passed)
    chunks = lax.all_to_all(copies, "z", 0, 0, tiled=True)
    packed_normal = pl.pallas_call(
        lambda *refs: normal_kernel(total_rows, lax.axis_size("m") * BPL, *refs),
        out_shape=jax.ShapeDtypeStruct((PACKED_ROWS, TILE), jnp.bfloat16),
        in_specs=[VMEM],
        out_specs=VMEM,
        compiler_params=PARAMS,
        name="normal",
    )(chunks)
    swap = [(0, 1), (1, 0)]
    packed_across = lax.ppermute(packed_normal, "x", swap)
    factor = root(packed_normal, block_width)
    beside = lax.ppermute(factor, "c", swap)
    across = root(packed_across, block_width)
    both = lax.ppermute(across, "c", swap)
    preconditioned, owned = pl.pallas_call(
        apply_kernel,
        out_shape=(
            jax.ShapeDtypeStruct((block_count, row_count, block_width), jnp.bfloat16),
            jax.ShapeDtypeStruct((1, CAP, block_width, block_width), jnp.bfloat16),
        ),
        in_specs=[SMEM, SMEM] + [VMEM] * 5,
        out_specs=(HBM, HBM),
        scratch_shapes=[
            pltpu.VMEM((block_count, row_count, block_width), jnp.bfloat16),
            pltpu.VMEM((block_width, block_width), jnp.bfloat16),
            pltpu.SemaphoreType.DMA((block_count,)),
            pltpu.SemaphoreType.DMA((CAP,)),
        ],
        compiler_params=PARAMS,
        name="apply",
    )(block_owner, owner_counts, grads, factor, beside, across, both)
    return preconditioned, owned


def solution(mesh):
    fine = Mesh(mesh.devices.reshape(2, 16, 2, 8), ("x", "z", "c", "m"))
    dp = ("x", "z", "c")
    return jax.shard_map(
        per_device,
        mesh=fine,
        in_specs=(P("m", dp, None), P("m", None), P("m", dp)),
        out_specs=(P("m", dp, None), P("m", dp, None, None)),
        check_vma=False,
    )
```

```python
import jax
import jax.numpy as jnp
from jax import lax
from jax.experimental import pallas as pl
from jax.experimental.pallas import tpu as pltpu
from jax.sharding import Mesh
from jax.sharding import PartitionSpec as P

LAYERS = 2
BPL = 2
CAP = 3
ITERS = 3
NB = 4
TILE = 128
CHUNKS = 16
HALF = 64
SENT_ROWS = 72
TILES = 8
PACKED_ROWS = TILES * TILE + 16

eps_rel = 0.1

QUAD = ("x", "c")
VMEM = pl.BlockSpec(memory_space=pltpu.VMEM)
SMEM = pl.BlockSpec(memory_space=pltpu.SMEM)
HBM = pl.BlockSpec(memory_space=pl.ANY)
PARAMS = pltpu.CompilerParams(vmem_limit_bytes=40 * 1024 * 1024)
OFF_TILES = ((0, 1), (0, 2), (0, 3), (1, 2), (1, 3), (2, 3))
PAIRS = OFF_TILES + ((0, 1), (2, 3))
DIAGONAL_CHUNK = (0, 1, 2, 4)


def row_col():
    rows = lax.broadcasted_iota(jnp.int32, (TILE, TILE), 0)
    cols = lax.broadcasted_iota(jnp.int32, (TILE, TILE), 1)
    return rows, cols


def pieces(value):
    high = value.astype(jnp.bfloat16).astype(jnp.float32)
    middle = (value - high).astype(jnp.bfloat16).astype(jnp.float32)
    return [high, middle, value - high - middle]


def spread_scale(source):
    rows = lax.broadcasted_iota(jnp.int32, (HALF, TILE), 0)
    return 1.0 + ((rows * 37 + source * 11) & (HALF - 1)).astype(jnp.float32) / HALF


def extra_rows(values):
    rows = lax.broadcasted_iota(jnp.int32, (8, TILE), 0)
    extra = jnp.zeros((8, TILE), jnp.float32)
    for row, value in enumerate(values):
        extra = jnp.where(rows == row, value, extra)
    return extra


def read_extra(chunk, first, count):
    rows = lax.broadcasted_iota(jnp.int32, (8, TILE), 0)
    chosen = jnp.where((rows >= first) & (rows < first + count), chunk[HALF:], 0.0)
    return jnp.sum(chosen, axis=0, keepdims=True)


def down(row):
    return jnp.broadcast_to(row, (TILE, TILE)).T


def gram_kernel(grads_ref, out_ref):
    scale = spread_scale(lax.axis_index("z"))
    gradient = grads_ref[...].reshape(-1, grads_ref.shape[2])
    strips = []
    for i in range(4):
        strips.append(
            lax.dot_general(
                gradient[:, i * TILE : (i + 1) * TILE],
                gradient[:, i * TILE :],
                (((0,), (0,)), ((), ())),
                preferred_element_type=jnp.float32,
            )
        )
    rows, cols = row_col()

    def tile(i, j):
        return strips[i][:, (j - i) * TILE : (j - i + 1) * TILE]

    tiles = [tile(i, j) for i, j in OFF_TILES]
    for i in (0, 2):
        tiles.append(jnp.where(rows < cols, tile(i, i), tile(i + 1, i + 1)))
    diagonals = [
        jnp.sum(jnp.where(rows == cols, tile(i, i), 0.0), axis=0, keepdims=True) for i in range(4)
    ]
    trace = diagonals[0] + diagonals[1] + diagonals[2] + diagonals[3]
    for k in range(CHUNKS):
        half = tiles[k // 2][(k % 2) * HALF : (k % 2 + 1) * HALF]
        first, second = PAIRS[k // 2]
        extra = extra_rows(pieces(diagonals[first]) + pieces(diagonals[second]) + pieces(trace)[:2])
        out_ref[k] = jnp.concatenate([half * scale, extra], axis=0).astype(jnp.bfloat16)


def trace_kernel(parts_ref, trace_ref):
    trace = jnp.zeros((1, TILE), jnp.float32)
    for k in range(CHUNKS):
        trace = trace + read_extra(parts_ref[k].astype(jnp.float32), 6, 2)
    trace_ref[...] = jnp.broadcast_to(trace, (8, TILE))


def sum_kernel(parts_ref, trace_ref, out_ref):
    total = jnp.zeros((HALF, TILE), jnp.float32)
    first = jnp.zeros((1, TILE), jnp.float32)
    second = jnp.zeros((1, TILE), jnp.float32)
    for k in range(CHUNKS):
        chunk = parts_ref[k].astype(jnp.float32)
        total = total + chunk[:HALF] / spread_scale(k)
        first = first + read_extra(chunk, 0, 3)
        second = second + read_extra(chunk, 3, 3)
    z = lax.axis_index("z")
    merged = z >= 2 * len(OFF_TILES)
    lower_half = (z & 1) == 1
    cols = lax.broadcasted_iota(jnp.int32, (HALF, TILE), 1)
    rows = lax.broadcasted_iota(jnp.int32, (HALF, TILE), 0) + HALF * (z & 1)
    first_root, second_root = jnp.sqrt(first), jnp.sqrt(second)

    def half_down(row):
        tile = down(row)
        return jnp.where(lower_half, tile[HALF:], tile[:HALF])

    first_down, second_down = half_down(first_root), half_down(second_root)
    outer = jnp.where(
        merged,
        jnp.where(rows < cols, first_down * first_root, second_down * second_root),
        first_down * second_root,
    )
    valid = jnp.where(merged & (rows == cols), 0.0, outer)

    def sum_all(value):
        return jnp.sum(jnp.sum(value, axis=0, keepdims=True), axis=1, keepdims=True)

    alpha = sum_all(total * valid) / jnp.maximum(sum_all(valid * valid), 1e-30)
    alpha = pieces(jnp.broadcast_to(alpha, (1, TILE)))[:2]
    rest = (total - (alpha[0] + alpha[1]) * outer) * spread_scale(CHUNKS)
    diagonal = jnp.where(z == DIAGONAL_CHUNK[0], first, second)
    extra = extra_rows(pieces(diagonal) + pieces(trace_ref[0:1])[:2] + alpha)
    rest = jnp.concatenate([rest, extra], axis=0).astype(jnp.bfloat16)
    for k in range(CHUNKS):
        out_ref[k] = rest


def normal_kernel(total_rows, layer_blocks, chunks_ref, out_ref):
    width = 4 * TILE
    rows, cols = row_col()
    scale = 1.0 / total_rows
    chunks = [chunks_ref[k].astype(jnp.float32) for k in range(CHUNKS)]
    traces = jnp.zeros((1, TILE), jnp.float32)
    for k in range(CHUNKS):
        traces = traces + read_extra(chunks[k], 3, 2)
    layer_sum = jnp.sum(traces, axis=1, keepdims=True) * scale
    spread = spread_scale(CHUNKS)
    diagonals = [read_extra(chunks[DIAGONAL_CHUNK[i]], 0, 3) for i in range(4)]
    roots = [jnp.sqrt(diagonal) for diagonal in diagonals]
    roots_down = [down(root) for root in roots]
    damping = layer_sum * (eps_rel / (layer_blocks * width))
    tiles = []
    square_sum = jnp.zeros((TILE, TILE), jnp.float32)
    for t in range(TILES):
        first, second = PAIRS[t]
        if t < len(OFF_TILES):
            outer = roots_down[first] * roots[second]
        else:
            outer = jnp.where(
                rows < cols, roots_down[first] * roots[first], roots_down[second] * roots[second]
            )
        halves = []
        for h in range(2):
            chunk = chunks[2 * t + h]
            alpha = read_extra(chunk, 5, 2)
            halves.append((chunk[:HALF] / spread + alpha * outer[h * HALF : (h + 1) * HALF]) * scale)
        tile = jnp.concatenate(halves, axis=0)
        if t >= len(OFF_TILES):
            tile = jnp.where(rows == cols, 0.0, tile)
        tiles.append(tile)
        square_sum = square_sum + tile * tile
    diagonals = [diagonal * scale + damping for diagonal in diagonals]
    by_lane = 2.0 * jnp.sum(square_sum, axis=0, keepdims=True)
    for diagonal in diagonals:
        by_lane = by_lane + diagonal * diagonal
    norm_scale = jnp.sqrt(jnp.sum(by_lane, axis=1, keepdims=True))
    root_scale = 1.0 / jnp.sqrt(jnp.sqrt(norm_scale))
    for t in range(TILES):
        out_ref[t * TILE : (t + 1) * TILE] = (tiles[t] / norm_scale).astype(jnp.bfloat16)
    row16 = lax.broadcasted_iota(jnp.int32, (16, TILE), 0)
    extra = jnp.zeros((16, TILE), jnp.float32)
    for row, value in enumerate([diagonal / norm_scale for diagonal in diagonals] + pieces(root_scale)):
        extra = jnp.where(row16 == row, value, extra)
    out_ref[TILES * TILE :] = extra.astype(jnp.bfloat16)


def root_kernel(packed_ref, factor_ref, normal_ref):
    width = factor_ref.shape[0]
    rows, cols = row_col()
    extra = packed_ref[TILES * TILE :].astype(jnp.float32)
    root_scale = (extra[4:5] + extra[5:6] + extra[6:7])[:, 0:1]

    def stored(t):
        return packed_ref[t * TILE : (t + 1) * TILE].astype(jnp.float32)

    for t, (i, j) in enumerate(OFF_TILES):
        value = stored(t)
        normal_ref[i * TILE : (i + 1) * TILE, j * TILE : (j + 1) * TILE] = value.astype(jnp.bfloat16)
        normal_ref[j * TILE : (j + 1) * TILE, i * TILE : (i + 1) * TILE] = value.T.astype(jnp.bfloat16)
    for i in range(4):
        value = stored(len(OFF_TILES) + i // 2)
        value = jnp.where(rows < cols if i % 2 == 0 else rows > cols, value, 0.0)
        value = jnp.where(rows == cols, extra[i : i + 1], value + value.T)
        normal_ref[i * TILE : (i + 1) * TILE, i * TILE : (i + 1) * TILE] = value.astype(jnp.bfloat16)
    eye_rows = lax.broadcasted_iota(jnp.int32, (width, width), 0)
    eye_cols = lax.broadcasted_iota(jnp.int32, (width, width), 1)
    five = jnp.where(eye_rows == eye_cols, 5.0, 0.0)

    def mm(a, b):
        return jnp.dot(a, b, preferred_element_type=jnp.float32).astype(jnp.bfloat16)

    current = normal_ref[...]
    factor = None
    for iteration in range(ITERS):
        step = ((five - current.astype(jnp.float32)) * 0.25).astype(jnp.bfloat16)
        if iteration == 0:
            factor = (root_scale * step.astype(jnp.float32)).astype(jnp.bfloat16)
        else:
            factor = mm(factor, step)
        if iteration + 1 < ITERS:
            square = mm(step, step)
            fourth = mm(square, square)
            current = mm(fourth, current)
    factor_ref[...] = factor


def root(packed, width):
    return pl.pallas_call(
        root_kernel,
        out_shape=jax.ShapeDtypeStruct((width, width), jnp.bfloat16),
        in_specs=[VMEM],
        out_specs=VMEM,
        scratch_shapes=[pltpu.VMEM((width, width), jnp.bfloat16)],
        compiler_params=PARAMS,
        cost_estimate=pl.CostEstimate(flops=16 * width**3, bytes_accessed=4 * width * width, transcendentals=0),
        name="root",
    )(packed)


def apply_kernel(
    owner_ref,
    count_ref,
    grads_ref,
    f0_ref,
    f1_ref,
    f2_ref,
    f3_ref,
    pre_ref,
    own_ref,
    rows_ref,
    zero_ref,
    pre_sem,
    own_sem,
):
    quad = lax.axis_index("x") * 2 + lax.axis_index("c")
    mine = (lax.axis_index("x") * lax.axis_size("z") + lax.axis_index("z")) * 2 + lax.axis_index("c")
    factors = (f0_ref, f1_ref, f2_ref, f3_ref)
    owners = [owner_ref[0, j] for j in range(NB)]
    slots = []
    for j in range(NB):
        slot = jnp.int32(0)
        for i in range(j):
            slot = slot + (owners[i] == owners[j]).astype(jnp.int32)
        slots.append(slot)
    zero_ref[...] = jnp.zeros_like(zero_ref)

    def slot_copy(source, s):
        return pltpu.make_async_copy(source, own_ref.at[0, s], own_sem.at[s])

    for s in range(CAP):
        chosen = jnp.int32(-1)
        for j in range(NB):
            held = (owners[j] == mine) & (slots[j] == s) & (s < count_ref[0, 0])
            chosen = jnp.where(held, j ^ quad, chosen)
        for k, ref in ((-1, zero_ref),) + tuple(enumerate(factors)):

            @pl.when(chosen == k)
            def _():
                slot_copy(ref, s).start()

    copies = []
    for k, ref in enumerate(factors):
        block = quad ^ k
        rows_ref[k] = jnp.dot(
            grads_ref[block], ref[...], preferred_element_type=jnp.float32
        ).astype(jnp.bfloat16)
        copies.append(pltpu.make_async_copy(rows_ref.at[k], pre_ref.at[block], pre_sem.at[k]))
        copies[-1].start()
    for copy in copies:
        copy.wait()
    for s in range(CAP):
        slot_copy(zero_ref, s).wait()


def per_device(grads, block_owner, owner_counts):
    block_count, row_count, block_width = grads.shape
    z_size = lax.axis_size("z")
    total_rows = row_count * lax.axis_size("x") * z_size * lax.axis_size("c")
    held = lax.all_to_all(grads, QUAD, 0, 0, tiled=True)
    packed = pl.pallas_call(
        gram_kernel,
        out_shape=jax.ShapeDtypeStruct((CHUNKS, SENT_ROWS, TILE), jnp.bfloat16),
        in_specs=[VMEM],
        out_specs=VMEM,
        compiler_params=PARAMS,
        name="gram",
    )(held)
    parts = lax.all_to_all(packed, "z", 0, 0, tiled=True)
    trace = pl.pallas_call(
        trace_kernel,
        out_shape=jax.ShapeDtypeStruct((8, TILE), jnp.float32),
        in_specs=[VMEM],
        out_specs=VMEM,
        compiler_params=PARAMS,
        name="trace",
    )(parts)
    peers = lax.axis_size(("c", "m"))
    pairs = [(z * peers + p, z * peers + (p ^ z)) for z in range(peers) for p in range(peers)]
    passed = lax.ppermute(trace, ("z", "c", "m"), pairs)
    copies = pl.pallas_call(
        sum_kernel,
        out_shape=jax.ShapeDtypeStruct((CHUNKS, SENT_ROWS, TILE), jnp.bfloat16),
        in_specs=[VMEM] * 2,
        out_specs=VMEM,
        compiler_params=PARAMS,
        name="sum",
    )(parts, passed)
    chunks = lax.all_to_all(copies, "z", 0, 0, tiled=True)
    packed_normal = pl.pallas_call(
        lambda *refs: normal_kernel(total_rows, lax.axis_size("m") * BPL, *refs),
        out_shape=jax.ShapeDtypeStruct((PACKED_ROWS, TILE), jnp.bfloat16),
        in_specs=[VMEM],
        out_specs=VMEM,
        compiler_params=PARAMS,
        name="normal",
    )(chunks)
    swap = [(0, 1), (1, 0)]
    packed_across = lax.ppermute(packed_normal, "x", swap)
    factor = root(packed_normal, block_width)
    beside = lax.ppermute(factor, "c", swap)
    across = root(packed_across, block_width)
    both = lax.ppermute(across, "c", swap)
    preconditioned, owned = pl.pallas_call(
        apply_kernel,
        out_shape=(
            jax.ShapeDtypeStruct((block_count, row_count, block_width), jnp.bfloat16),
            jax.ShapeDtypeStruct((1, CAP, block_width, block_width), jnp.bfloat16),
        ),
        in_specs=[SMEM, SMEM] + [VMEM] * 5,
        out_specs=(HBM, HBM),
        scratch_shapes=[
            pltpu.VMEM((block_count, row_count, block_width), jnp.bfloat16),
            pltpu.VMEM((block_width, block_width), jnp.bfloat16),
            pltpu.SemaphoreType.DMA((block_count,)),
            pltpu.SemaphoreType.DMA((CAP,)),
        ],
        compiler_params=PARAMS,
        name="apply",
    )(block_owner, owner_counts, grads, factor, beside, across, both)
    return preconditioned, owned


def solution(mesh):
    fine = Mesh(mesh.devices.reshape(2, 16, 2, 8), ("x", "z", "c", "m"))
    dp = ("x", "z", "c")
    return jax.shard_map(
        per_device,
        mesh=fine,
        in_specs=(P("m", dp, None), P("m", None), P("m", dp)),
        out_specs=(P("m", dp, None), P("m", dp, None, None)),
        check_vma=False,
    )
```

```python
import jax
import jax.numpy as jnp
from jax import lax
from jax.experimental import pallas as pl
from jax.experimental.pallas import tpu as pltpu
from jax.sharding import Mesh
from jax.sharding import PartitionSpec as P

LAYERS = 2
BPL = 2
CAP = 3
ITERS = 3
NB = 4
TILE = 128
CHUNKS = 16
HALF = 64
SENT_ROWS = 72
TILES = 8
PACKED_ROWS = TILES * TILE + 16

eps_rel = 0.1

ALL = ("x", "z", "c", "m")
VMEM = pl.BlockSpec(memory_space=pltpu.VMEM)
SMEM = pl.BlockSpec(memory_space=pltpu.SMEM)
HBM = pl.BlockSpec(memory_space=pl.ANY)
PARAMS = pltpu.CompilerParams(vmem_limit_bytes=40 * 1024 * 1024)
OFF_TILES = ((0, 1), (0, 2), (0, 3), (1, 2), (1, 3), (2, 3))
PAIRS = OFF_TILES + ((0, 1), (2, 3))
DIAGONAL_CHUNK = (0, 1, 2, 4)


def row_col():
    rows = lax.broadcasted_iota(jnp.int32, (TILE, TILE), 0)
    cols = lax.broadcasted_iota(jnp.int32, (TILE, TILE), 1)
    return rows, cols


def pieces(value):
    high = value.astype(jnp.bfloat16).astype(jnp.float32)
    middle = (value - high).astype(jnp.bfloat16).astype(jnp.float32)
    return [high, middle, value - high - middle]


def spread_scale(source):
    rows = lax.broadcasted_iota(jnp.int32, (HALF, TILE), 0)
    return 1.0 + ((rows * 37 + source * 11) & (HALF - 1)).astype(jnp.float32) / HALF


def extra_rows(values):
    rows = lax.broadcasted_iota(jnp.int32, (8, TILE), 0)
    extra = jnp.zeros((8, TILE), jnp.float32)
    for row, value in enumerate(values):
        extra = jnp.where(rows == row, value, extra)
    return extra


def read_extra(chunk, first, count):
    rows = lax.broadcasted_iota(jnp.int32, (8, TILE), 0)
    chosen = jnp.where((rows >= first) & (rows < first + count), chunk[HALF:], 0.0)
    return jnp.sum(chosen, axis=0, keepdims=True)


def down(row):
    return jnp.broadcast_to(row, (TILE, TILE)).T


def gram_kernel(grads_ref, out_ref):
    scale = spread_scale(lax.axis_index("z"))
    gradient = grads_ref[...].reshape(-1, grads_ref.shape[2])
    strips = []
    for i in range(4):
        strips.append(
            lax.dot_general(
                gradient[:, i * TILE : (i + 1) * TILE],
                gradient[:, i * TILE :],
                (((0,), (0,)), ((), ())),
                preferred_element_type=jnp.float32,
            )
        )
    rows, cols = row_col()

    def tile(i, j):
        return strips[i][:, (j - i) * TILE : (j - i + 1) * TILE]

    tiles = [tile(i, j) for i, j in OFF_TILES]
    for i in (0, 2):
        tiles.append(jnp.where(rows < cols, tile(i, i), tile(i + 1, i + 1)))
    diagonals = [
        jnp.sum(jnp.where(rows == cols, tile(i, i), 0.0), axis=0, keepdims=True) for i in range(4)
    ]
    trace = diagonals[0] + diagonals[1] + diagonals[2] + diagonals[3]
    for k in range(CHUNKS):
        half = tiles[k // 2][(k % 2) * HALF : (k % 2 + 1) * HALF]
        first, second = PAIRS[k // 2]
        extra = extra_rows(pieces(diagonals[first]) + pieces(diagonals[second]) + pieces(trace)[:2])
        out_ref[k] = jnp.concatenate([half * scale, extra], axis=0).astype(jnp.bfloat16)


def trace_kernel(parts_ref, trace_ref):
    trace = jnp.zeros((1, TILE), jnp.float32)
    for k in range(CHUNKS):
        trace = trace + read_extra(parts_ref[k].astype(jnp.float32), 6, 2)
    trace_ref[...] = jnp.broadcast_to(trace, (8, TILE))


def sum_kernel(parts_ref, trace_ref, out_ref):
    total = jnp.zeros((HALF, TILE), jnp.float32)
    first = jnp.zeros((1, TILE), jnp.float32)
    second = jnp.zeros((1, TILE), jnp.float32)
    for k in range(CHUNKS):
        chunk = parts_ref[k].astype(jnp.float32)
        total = total + chunk[:HALF] / spread_scale(k)
        first = first + read_extra(chunk, 0, 3)
        second = second + read_extra(chunk, 3, 3)
    z = lax.axis_index("z")
    merged = z >= 2 * len(OFF_TILES)
    lower_half = (z & 1) == 1
    cols = lax.broadcasted_iota(jnp.int32, (HALF, TILE), 1)
    rows = lax.broadcasted_iota(jnp.int32, (HALF, TILE), 0) + HALF * (z & 1)
    first_root, second_root = jnp.sqrt(first), jnp.sqrt(second)

    def half_down(row):
        tile = down(row)
        return jnp.where(lower_half, tile[HALF:], tile[:HALF])

    first_down, second_down = half_down(first_root), half_down(second_root)
    outer = jnp.where(
        merged,
        jnp.where(rows < cols, first_down * first_root, second_down * second_root),
        first_down * second_root,
    )
    valid = jnp.where(merged & (rows == cols), 0.0, outer)

    def sum_all(value):
        return jnp.sum(jnp.sum(value, axis=0, keepdims=True), axis=1, keepdims=True)

    alpha = sum_all(total * valid) / jnp.maximum(sum_all(valid * valid), 1e-30)
    alpha = pieces(jnp.broadcast_to(alpha, (1, TILE)))[:2]
    rest = (total - (alpha[0] + alpha[1]) * outer) * spread_scale(CHUNKS)
    diagonal = jnp.where(z == DIAGONAL_CHUNK[0], first, second)
    extra = extra_rows(pieces(diagonal) + pieces(trace_ref[0:1])[:2] + alpha)
    rest = jnp.concatenate([rest, extra], axis=0).astype(jnp.bfloat16)
    for k in range(CHUNKS):
        out_ref[k] = rest


def normal_kernel(total_rows, layer_blocks, chunks_ref, out_ref):
    width = 4 * TILE
    rows, cols = row_col()
    scale = 1.0 / total_rows
    chunks = [chunks_ref[k].astype(jnp.float32) for k in range(CHUNKS)]
    traces = jnp.zeros((1, TILE), jnp.float32)
    for k in range(CHUNKS):
        traces = traces + read_extra(chunks[k], 3, 2)
    layer_sum = jnp.sum(traces, axis=1, keepdims=True) * scale
    spread = spread_scale(CHUNKS)
    diagonals = [read_extra(chunks[DIAGONAL_CHUNK[i]], 0, 3) for i in range(4)]
    roots = [jnp.sqrt(diagonal) for diagonal in diagonals]
    roots_down = [down(root) for root in roots]
    damping = layer_sum * (eps_rel / (layer_blocks * width))
    tiles = []
    square_sum = jnp.zeros((TILE, TILE), jnp.float32)
    for t in range(TILES):
        first, second = PAIRS[t]
        if t < len(OFF_TILES):
            outer = roots_down[first] * roots[second]
        else:
            outer = jnp.where(
                rows < cols, roots_down[first] * roots[first], roots_down[second] * roots[second]
            )
        halves = []
        for h in range(2):
            chunk = chunks[2 * t + h]
            alpha = read_extra(chunk, 5, 2)
            halves.append((chunk[:HALF] / spread + alpha * outer[h * HALF : (h + 1) * HALF]) * scale)
        tile = jnp.concatenate(halves, axis=0)
        if t >= len(OFF_TILES):
            tile = jnp.where(rows == cols, 0.0, tile)
        tiles.append(tile)
        square_sum = square_sum + tile * tile
    diagonals = [diagonal * scale + damping for diagonal in diagonals]
    by_lane = 2.0 * jnp.sum(square_sum, axis=0, keepdims=True)
    for diagonal in diagonals:
        by_lane = by_lane + diagonal * diagonal
    norm_scale = jnp.sqrt(jnp.sum(by_lane, axis=1, keepdims=True))
    root_scale = 1.0 / jnp.sqrt(jnp.sqrt(norm_scale))
    for t in range(TILES):
        out_ref[t * TILE : (t + 1) * TILE] = (tiles[t] / norm_scale).astype(jnp.bfloat16)
    row16 = lax.broadcasted_iota(jnp.int32, (16, TILE), 0)
    extra = jnp.zeros((16, TILE), jnp.float32)
    for row, value in enumerate([diagonal / norm_scale for diagonal in diagonals] + pieces(root_scale)):
        extra = jnp.where(row16 == row, value, extra)
    out_ref[TILES * TILE :] = extra.astype(jnp.bfloat16)


def root_kernel(packed_ref, factor_ref, normal_ref):
    width = factor_ref.shape[0]
    rows, cols = row_col()
    extra = packed_ref[TILES * TILE :].astype(jnp.float32)
    root_scale = (extra[4:5] + extra[5:6] + extra[6:7])[:, 0:1]

    def stored(t):
        return packed_ref[t * TILE : (t + 1) * TILE].astype(jnp.float32)

    for t, (i, j) in enumerate(OFF_TILES):
        value = stored(t)
        normal_ref[i * TILE : (i + 1) * TILE, j * TILE : (j + 1) * TILE] = value.astype(jnp.bfloat16)
        normal_ref[j * TILE : (j + 1) * TILE, i * TILE : (i + 1) * TILE] = value.T.astype(jnp.bfloat16)
    for i in range(4):
        value = stored(len(OFF_TILES) + i // 2)
        value = jnp.where(rows < cols if i % 2 == 0 else rows > cols, value, 0.0)
        value = jnp.where(rows == cols, extra[i : i + 1], value + value.T)
        normal_ref[i * TILE : (i + 1) * TILE, i * TILE : (i + 1) * TILE] = value.astype(jnp.bfloat16)
    eye_rows = lax.broadcasted_iota(jnp.int32, (width, width), 0)
    eye_cols = lax.broadcasted_iota(jnp.int32, (width, width), 1)
    five = jnp.where(eye_rows == eye_cols, 5.0, 0.0)

    def mm(a, b):
        return jnp.dot(a, b, preferred_element_type=jnp.float32).astype(jnp.bfloat16)

    current = normal_ref[...]
    factor = None
    for iteration in range(ITERS):
        step = ((five - current.astype(jnp.float32)) * 0.25).astype(jnp.bfloat16)
        if iteration == 0:
            factor = (root_scale * step.astype(jnp.float32)).astype(jnp.bfloat16)
        else:
            factor = mm(factor, step)
        if iteration + 1 < ITERS:
            square = mm(step, step)
            fourth = mm(square, square)
            current = mm(fourth, current)
    factor_ref[...] = factor


def root(packed, width):
    return pl.pallas_call(
        root_kernel,
        out_shape=jax.ShapeDtypeStruct((width, width), jnp.bfloat16),
        in_specs=[VMEM],
        out_specs=VMEM,
        scratch_shapes=[pltpu.VMEM((width, width), jnp.bfloat16)],
        compiler_params=PARAMS,
        cost_estimate=pl.CostEstimate(flops=16 * width**3, bytes_accessed=4 * width * width, transcendentals=0),
        name="root",
    )(packed)


def apply_kernel(
    owner_ref,
    count_ref,
    grads_ref,
    f0_ref,
    f1_ref,
    f2_ref,
    f3_ref,
    pre_ref,
    own_ref,
    rows_ref,
    zero_ref,
    pre_sem,
    own_sem,
):
    quad = (lax.axis_index("x") ^ (lax.axis_index("m") >> 2)) * 2 + lax.axis_index("c")
    mine = (lax.axis_index("x") * lax.axis_size("z") + lax.axis_index("z")) * 2 + lax.axis_index("c")
    factors = (f0_ref, f1_ref, f2_ref, f3_ref)
    owners = [owner_ref[0, j] for j in range(NB)]
    slots = []
    for j in range(NB):
        slot = jnp.int32(0)
        for i in range(j):
            slot = slot + (owners[i] == owners[j]).astype(jnp.int32)
        slots.append(slot)
    zero_ref[...] = jnp.zeros_like(zero_ref)

    def slot_copy(source, s):
        return pltpu.make_async_copy(source, own_ref.at[0, s], own_sem.at[s])

    for s in range(CAP):
        chosen = jnp.int32(-1)
        for j in range(NB):
            held = (owners[j] == mine) & (slots[j] == s) & (s < count_ref[0, 0])
            chosen = jnp.where(held, j ^ quad, chosen)
        for k, ref in ((-1, zero_ref),) + tuple(enumerate(factors)):

            @pl.when(chosen == k)
            def _():
                slot_copy(ref, s).start()

    copies = []
    for k, ref in enumerate(factors):
        block = quad ^ k
        rows_ref[k] = jnp.dot(
            grads_ref[block], ref[...], preferred_element_type=jnp.float32
        ).astype(jnp.bfloat16)
        copies.append(pltpu.make_async_copy(rows_ref.at[k], pre_ref.at[block], pre_sem.at[k]))
        copies[-1].start()
    for copy in copies:
        copy.wait()
    for s in range(CAP):
        slot_copy(zero_ref, s).wait()


def per_device(grads, block_owner, owner_counts):
    block_count, row_count, block_width = grads.shape
    z_size = lax.axis_size("z")
    total_rows = row_count * lax.axis_size("x") * z_size * lax.axis_size("c")
    sizes = [lax.axis_size(name) for name in ALL]

    def device(x, z, c, m):
        return ((x * sizes[1] + z) * sizes[2] + c) * sizes[3] + m

    groups = [
        [device((b // 2) ^ (m // 4), z, b % 2, m) for b in range(NB)]
        for z in range(sizes[1])
        for m in range(sizes[3])
    ]
    held = lax.all_to_all(grads, ALL, 0, 0, tiled=True, axis_index_groups=groups)
    packed = pl.pallas_call(
        gram_kernel,
        out_shape=jax.ShapeDtypeStruct((CHUNKS, SENT_ROWS, TILE), jnp.bfloat16),
        in_specs=[VMEM],
        out_specs=VMEM,
        compiler_params=PARAMS,
        name="gram",
    )(held)
    parts = lax.all_to_all(packed, "z", 0, 0, tiled=True)
    trace = pl.pallas_call(
        trace_kernel,
        out_shape=jax.ShapeDtypeStruct((8, TILE), jnp.float32),
        in_specs=[VMEM],
        out_specs=VMEM,
        compiler_params=PARAMS,
        name="trace",
    )(parts)
    pairs = [
        (device(x, z, c, m), device(x ^ (z // 4 % 2), z, c ^ (z // 8), m ^ (z % 8)))
        for x in range(sizes[0])
        for z in range(sizes[1])
        for c in range(sizes[2])
        for m in range(sizes[3])
    ]
    passed = lax.ppermute(trace, ALL, pairs)
    copies = pl.pallas_call(
        sum_kernel,
        out_shape=jax.ShapeDtypeStruct((CHUNKS, SENT_ROWS, TILE), jnp.bfloat16),
        in_specs=[VMEM] * 2,
        out_specs=VMEM,
        compiler_params=PARAMS,
        name="sum",
    )(parts, passed)
    chunks = lax.all_to_all(copies, "z", 0, 0, tiled=True)
    packed_normal = pl.pallas_call(
        lambda *refs: normal_kernel(total_rows, lax.axis_size("m") * BPL, *refs),
        out_shape=jax.ShapeDtypeStruct((PACKED_ROWS, TILE), jnp.bfloat16),
        in_specs=[VMEM],
        out_specs=VMEM,
        compiler_params=PARAMS,
        name="normal",
    )(chunks)
    swap = [(0, 1), (1, 0)]
    packed_across = lax.ppermute(packed_normal, "x", swap)
    factor = root(packed_normal, block_width)
    beside = lax.ppermute(factor, "c", swap)
    across = root(packed_across, block_width)
    both = lax.ppermute(across, "c", swap)
    preconditioned, owned = pl.pallas_call(
        apply_kernel,
        out_shape=(
            jax.ShapeDtypeStruct((block_count, row_count, block_width), jnp.bfloat16),
            jax.ShapeDtypeStruct((1, CAP, block_width, block_width), jnp.bfloat16),
        ),
        in_specs=[SMEM, SMEM] + [VMEM] * 5,
        out_specs=(HBM, HBM),
        scratch_shapes=[
            pltpu.VMEM((block_count, row_count, block_width), jnp.bfloat16),
            pltpu.VMEM((block_width, block_width), jnp.bfloat16),
            pltpu.SemaphoreType.DMA((block_count,)),
            pltpu.SemaphoreType.DMA((CAP,)),
        ],
        compiler_params=PARAMS,
        name="apply",
    )(block_owner, owner_counts, grads, factor, beside, across, both)
    return preconditioned, owned


def solution(mesh):
    fine = Mesh(mesh.devices.reshape(2, 16, 2, 8), ("x", "z", "c", "m"))
    dp = ("x", "z", "c")
    return jax.shard_map(
        per_device,
        mesh=fine,
        in_specs=(P("m", dp, None), P("m", None), P("m", dp)),
        out_specs=(P("m", dp, None), P("m", dp, None, None)),
        check_vma=False,
    )
```

```python
import jax
import jax.numpy as jnp
from jax import lax
from jax.experimental import pallas as pl
from jax.experimental.pallas import tpu as pltpu
from jax.sharding import Mesh
from jax.sharding import PartitionSpec as P

LAYERS = 2
BPL = 2
CAP = 3
ITERS = 3
NB = 4
TILE = 128
CHUNKS = 16
HALF = 64
SENT_ROWS = 72
TILES = 8
PACKED_ROWS = TILES * TILE + 16

eps_rel = 0.1

ALL = ("x", "z", "c", "m")
VMEM = pl.BlockSpec(memory_space=pltpu.VMEM)
SMEM = pl.BlockSpec(memory_space=pltpu.SMEM)
HBM = pl.BlockSpec(memory_space=pl.ANY)
PARAMS = pltpu.CompilerParams(vmem_limit_bytes=40 * 1024 * 1024)
OFF_TILES = ((0, 1), (0, 2), (0, 3), (1, 2), (1, 3), (2, 3))
PAIRS = OFF_TILES + ((0, 1), (2, 3))
DIAGONAL_CHUNK = (0, 1, 2, 4)


def row_col():
    rows = lax.broadcasted_iota(jnp.int32, (TILE, TILE), 0)
    cols = lax.broadcasted_iota(jnp.int32, (TILE, TILE), 1)
    return rows, cols


def pieces(value):
    high = value.astype(jnp.bfloat16).astype(jnp.float32)
    middle = (value - high).astype(jnp.bfloat16).astype(jnp.float32)
    return [high, middle, value - high - middle]


def spread_scale(source):
    rows = lax.broadcasted_iota(jnp.int32, (HALF, TILE), 0)
    return 1.0 + ((rows * 37 + source * 11) & (HALF - 1)).astype(jnp.float32) / HALF


def extra_rows(values):
    rows = lax.broadcasted_iota(jnp.int32, (8, TILE), 0)
    extra = jnp.zeros((8, TILE), jnp.float32)
    for row, value in enumerate(values):
        extra = jnp.where(rows == row, value, extra)
    return extra


def read_extra(chunk, first, count):
    rows = lax.broadcasted_iota(jnp.int32, (8, TILE), 0)
    chosen = jnp.where((rows >= first) & (rows < first + count), chunk[HALF:], 0.0)
    return jnp.sum(chosen, axis=0, keepdims=True)


def down(row):
    return jnp.broadcast_to(row, (TILE, TILE)).T


def gram_kernel(grads_ref, out_ref):
    scale = spread_scale(lax.axis_index("z"))
    gradient = grads_ref[...].reshape(-1, grads_ref.shape[2])
    strips = []
    for i in range(4):
        strips.append(
            lax.dot_general(
                gradient[:, i * TILE : (i + 1) * TILE],
                gradient[:, i * TILE :],
                (((0,), (0,)), ((), ())),
                preferred_element_type=jnp.float32,
            )
        )
    rows, cols = row_col()

    def tile(i, j):
        return strips[i][:, (j - i) * TILE : (j - i + 1) * TILE]

    tiles = [tile(i, j) for i, j in OFF_TILES]
    for i in (0, 2):
        tiles.append(jnp.where(rows < cols, tile(i, i), tile(i + 1, i + 1)))
    diagonals = [
        jnp.sum(jnp.where(rows == cols, tile(i, i), 0.0), axis=0, keepdims=True) for i in range(4)
    ]
    trace = diagonals[0] + diagonals[1] + diagonals[2] + diagonals[3]
    for k in range(CHUNKS):
        half = tiles[k // 2][(k % 2) * HALF : (k % 2 + 1) * HALF]
        first, second = PAIRS[k // 2]
        extra = extra_rows(pieces(diagonals[first]) + pieces(diagonals[second]) + pieces(trace)[:2])
        out_ref[k] = jnp.concatenate([half * scale, extra], axis=0).astype(jnp.bfloat16)


def trace_kernel(parts_ref, trace_ref):
    trace = jnp.zeros((1, TILE), jnp.float32)
    for k in range(CHUNKS):
        trace = trace + read_extra(parts_ref[k].astype(jnp.float32), 6, 2)
    trace_ref[...] = jnp.broadcast_to(trace, (8, TILE))


def sum_kernel(parts_ref, trace_ref, out_ref):
    total = jnp.zeros((HALF, TILE), jnp.float32)
    first = jnp.zeros((1, TILE), jnp.float32)
    second = jnp.zeros((1, TILE), jnp.float32)
    for k in range(CHUNKS):
        chunk = parts_ref[k].astype(jnp.float32)
        total = total + chunk[:HALF] / spread_scale(k)
        first = first + read_extra(chunk, 0, 3)
        second = second + read_extra(chunk, 3, 3)
    z = lax.axis_index("z")
    merged = z >= 2 * len(OFF_TILES)
    lower_half = (z & 1) == 1
    cols = lax.broadcasted_iota(jnp.int32, (HALF, TILE), 1)
    rows = lax.broadcasted_iota(jnp.int32, (HALF, TILE), 0) + HALF * (z & 1)
    first_root, second_root = jnp.sqrt(first), jnp.sqrt(second)

    def half_down(row):
        tile = down(row)
        return jnp.where(lower_half, tile[HALF:], tile[:HALF])

    first_down, second_down = half_down(first_root), half_down(second_root)
    outer = jnp.where(
        merged,
        jnp.where(rows < cols, first_down * first_root, second_down * second_root),
        first_down * second_root,
    )
    valid = jnp.where(merged & (rows == cols), 0.0, outer)

    def sum_all(value):
        return jnp.sum(jnp.sum(value, axis=0, keepdims=True), axis=1, keepdims=True)

    alpha = sum_all(total * valid) / jnp.maximum(sum_all(valid * valid), 1e-30)
    alpha = pieces(jnp.broadcast_to(alpha, (1, TILE)))[:2]
    rest = (total - (alpha[0] + alpha[1]) * outer) * spread_scale(CHUNKS)
    diagonal = jnp.where(z == DIAGONAL_CHUNK[0], first, second)
    extra = extra_rows(pieces(diagonal) + pieces(trace_ref[0:1])[:2] + alpha)
    rest = jnp.concatenate([rest, extra], axis=0).astype(jnp.bfloat16)
    for k in range(CHUNKS):
        out_ref[k] = rest


def normal_kernel(total_rows, layer_blocks, chunks_ref, out_ref):
    width = 4 * TILE
    rows, cols = row_col()
    scale = 1.0 / total_rows
    chunks = [chunks_ref[k].astype(jnp.float32) for k in range(CHUNKS)]
    traces = jnp.zeros((1, TILE), jnp.float32)
    for k in range(CHUNKS):
        traces = traces + read_extra(chunks[k], 3, 2)
    layer_sum = jnp.sum(traces, axis=1, keepdims=True) * scale
    spread = spread_scale(CHUNKS)
    diagonals = [read_extra(chunks[DIAGONAL_CHUNK[i]], 0, 3) for i in range(4)]
    roots = [jnp.sqrt(diagonal) for diagonal in diagonals]
    roots_down = [down(root) for root in roots]
    damping = layer_sum * (eps_rel / (layer_blocks * width))
    tiles = []
    square_sum = jnp.zeros((TILE, TILE), jnp.float32)
    for t in range(TILES):
        first, second = PAIRS[t]
        if t < len(OFF_TILES):
            outer = roots_down[first] * roots[second]
        else:
            outer = jnp.where(
                rows < cols, roots_down[first] * roots[first], roots_down[second] * roots[second]
            )
        halves = []
        for h in range(2):
            chunk = chunks[2 * t + h]
            alpha = read_extra(chunk, 5, 2)
            halves.append((chunk[:HALF] / spread + alpha * outer[h * HALF : (h + 1) * HALF]) * scale)
        tile = jnp.concatenate(halves, axis=0)
        if t >= len(OFF_TILES):
            tile = jnp.where(rows == cols, 0.0, tile)
        tiles.append(tile)
        square_sum = square_sum + tile * tile
    diagonals = [diagonal * scale + damping for diagonal in diagonals]
    by_lane = 2.0 * jnp.sum(square_sum, axis=0, keepdims=True)
    for diagonal in diagonals:
        by_lane = by_lane + diagonal * diagonal
    norm_scale = jnp.sqrt(jnp.sum(by_lane, axis=1, keepdims=True))
    root_scale = 1.0 / jnp.sqrt(jnp.sqrt(norm_scale))
    for t in range(TILES):
        out_ref[t * TILE : (t + 1) * TILE] = (tiles[t] / norm_scale).astype(jnp.bfloat16)
    row16 = lax.broadcasted_iota(jnp.int32, (16, TILE), 0)
    extra = jnp.zeros((16, TILE), jnp.float32)
    for row, value in enumerate([diagonal / norm_scale for diagonal in diagonals] + pieces(root_scale)):
        extra = jnp.where(row16 == row, value, extra)
    out_ref[TILES * TILE :] = extra.astype(jnp.bfloat16)


def root_kernel(packed_ref, factor_ref, normal_ref):
    width = factor_ref.shape[0]
    rows, cols = row_col()
    extra = packed_ref[TILES * TILE :].astype(jnp.float32)
    root_scale = (extra[4:5] + extra[5:6] + extra[6:7])[:, 0:1]

    def stored(t):
        return packed_ref[t * TILE : (t + 1) * TILE].astype(jnp.float32)

    for t, (i, j) in enumerate(OFF_TILES):
        value = stored(t)
        normal_ref[i * TILE : (i + 1) * TILE, j * TILE : (j + 1) * TILE] = value.astype(jnp.bfloat16)
        normal_ref[j * TILE : (j + 1) * TILE, i * TILE : (i + 1) * TILE] = value.T.astype(jnp.bfloat16)
    for i in range(4):
        value = stored(len(OFF_TILES) + i // 2)
        value = jnp.where(rows < cols if i % 2 == 0 else rows > cols, value, 0.0)
        value = jnp.where(rows == cols, extra[i : i + 1], value + value.T)
        normal_ref[i * TILE : (i + 1) * TILE, i * TILE : (i + 1) * TILE] = value.astype(jnp.bfloat16)
    eye_rows = lax.broadcasted_iota(jnp.int32, (width, width), 0)
    eye_cols = lax.broadcasted_iota(jnp.int32, (width, width), 1)
    five = jnp.where(eye_rows == eye_cols, 5.0, 0.0)

    def mm(a, b):
        return jnp.dot(a, b, preferred_element_type=jnp.float32).astype(jnp.bfloat16)

    current = normal_ref[...]
    factor = None
    for iteration in range(ITERS):
        step = ((five - current.astype(jnp.float32)) * 0.25).astype(jnp.bfloat16)
        if iteration == 0:
            factor = (root_scale * step.astype(jnp.float32)).astype(jnp.bfloat16)
        else:
            factor = mm(factor, step)
        if iteration + 1 < ITERS:
            square = mm(step, step)
            fourth = mm(square, square)
            current = mm(fourth, current)
    factor_ref[...] = factor


def block_of(k):
    quad = (lax.axis_index("x") ^ (lax.axis_index("m") >> 2)) * 2 + lax.axis_index("c")
    return quad ^ k


def product(grads_ref, factor, k):
    rows = jnp.dot(grads_ref[block_of(k)], factor, preferred_element_type=jnp.float32)
    return rows.astype(jnp.bfloat16)


def own_root_kernel(packed_ref, grads_ref, factor_ref, rows_ref, normal_ref):
    root_kernel(packed_ref, factor_ref, normal_ref)
    rows_ref[...] = product(grads_ref, factor_ref[...], 0)


def rows_kernel(grads_ref, f1_ref, f2_ref, rows_ref):
    for k, ref in ((1, f1_ref), (2, f2_ref)):
        rows_ref[k - 1] = product(grads_ref, ref[...], k)


def root(packed, width):
    return pl.pallas_call(
        root_kernel,
        out_shape=jax.ShapeDtypeStruct((width, width), jnp.bfloat16),
        in_specs=[VMEM],
        out_specs=VMEM,
        scratch_shapes=[pltpu.VMEM((width, width), jnp.bfloat16)],
        compiler_params=PARAMS,
        cost_estimate=pl.CostEstimate(flops=16 * width**3, bytes_accessed=4 * width * width, transcendentals=0),
        name="root",
    )(packed)


def apply_kernel(
    owner_ref,
    count_ref,
    grads_ref,
    own_rows_ref,
    rows_ref,
    f0_ref,
    f1_ref,
    f2_ref,
    f3_ref,
    pre_ref,
    own_ref,
    last_ref,
    zero_ref,
    pre_sem,
    own_sem,
):
    quad = block_of(0)
    mine = (lax.axis_index("x") * lax.axis_size("z") + lax.axis_index("z")) * 2 + lax.axis_index("c")
    factors = (f0_ref, f1_ref, f2_ref, f3_ref)

    def rows_copy(source, k):
        return pltpu.make_async_copy(source, pre_ref.at[block_of(k)], pre_sem.at[k])

    ready = [(0, own_rows_ref), (1, rows_ref.at[0]), (2, rows_ref.at[1])]
    copies = [rows_copy(source, k) for k, source in ready]
    for copy in copies:
        copy.start()
    owners = [owner_ref[0, j] for j in range(NB)]
    slots = []
    for j in range(NB):
        slot = jnp.int32(0)
        for i in range(j):
            slot = slot + (owners[i] == owners[j]).astype(jnp.int32)
        slots.append(slot)
    zero_ref[...] = jnp.zeros_like(zero_ref)

    def slot_copy(source, s):
        return pltpu.make_async_copy(source, own_ref.at[0, s], own_sem.at[s])

    for s in range(CAP):
        chosen = jnp.int32(-1)
        for j in range(NB):
            held = (owners[j] == mine) & (slots[j] == s) & (s < count_ref[0, 0])
            chosen = jnp.where(held, j ^ quad, chosen)
        for k, ref in ((-1, zero_ref),) + tuple(enumerate(factors)):

            @pl.when(chosen == k)
            def _():
                slot_copy(ref, s).start()

    last_ref[...] = product(grads_ref, f3_ref[...], 3)
    copies.append(rows_copy(last_ref, 3))
    copies[-1].start()
    for copy in copies:
        copy.wait()
    for s in range(CAP):
        slot_copy(zero_ref, s).wait()


def per_device(grads, block_owner, owner_counts):
    block_count, row_count, block_width = grads.shape
    z_size = lax.axis_size("z")
    total_rows = row_count * lax.axis_size("x") * z_size * lax.axis_size("c")
    sizes = [lax.axis_size(name) for name in ALL]

    def device(x, z, c, m):
        return ((x * sizes[1] + z) * sizes[2] + c) * sizes[3] + m

    groups = [
        [device((b // 2) ^ (m // 4), z, b % 2, m) for b in range(NB)]
        for z in range(sizes[1])
        for m in range(sizes[3])
    ]
    held = lax.all_to_all(grads, ALL, 0, 0, tiled=True, axis_index_groups=groups)
    packed = pl.pallas_call(
        gram_kernel,
        out_shape=jax.ShapeDtypeStruct((CHUNKS, SENT_ROWS, TILE), jnp.bfloat16),
        in_specs=[VMEM],
        out_specs=VMEM,
        compiler_params=PARAMS,
        name="gram",
    )(held)
    parts = lax.all_to_all(packed, "z", 0, 0, tiled=True)
    trace = pl.pallas_call(
        trace_kernel,
        out_shape=jax.ShapeDtypeStruct((8, TILE), jnp.float32),
        in_specs=[VMEM],
        out_specs=VMEM,
        compiler_params=PARAMS,
        name="trace",
    )(parts)
    pairs = [
        (device(x, z, c, m), device(x ^ (z // 4 % 2), z, c ^ (z // 8), m ^ (z % 8)))
        for x in range(sizes[0])
        for z in range(sizes[1])
        for c in range(sizes[2])
        for m in range(sizes[3])
    ]
    passed = lax.ppermute(trace, ALL, pairs)
    copies = pl.pallas_call(
        sum_kernel,
        out_shape=jax.ShapeDtypeStruct((CHUNKS, SENT_ROWS, TILE), jnp.bfloat16),
        in_specs=[VMEM] * 2,
        out_specs=VMEM,
        compiler_params=PARAMS,
        name="sum",
    )(parts, passed)
    chunks = lax.all_to_all(copies, "z", 0, 0, tiled=True)
    packed_normal = pl.pallas_call(
        lambda *refs: normal_kernel(total_rows, lax.axis_size("m") * BPL, *refs),
        out_shape=jax.ShapeDtypeStruct((PACKED_ROWS, TILE), jnp.bfloat16),
        in_specs=[VMEM],
        out_specs=VMEM,
        compiler_params=PARAMS,
        name="normal",
    )(chunks)
    swap = [(0, 1), (1, 0)]
    packed_across = lax.ppermute(packed_normal, "x", swap)
    block_rows = (row_count, block_width)
    factor, own_rows = pl.pallas_call(
        own_root_kernel,
        out_shape=(
            jax.ShapeDtypeStruct((block_width, block_width), jnp.bfloat16),
            jax.ShapeDtypeStruct(block_rows, jnp.bfloat16),
        ),
        in_specs=[VMEM] * 2,
        out_specs=(VMEM, VMEM),
        scratch_shapes=[pltpu.VMEM((block_width, block_width), jnp.bfloat16)],
        compiler_params=PARAMS,
        cost_estimate=pl.CostEstimate(flops=16 * block_width**3, bytes_accessed=2**20, transcendentals=0),
        name="own_root",
    )(packed_normal, grads)
    beside = lax.ppermute(factor, "c", swap)
    across = root(packed_across, block_width)
    both = lax.ppermute(across, "c", swap)
    rows = pl.pallas_call(
        rows_kernel,
        out_shape=jax.ShapeDtypeStruct((2,) + block_rows, jnp.bfloat16),
        in_specs=[VMEM] * 3,
        out_specs=VMEM,
        compiler_params=PARAMS,
        cost_estimate=pl.CostEstimate(flops=10**9, bytes_accessed=2**20, transcendentals=0),
        name="rows",
    )(grads, beside, across)
    preconditioned, owned = pl.pallas_call(
        apply_kernel,
        out_shape=(
            jax.ShapeDtypeStruct((block_count, row_count, block_width), jnp.bfloat16),
            jax.ShapeDtypeStruct((1, CAP, block_width, block_width), jnp.bfloat16),
        ),
        in_specs=[SMEM, SMEM] + [VMEM] * 7,
        out_specs=(HBM, HBM),
        scratch_shapes=[
            pltpu.VMEM(block_rows, jnp.bfloat16),
            pltpu.VMEM((block_width, block_width), jnp.bfloat16),
            pltpu.SemaphoreType.DMA((block_count,)),
            pltpu.SemaphoreType.DMA((CAP,)),
        ],
        compiler_params=PARAMS,
        name="apply",
    )(block_owner, owner_counts, grads, own_rows, rows, factor, beside, across, both)
    return preconditioned, owned


def solution(mesh):
    fine = Mesh(mesh.devices.reshape(2, 16, 2, 8), ("x", "z", "c", "m"))
    dp = ("x", "z", "c")
    return jax.shard_map(
        per_device,
        mesh=fine,
        in_specs=(P("m", dp, None), P("m", None), P("m", dp)),
        out_specs=(P("m", dp, None), P("m", dp, None, None)),
        check_vma=False,
    )
```

```python
import jax
import jax.numpy as jnp
from jax import lax
from jax.experimental import pallas as pl
from jax.experimental.pallas import tpu as pltpu
from jax.sharding import Mesh
from jax.sharding import PartitionSpec as P

LAYERS = 2
BPL = 2
CAP = 3
ITERS = 3
NB = 4
TILE = 128
CHUNKS = 16
HALF = 64
SENT_ROWS = 72
TILES = 8
PACKED_ROWS = TILES * TILE + 16

eps_rel = 0.1

ALL = ("x", "z", "c", "m")
VMEM = pl.BlockSpec(memory_space=pltpu.VMEM)
SMEM = pl.BlockSpec(memory_space=pltpu.SMEM)
HBM = pl.BlockSpec(memory_space=pl.ANY)
PARAMS = pltpu.CompilerParams(vmem_limit_bytes=40 * 1024 * 1024)
OFF_TILES = ((0, 1), (0, 2), (0, 3), (1, 2), (1, 3), (2, 3))
PAIRS = OFF_TILES + ((0, 1), (2, 3))
DIAGONAL_CHUNK = (0, 1, 2, 4)


def row_col():
    rows = lax.broadcasted_iota(jnp.int32, (TILE, TILE), 0)
    cols = lax.broadcasted_iota(jnp.int32, (TILE, TILE), 1)
    return rows, cols


def pieces(value):
    high = value.astype(jnp.bfloat16).astype(jnp.float32)
    middle = (value - high).astype(jnp.bfloat16).astype(jnp.float32)
    return [high, middle, value - high - middle]


def spread_scale(source):
    rows = lax.broadcasted_iota(jnp.int32, (HALF, TILE), 0)
    return 1.0 + ((rows * 37 + source * 11) & (HALF - 1)).astype(jnp.float32) / HALF


def extra_rows(values):
    rows = lax.broadcasted_iota(jnp.int32, (8, TILE), 0)
    extra = jnp.zeros((8, TILE), jnp.float32)
    for row, value in enumerate(values):
        extra = jnp.where(rows == row, value, extra)
    return extra


def read_extra(chunk, first, count):
    rows = lax.broadcasted_iota(jnp.int32, (8, TILE), 0)
    chosen = jnp.where((rows >= first) & (rows < first + count), chunk[HALF:], 0.0)
    return jnp.sum(chosen, axis=0, keepdims=True)


def down(row):
    return jnp.broadcast_to(row, (TILE, TILE)).T


def gram_kernel(grads_ref, out_ref):
    scale = spread_scale(lax.axis_index("z"))
    gradient = grads_ref[...].reshape(-1, grads_ref.shape[2])
    strips = []
    for i in range(4):
        strips.append(
            lax.dot_general(
                gradient[:, i * TILE : (i + 1) * TILE],
                gradient[:, i * TILE :],
                (((0,), (0,)), ((), ())),
                preferred_element_type=jnp.float32,
            )
        )
    rows, cols = row_col()

    def tile(i, j):
        return strips[i][:, (j - i) * TILE : (j - i + 1) * TILE]

    tiles = [tile(i, j) for i, j in OFF_TILES]
    for i in (0, 2):
        tiles.append(jnp.where(rows < cols, tile(i, i), tile(i + 1, i + 1)))
    diagonals = [
        jnp.sum(jnp.where(rows == cols, tile(i, i), 0.0), axis=0, keepdims=True) for i in range(4)
    ]
    trace = diagonals[0] + diagonals[1] + diagonals[2] + diagonals[3]
    for k in range(CHUNKS):
        half = tiles[k // 2][(k % 2) * HALF : (k % 2 + 1) * HALF]
        first, second = PAIRS[k // 2]
        extra = extra_rows(pieces(diagonals[first]) + pieces(diagonals[second]) + pieces(trace)[:2])
        out_ref[k] = jnp.concatenate([half * scale, extra], axis=0).astype(jnp.bfloat16)


def trace_kernel(parts_ref, trace_ref):
    trace = jnp.zeros((1, TILE), jnp.float32)
    for k in range(CHUNKS):
        trace = trace + read_extra(parts_ref[k].astype(jnp.float32), 6, 2)
    trace_ref[...] = jnp.broadcast_to(trace, (8, TILE))


def zero_kernel(trace_ref, own_ref, done_ref, zero_ref, sem):
    done_ref[...] = trace_ref[...]
    zero_ref[...] = jnp.zeros_like(zero_ref)
    copies = [pltpu.make_async_copy(zero_ref, own_ref.at[0, s], sem.at[s]) for s in range(CAP)]
    for copy in copies:
        copy.start()
    for copy in copies:
        copy.wait()


def sum_kernel(parts_ref, trace_ref, done_ref, out_ref):
    total = jnp.zeros((HALF, TILE), jnp.float32)
    first = jnp.zeros((1, TILE), jnp.float32)
    second = jnp.zeros((1, TILE), jnp.float32)
    for k in range(CHUNKS):
        chunk = parts_ref[k].astype(jnp.float32)
        total = total + chunk[:HALF] / spread_scale(k)
        first = first + read_extra(chunk, 0, 3)
        second = second + read_extra(chunk, 3, 3)
    z = lax.axis_index("z")
    merged = z >= 2 * len(OFF_TILES)
    lower_half = (z & 1) == 1
    cols = lax.broadcasted_iota(jnp.int32, (HALF, TILE), 1)
    rows = lax.broadcasted_iota(jnp.int32, (HALF, TILE), 0) + HALF * (z & 1)
    first_root, second_root = jnp.sqrt(first), jnp.sqrt(second)

    def half_down(row):
        tile = down(row)
        return jnp.where(lower_half, tile[HALF:], tile[:HALF])

    first_down, second_down = half_down(first_root), half_down(second_root)
    outer = jnp.where(
        merged,
        jnp.where(rows < cols, first_down * first_root, second_down * second_root),
        first_down * second_root,
    )
    valid = jnp.where(merged & (rows == cols), 0.0, outer)

    def sum_all(value):
        return jnp.sum(jnp.sum(value, axis=0, keepdims=True), axis=1, keepdims=True)

    alpha = sum_all(total * valid) / jnp.maximum(sum_all(valid * valid), 1e-30)
    alpha = pieces(jnp.broadcast_to(alpha, (1, TILE)))[:2]
    rest = (total - (alpha[0] + alpha[1]) * outer) * spread_scale(CHUNKS)
    diagonal = jnp.where(z == DIAGONAL_CHUNK[0], first, second)
    extra = extra_rows(pieces(diagonal) + pieces(trace_ref[0:1])[:2] + alpha)
    rest = jnp.concatenate([rest, extra], axis=0).astype(jnp.bfloat16)
    for k in range(CHUNKS):
        out_ref[k] = rest


def normal_kernel(total_rows, layer_blocks, chunks_ref, out_ref):
    width = 4 * TILE
    rows, cols = row_col()
    scale = 1.0 / total_rows
    chunks = [chunks_ref[k].astype(jnp.float32) for k in range(CHUNKS)]
    traces = jnp.zeros((1, TILE), jnp.float32)
    for k in range(CHUNKS):
        traces = traces + read_extra(chunks[k], 3, 2)
    layer_sum = jnp.sum(traces, axis=1, keepdims=True) * scale
    spread = spread_scale(CHUNKS)
    diagonals = [read_extra(chunks[DIAGONAL_CHUNK[i]], 0, 3) for i in range(4)]
    roots = [jnp.sqrt(diagonal) for diagonal in diagonals]
    roots_down = [down(root) for root in roots]
    damping = layer_sum * (eps_rel / (layer_blocks * width))
    tiles = []
    square_sum = jnp.zeros((TILE, TILE), jnp.float32)
    for t in range(TILES):
        first, second = PAIRS[t]
        if t < len(OFF_TILES):
            outer = roots_down[first] * roots[second]
        else:
            outer = jnp.where(
                rows < cols, roots_down[first] * roots[first], roots_down[second] * roots[second]
            )
        halves = []
        for h in range(2):
            chunk = chunks[2 * t + h]
            alpha = read_extra(chunk, 5, 2)
            halves.append((chunk[:HALF] / spread + alpha * outer[h * HALF : (h + 1) * HALF]) * scale)
        tile = jnp.concatenate(halves, axis=0)
        if t >= len(OFF_TILES):
            tile = jnp.where(rows == cols, 0.0, tile)
        tiles.append(tile)
        square_sum = square_sum + tile * tile
    diagonals = [diagonal * scale + damping for diagonal in diagonals]
    by_lane = 2.0 * jnp.sum(square_sum, axis=0, keepdims=True)
    for diagonal in diagonals:
        by_lane = by_lane + diagonal * diagonal
    norm_scale = jnp.sqrt(jnp.sum(by_lane, axis=1, keepdims=True))
    root_scale = 1.0 / jnp.sqrt(jnp.sqrt(norm_scale))
    for t in range(TILES):
        out_ref[t * TILE : (t + 1) * TILE] = (tiles[t] / norm_scale).astype(jnp.bfloat16)
    row16 = lax.broadcasted_iota(jnp.int32, (16, TILE), 0)
    extra = jnp.zeros((16, TILE), jnp.float32)
    for row, value in enumerate([diagonal / norm_scale for diagonal in diagonals] + pieces(root_scale)):
        extra = jnp.where(row16 == row, value, extra)
    out_ref[TILES * TILE :] = extra.astype(jnp.bfloat16)


def root_kernel(packed_ref, factor_ref, normal_ref):
    width = factor_ref.shape[0]
    rows, cols = row_col()
    extra = packed_ref[TILES * TILE :].astype(jnp.float32)
    root_scale = (extra[4:5] + extra[5:6] + extra[6:7])[:, 0:1]

    def stored(t):
        return packed_ref[t * TILE : (t + 1) * TILE].astype(jnp.float32)

    for t, (i, j) in enumerate(OFF_TILES):
        value = stored(t)
        normal_ref[i * TILE : (i + 1) * TILE, j * TILE : (j + 1) * TILE] = value.astype(jnp.bfloat16)
        normal_ref[j * TILE : (j + 1) * TILE, i * TILE : (i + 1) * TILE] = value.T.astype(jnp.bfloat16)
    for i in range(4):
        value = stored(len(OFF_TILES) + i // 2)
        value = jnp.where(rows < cols if i % 2 == 0 else rows > cols, value, 0.0)
        value = jnp.where(rows == cols, extra[i : i + 1], value + value.T)
        normal_ref[i * TILE : (i + 1) * TILE, i * TILE : (i + 1) * TILE] = value.astype(jnp.bfloat16)
    eye_rows = lax.broadcasted_iota(jnp.int32, (width, width), 0)
    eye_cols = lax.broadcasted_iota(jnp.int32, (width, width), 1)
    five = jnp.where(eye_rows == eye_cols, 5.0, 0.0)

    def mm(a, b):
        return jnp.dot(a, b, preferred_element_type=jnp.float32).astype(jnp.bfloat16)

    current = normal_ref[...]
    factor = None
    for iteration in range(ITERS):
        step = ((five - current.astype(jnp.float32)) * 0.25).astype(jnp.bfloat16)
        if iteration == 0:
            factor = (root_scale * step.astype(jnp.float32)).astype(jnp.bfloat16)
        else:
            factor = mm(factor, step)
        if iteration + 1 < ITERS:
            square = mm(step, step)
            fourth = mm(square, square)
            current = mm(fourth, current)
    factor_ref[...] = factor


def block_of(k):
    quad = (lax.axis_index("x") ^ (lax.axis_index("m") >> 2)) * 2 + lax.axis_index("c")
    return quad ^ k


def product(grads_ref, factor, k):
    rows = jnp.dot(grads_ref[block_of(k)], factor, preferred_element_type=jnp.float32)
    return rows.astype(jnp.bfloat16)


def own_root_kernel(packed_ref, grads_ref, factor_ref, rows_ref, normal_ref):
    root_kernel(packed_ref, factor_ref, normal_ref)
    rows_ref[...] = product(grads_ref, factor_ref[...], 0)


def rows_kernel(grads_ref, f1_ref, f2_ref, rows_ref):
    for k, ref in ((1, f1_ref), (2, f2_ref)):
        rows_ref[k - 1] = product(grads_ref, ref[...], k)


def root(packed, width):
    return pl.pallas_call(
        root_kernel,
        out_shape=jax.ShapeDtypeStruct((width, width), jnp.bfloat16),
        in_specs=[VMEM],
        out_specs=VMEM,
        scratch_shapes=[pltpu.VMEM((width, width), jnp.bfloat16)],
        compiler_params=PARAMS,
        cost_estimate=pl.CostEstimate(flops=16 * width**3, bytes_accessed=4 * width * width, transcendentals=0),
        name="root",
    )(packed)


def apply_kernel(
    owner_ref,
    count_ref,
    grads_ref,
    own_rows_ref,
    rows_ref,
    f0_ref,
    f1_ref,
    f2_ref,
    f3_ref,
    empty_ref,
    pre_ref,
    own_ref,
    last_ref,
    pre_sem,
    own_sem,
):
    quad = block_of(0)
    mine = (lax.axis_index("x") * lax.axis_size("z") + lax.axis_index("z")) * 2 + lax.axis_index("c")
    factors = (f0_ref, f1_ref, f2_ref, f3_ref)

    def rows_copy(source, k):
        return pltpu.make_async_copy(source, pre_ref.at[block_of(k)], pre_sem.at[k])

    ready = [(0, own_rows_ref), (1, rows_ref.at[0]), (2, rows_ref.at[1])]
    copies = [rows_copy(source, k) for k, source in ready]
    for copy in copies:
        copy.start()
    owners = [owner_ref[0, j] for j in range(NB)]
    slots = []
    for j in range(NB):
        slot = jnp.int32(0)
        for i in range(j):
            slot = slot + (owners[i] == owners[j]).astype(jnp.int32)
        slots.append(slot)

    def slot_copy(source, s):
        return pltpu.make_async_copy(source, own_ref.at[0, s], own_sem.at[s])

    choice = []
    for s in range(CAP):
        chosen = jnp.int32(-1)
        for j in range(NB):
            held = (owners[j] == mine) & (slots[j] == s) & (s < count_ref[0, 0])
            chosen = jnp.where(held, j ^ quad, chosen)
        choice.append(chosen)
        for k, ref in enumerate(factors):

            @pl.when(chosen == k)
            def _():
                slot_copy(ref, s).start()

    last_ref[...] = product(grads_ref, f3_ref[...], 3)
    copies.append(rows_copy(last_ref, 3))
    copies[-1].start()
    for copy in copies:
        copy.wait()
    for s in range(CAP):

        @pl.when(choice[s] >= 0)
        def _():
            slot_copy(f0_ref, s).wait()


def per_device(grads, block_owner, owner_counts):
    block_count, row_count, block_width = grads.shape
    z_size = lax.axis_size("z")
    total_rows = row_count * lax.axis_size("x") * z_size * lax.axis_size("c")
    sizes = [lax.axis_size(name) for name in ALL]

    def device(x, z, c, m):
        return ((x * sizes[1] + z) * sizes[2] + c) * sizes[3] + m

    groups = [
        [device((b // 2) ^ (m // 4), z, b % 2, m) for b in range(NB)]
        for z in range(sizes[1])
        for m in range(sizes[3])
    ]
    held = lax.all_to_all(grads, ALL, 0, 0, tiled=True, axis_index_groups=groups)
    packed = pl.pallas_call(
        gram_kernel,
        out_shape=jax.ShapeDtypeStruct((CHUNKS, SENT_ROWS, TILE), jnp.bfloat16),
        in_specs=[VMEM],
        out_specs=VMEM,
        compiler_params=PARAMS,
        name="gram",
    )(held)
    parts = lax.all_to_all(packed, "z", 0, 0, tiled=True)
    trace = pl.pallas_call(
        trace_kernel,
        out_shape=jax.ShapeDtypeStruct((8, TILE), jnp.float32),
        in_specs=[VMEM],
        out_specs=VMEM,
        compiler_params=PARAMS,
        name="trace",
    )(parts)
    pairs = [
        (device(x, z, c, m), device(x ^ (z // 4 % 2), z, c ^ (z // 8), m ^ (z % 8)))
        for x in range(sizes[0])
        for z in range(sizes[1])
        for c in range(sizes[2])
        for m in range(sizes[3])
    ]
    passed = lax.ppermute(trace, ALL, pairs)
    slots = jax.ShapeDtypeStruct((1, CAP, block_width, block_width), jnp.bfloat16)
    empty, done = pl.pallas_call(
        zero_kernel,
        out_shape=(slots, jax.ShapeDtypeStruct(trace.shape, trace.dtype)),
        in_specs=[VMEM],
        out_specs=(HBM, VMEM),
        scratch_shapes=[
            pltpu.VMEM((block_width, block_width), jnp.bfloat16),
            pltpu.SemaphoreType.DMA((CAP,)),
        ],
        compiler_params=PARAMS,
        cost_estimate=pl.CostEstimate(flops=0, bytes_accessed=4 * 10**6, transcendentals=0),
        name="empty",
    )(trace)
    copies = pl.pallas_call(
        sum_kernel,
        out_shape=jax.ShapeDtypeStruct((CHUNKS, SENT_ROWS, TILE), jnp.bfloat16),
        in_specs=[VMEM] * 3,
        out_specs=VMEM,
        compiler_params=PARAMS,
        name="sum",
    )(parts, passed, done)
    chunks = lax.all_to_all(copies, "z", 0, 0, tiled=True)
    packed_normal = pl.pallas_call(
        lambda *refs: normal_kernel(total_rows, lax.axis_size("m") * BPL, *refs),
        out_shape=jax.ShapeDtypeStruct((PACKED_ROWS, TILE), jnp.bfloat16),
        in_specs=[VMEM],
        out_specs=VMEM,
        compiler_params=PARAMS,
        name="normal",
    )(chunks)
    swap = [(0, 1), (1, 0)]
    packed_across = lax.ppermute(packed_normal, "x", swap)
    block_rows = (row_count, block_width)
    factor, own_rows = pl.pallas_call(
        own_root_kernel,
        out_shape=(
            jax.ShapeDtypeStruct((block_width, block_width), jnp.bfloat16),
            jax.ShapeDtypeStruct(block_rows, jnp.bfloat16),
        ),
        in_specs=[VMEM] * 2,
        out_specs=(VMEM, VMEM),
        scratch_shapes=[pltpu.VMEM((block_width, block_width), jnp.bfloat16)],
        compiler_params=PARAMS,
        cost_estimate=pl.CostEstimate(flops=16 * block_width**3, bytes_accessed=2**20, transcendentals=0),
        name="own_root",
    )(packed_normal, grads)
    beside = lax.ppermute(factor, "c", swap)
    across = root(packed_across, block_width)
    both = lax.ppermute(across, "c", swap)
    rows = pl.pallas_call(
        rows_kernel,
        out_shape=jax.ShapeDtypeStruct((2,) + block_rows, jnp.bfloat16),
        in_specs=[VMEM] * 3,
        out_specs=VMEM,
        compiler_params=PARAMS,
        cost_estimate=pl.CostEstimate(flops=10**9, bytes_accessed=2**20, transcendentals=0),
        name="rows",
    )(grads, beside, across)
    preconditioned, owned = pl.pallas_call(
        apply_kernel,
        out_shape=(
            jax.ShapeDtypeStruct((block_count, row_count, block_width), jnp.bfloat16),
            slots,
        ),
        in_specs=[SMEM, SMEM] + [VMEM] * 7 + [HBM],
        out_specs=(HBM, HBM),
        scratch_shapes=[
            pltpu.VMEM(block_rows, jnp.bfloat16),
            pltpu.SemaphoreType.DMA((block_count,)),
            pltpu.SemaphoreType.DMA((CAP,)),
        ],
        input_output_aliases={9: 1},
        compiler_params=PARAMS,
        name="apply",
    )(block_owner, owner_counts, grads, own_rows, rows, factor, beside, across, both, empty)
    return preconditioned, owned


def solution(mesh):
    fine = Mesh(mesh.devices.reshape(2, 16, 2, 8), ("x", "z", "c", "m"))
    dp = ("x", "z", "c")
    return jax.shard_map(
        per_device,
        mesh=fine,
        in_specs=(P("m", dp, None), P("m", None), P("m", dp)),
        out_specs=(P("m", dp, None), P("m", dp, None, None)),
        check_vma=False,
    )
```

```python
import jax
import jax.numpy as jnp
from jax import lax
from jax.experimental import pallas as pl
from jax.experimental.pallas import tpu as pltpu
from jax.sharding import Mesh
from jax.sharding import PartitionSpec as P

LAYERS = 2
BPL = 2
CAP = 3
ITERS = 3
NB = 4
TILE = 128
CHUNKS = 16
HALF = 64
SENT_ROWS = 72
TILES = 8
PACKED_ROWS = TILES * TILE + 16

eps_rel = 0.1

ALL = ("x", "z", "c", "m")
VMEM = pl.BlockSpec(memory_space=pltpu.VMEM)
SMEM = pl.BlockSpec(memory_space=pltpu.SMEM)
HBM = pl.BlockSpec(memory_space=pl.ANY)
PARAMS = pltpu.CompilerParams(vmem_limit_bytes=40 * 1024 * 1024)
OFF_TILES = ((0, 1), (0, 2), (0, 3), (1, 2), (1, 3), (2, 3))
PAIRS = OFF_TILES + ((0, 1), (2, 3))
DIAGONAL_CHUNK = (0, 1, 2, 4)


def row_col():
    rows = lax.broadcasted_iota(jnp.int32, (TILE, TILE), 0)
    cols = lax.broadcasted_iota(jnp.int32, (TILE, TILE), 1)
    return rows, cols


def pieces(value):
    high = value.astype(jnp.bfloat16).astype(jnp.float32)
    middle = (value - high).astype(jnp.bfloat16).astype(jnp.float32)
    return [high, middle, value - high - middle]


def spread_scale(source):
    rows = lax.broadcasted_iota(jnp.int32, (HALF, TILE), 0)
    return 1.0 + ((rows * 37 + source * 11) & (HALF - 1)).astype(jnp.float32) / HALF


def extra_rows(values):
    rows = lax.broadcasted_iota(jnp.int32, (8, TILE), 0)
    extra = jnp.zeros((8, TILE), jnp.float32)
    for row, value in enumerate(values):
        extra = jnp.where(rows == row, value, extra)
    return extra


def read_extra(chunk, first, count):
    rows = lax.broadcasted_iota(jnp.int32, (8, TILE), 0)
    chosen = jnp.where((rows >= first) & (rows < first + count), chunk[HALF:], 0.0)
    return jnp.sum(chosen, axis=0, keepdims=True)


def down(row):
    return jnp.broadcast_to(row, (TILE, TILE)).T


def gram_kernel(grads_ref, out_ref):
    scale = spread_scale(lax.axis_index("z"))
    gradient = grads_ref[...].reshape(-1, grads_ref.shape[2])
    strips = []
    for i in range(4):
        strips.append(
            lax.dot_general(
                gradient[:, i * TILE : (i + 1) * TILE],
                gradient[:, i * TILE :],
                (((0,), (0,)), ((), ())),
                preferred_element_type=jnp.float32,
            )
        )
    rows, cols = row_col()

    def tile(i, j):
        return strips[i][:, (j - i) * TILE : (j - i + 1) * TILE]

    tiles = [tile(i, j) for i, j in OFF_TILES]
    for i in (0, 2):
        tiles.append(jnp.where(rows < cols, tile(i, i), tile(i + 1, i + 1)))
    diagonals = [
        jnp.sum(jnp.where(rows == cols, tile(i, i), 0.0), axis=0, keepdims=True) for i in range(4)
    ]
    trace = diagonals[0] + diagonals[1] + diagonals[2] + diagonals[3]
    for k in range(CHUNKS):
        half = tiles[k // 2][(k % 2) * HALF : (k % 2 + 1) * HALF]
        first, second = PAIRS[k // 2]
        extra = extra_rows(pieces(diagonals[first]) + pieces(diagonals[second]) + pieces(trace)[:2])
        out_ref[k] = jnp.concatenate([half * scale, extra], axis=0).astype(jnp.bfloat16)


def trace_kernel(parts_ref, trace_ref):
    trace = jnp.zeros((1, TILE), jnp.float32)
    for k in range(CHUNKS):
        trace = trace + read_extra(parts_ref[k].astype(jnp.float32), 6, 2)
    trace_ref[...] = jnp.broadcast_to(trace, (8, TILE))


def sum_kernel(parts_ref, trace_ref, own_ref, out_ref, zero_ref, sem):
    zero_ref[...] = jnp.zeros_like(zero_ref)
    copies = [pltpu.make_async_copy(zero_ref, own_ref.at[0, s], sem.at[s]) for s in range(CAP)]
    for copy in copies:
        copy.start()
    total = jnp.zeros((HALF, TILE), jnp.float32)
    first = jnp.zeros((1, TILE), jnp.float32)
    second = jnp.zeros((1, TILE), jnp.float32)
    for k in range(CHUNKS):
        chunk = parts_ref[k].astype(jnp.float32)
        total = total + chunk[:HALF] / spread_scale(k)
        first = first + read_extra(chunk, 0, 3)
        second = second + read_extra(chunk, 3, 3)
    z = lax.axis_index("z")
    merged = z >= 2 * len(OFF_TILES)
    lower_half = (z & 1) == 1
    cols = lax.broadcasted_iota(jnp.int32, (HALF, TILE), 1)
    rows = lax.broadcasted_iota(jnp.int32, (HALF, TILE), 0) + HALF * (z & 1)
    first_root, second_root = jnp.sqrt(first), jnp.sqrt(second)

    def half_down(row):
        tile = down(row)
        return jnp.where(lower_half, tile[HALF:], tile[:HALF])

    first_down, second_down = half_down(first_root), half_down(second_root)
    outer = jnp.where(
        merged,
        jnp.where(rows < cols, first_down * first_root, second_down * second_root),
        first_down * second_root,
    )
    valid = jnp.where(merged & (rows == cols), 0.0, outer)

    def sum_all(value):
        return jnp.sum(jnp.sum(value, axis=0, keepdims=True), axis=1, keepdims=True)

    alpha = sum_all(total * valid) / jnp.maximum(sum_all(valid * valid), 1e-30)
    alpha = pieces(jnp.broadcast_to(alpha, (1, TILE)))[:2]
    rest = (total - (alpha[0] + alpha[1]) * outer) * spread_scale(CHUNKS)
    diagonal = jnp.where(z == DIAGONAL_CHUNK[0], first, second)
    free = jnp.zeros((1, TILE), jnp.float32)
    out_ref[:HALF] = rest
    out_ref[HALF:] = extra_rows(pieces(diagonal) + [free, free] + alpha)
    for copy in copies:
        copy.wait()


def message_kernel(chunk_ref, trace_ref, out_ref):
    free = jnp.zeros((1, TILE), jnp.float32)
    extra = chunk_ref[HALF:] + extra_rows([free] * 3 + pieces(trace_ref[0:1])[:2])
    message = jnp.concatenate([chunk_ref[:HALF], extra], axis=0).astype(jnp.bfloat16)
    for k in range(CHUNKS):
        out_ref[k] = message


def normal_kernel(total_rows, layer_blocks, chunks_ref, out_ref):
    width = 4 * TILE
    rows, cols = row_col()
    scale = 1.0 / total_rows
    chunks = [chunks_ref[k].astype(jnp.float32) for k in range(CHUNKS)]
    traces = jnp.zeros((1, TILE), jnp.float32)
    for k in range(CHUNKS):
        traces = traces + read_extra(chunks[k], 3, 2)
    layer_sum = jnp.sum(traces, axis=1, keepdims=True) * scale
    spread = spread_scale(CHUNKS)
    diagonals = [read_extra(chunks[DIAGONAL_CHUNK[i]], 0, 3) for i in range(4)]
    roots = [jnp.sqrt(diagonal) for diagonal in diagonals]
    roots_down = [down(root) for root in roots]
    damping = layer_sum * (eps_rel / (layer_blocks * width))
    tiles = []
    square_sum = jnp.zeros((TILE, TILE), jnp.float32)
    for t in range(TILES):
        first, second = PAIRS[t]
        if t < len(OFF_TILES):
            outer = roots_down[first] * roots[second]
        else:
            outer = jnp.where(
                rows < cols, roots_down[first] * roots[first], roots_down[second] * roots[second]
            )
        halves = []
        for h in range(2):
            chunk = chunks[2 * t + h]
            alpha = read_extra(chunk, 5, 2)
            halves.append((chunk[:HALF] / spread + alpha * outer[h * HALF : (h + 1) * HALF]) * scale)
        tile = jnp.concatenate(halves, axis=0)
        if t >= len(OFF_TILES):
            tile = jnp.where(rows == cols, 0.0, tile)
        tiles.append(tile)
        square_sum = square_sum + tile * tile
    diagonals = [diagonal * scale + damping for diagonal in diagonals]
    by_lane = 2.0 * jnp.sum(square_sum, axis=0, keepdims=True)
    for diagonal in diagonals:
        by_lane = by_lane + diagonal * diagonal
    norm_scale = jnp.sqrt(jnp.sum(by_lane, axis=1, keepdims=True))
    root_scale = 1.0 / jnp.sqrt(jnp.sqrt(norm_scale))
    for t in range(TILES):
        out_ref[t * TILE : (t + 1) * TILE] = (tiles[t] / norm_scale).astype(jnp.bfloat16)
    row16 = lax.broadcasted_iota(jnp.int32, (16, TILE), 0)
    extra = jnp.zeros((16, TILE), jnp.float32)
    for row, value in enumerate([diagonal / norm_scale for diagonal in diagonals] + pieces(root_scale)):
        extra = jnp.where(row16 == row, value, extra)
    out_ref[TILES * TILE :] = extra.astype(jnp.bfloat16)


def root_kernel(packed_ref, factor_ref, normal_ref):
    width = factor_ref.shape[0]
    rows, cols = row_col()
    extra = packed_ref[TILES * TILE :].astype(jnp.float32)
    root_scale = (extra[4:5] + extra[5:6] + extra[6:7])[:, 0:1]

    def stored(t):
        return packed_ref[t * TILE : (t + 1) * TILE].astype(jnp.float32)

    for t, (i, j) in enumerate(OFF_TILES):
        value = stored(t)
        normal_ref[i * TILE : (i + 1) * TILE, j * TILE : (j + 1) * TILE] = value.astype(jnp.bfloat16)
        normal_ref[j * TILE : (j + 1) * TILE, i * TILE : (i + 1) * TILE] = value.T.astype(jnp.bfloat16)
    for i in range(4):
        value = stored(len(OFF_TILES) + i // 2)
        value = jnp.where(rows < cols if i % 2 == 0 else rows > cols, value, 0.0)
        value = jnp.where(rows == cols, extra[i : i + 1], value + value.T)
        normal_ref[i * TILE : (i + 1) * TILE, i * TILE : (i + 1) * TILE] = value.astype(jnp.bfloat16)
    eye_rows = lax.broadcasted_iota(jnp.int32, (width, width), 0)
    eye_cols = lax.broadcasted_iota(jnp.int32, (width, width), 1)
    five = jnp.where(eye_rows == eye_cols, 5.0, 0.0)

    def mm(a, b):
        return jnp.dot(a, b, preferred_element_type=jnp.float32).astype(jnp.bfloat16)

    current = normal_ref[...]
    factor = None
    for iteration in range(ITERS):
        step = ((five - current.astype(jnp.float32)) * 0.25).astype(jnp.bfloat16)
        if iteration == 0:
            factor = (root_scale * step.astype(jnp.float32)).astype(jnp.bfloat16)
        else:
            factor = mm(factor, step)
        if iteration + 1 < ITERS:
            square = mm(step, step)
            fourth = mm(square, square)
            current = mm(fourth, current)
    factor_ref[...] = factor


def block_of(k):
    quad = (lax.axis_index("x") ^ (lax.axis_index("m") >> 2)) * 2 + lax.axis_index("c")
    return quad ^ k


def product(grads_ref, factor, k):
    rows = jnp.dot(grads_ref[block_of(k)], factor, preferred_element_type=jnp.float32)
    return rows.astype(jnp.bfloat16)


def own_root_kernel(packed_ref, grads_ref, factor_ref, rows_ref, normal_ref):
    root_kernel(packed_ref, factor_ref, normal_ref)
    rows_ref[...] = product(grads_ref, factor_ref[...], 0)


def rows_kernel(grads_ref, f1_ref, f2_ref, rows_ref):
    for k, ref in ((1, f1_ref), (2, f2_ref)):
        rows_ref[k - 1] = product(grads_ref, ref[...], k)


def root(packed, width):
    return pl.pallas_call(
        root_kernel,
        out_shape=jax.ShapeDtypeStruct((width, width), jnp.bfloat16),
        in_specs=[VMEM],
        out_specs=VMEM,
        scratch_shapes=[pltpu.VMEM((width, width), jnp.bfloat16)],
        compiler_params=PARAMS,
        cost_estimate=pl.CostEstimate(flops=16 * width**3, bytes_accessed=4 * width * width, transcendentals=0),
        name="root",
    )(packed)


def apply_kernel(
    owner_ref,
    count_ref,
    grads_ref,
    own_rows_ref,
    rows_ref,
    f0_ref,
    f1_ref,
    f2_ref,
    f3_ref,
    empty_ref,
    pre_ref,
    own_ref,
    last_ref,
    pre_sem,
    own_sem,
):
    quad = block_of(0)
    mine = (lax.axis_index("x") * lax.axis_size("z") + lax.axis_index("z")) * 2 + lax.axis_index("c")
    factors = (f0_ref, f1_ref, f2_ref, f3_ref)

    def rows_copy(source, k):
        return pltpu.make_async_copy(source, pre_ref.at[block_of(k)], pre_sem.at[k])

    ready = [(0, own_rows_ref), (1, rows_ref.at[0]), (2, rows_ref.at[1])]
    copies = [rows_copy(source, k) for k, source in ready]
    for copy in copies:
        copy.start()
    owners = [owner_ref[0, j] for j in range(NB)]
    slots = []
    for j in range(NB):
        slot = jnp.int32(0)
        for i in range(j):
            slot = slot + (owners[i] == owners[j]).astype(jnp.int32)
        slots.append(slot)

    def slot_copy(source, s):
        return pltpu.make_async_copy(source, own_ref.at[0, s], own_sem.at[s])

    choice = []
    for s in range(CAP):
        chosen = jnp.int32(-1)
        for j in range(NB):
            held = (owners[j] == mine) & (slots[j] == s) & (s < count_ref[0, 0])
            chosen = jnp.where(held, j ^ quad, chosen)
        choice.append(chosen)
        for k, ref in enumerate(factors):

            @pl.when(chosen == k)
            def _():
                slot_copy(ref, s).start()

    last_ref[...] = product(grads_ref, f3_ref[...], 3)
    copies.append(rows_copy(last_ref, 3))
    copies[-1].start()
    for copy in copies:
        copy.wait()
    for s in range(CAP):

        @pl.when(choice[s] >= 0)
        def _():
            slot_copy(f0_ref, s).wait()


def per_device(grads, block_owner, owner_counts):
    block_count, row_count, block_width = grads.shape
    z_size = lax.axis_size("z")
    total_rows = row_count * lax.axis_size("x") * z_size * lax.axis_size("c")
    sizes = [lax.axis_size(name) for name in ALL]

    def device(x, z, c, m):
        return ((x * sizes[1] + z) * sizes[2] + c) * sizes[3] + m

    groups = [
        [device((b // 2) ^ (m // 4), z, b % 2, m) for b in range(NB)]
        for z in range(sizes[1])
        for m in range(sizes[3])
    ]
    held = lax.all_to_all(grads, ALL, 0, 0, tiled=True, axis_index_groups=groups)
    packed = pl.pallas_call(
        gram_kernel,
        out_shape=jax.ShapeDtypeStruct((CHUNKS, SENT_ROWS, TILE), jnp.bfloat16),
        in_specs=[VMEM],
        out_specs=VMEM,
        compiler_params=PARAMS,
        name="gram",
    )(held)
    parts = lax.all_to_all(packed, "z", 0, 0, tiled=True)
    trace = pl.pallas_call(
        trace_kernel,
        out_shape=jax.ShapeDtypeStruct((8, TILE), jnp.float32),
        in_specs=[VMEM],
        out_specs=VMEM,
        compiler_params=PARAMS,
        name="trace",
    )(parts)
    pairs = [
        (device(x, z, c, m), device(x ^ (z // 4 % 2), z, c ^ (z // 8), m ^ (z % 8)))
        for x in range(sizes[0])
        for z in range(sizes[1])
        for c in range(sizes[2])
        for m in range(sizes[3])
    ]
    passed = lax.ppermute(trace, ALL, pairs)
    slots = jax.ShapeDtypeStruct((1, CAP, block_width, block_width), jnp.bfloat16)
    empty, chunk = pl.pallas_call(
        sum_kernel,
        out_shape=(slots, jax.ShapeDtypeStruct((SENT_ROWS, TILE), jnp.float32)),
        in_specs=[VMEM] * 2,
        out_specs=(HBM, VMEM),
        scratch_shapes=[
            pltpu.VMEM((block_width, block_width), jnp.bfloat16),
            pltpu.SemaphoreType.DMA((CAP,)),
        ],
        compiler_params=PARAMS,
        cost_estimate=pl.CostEstimate(flops=0, bytes_accessed=4 * 10**6, transcendentals=0),
        name="sum",
    )(parts, trace)
    copies = pl.pallas_call(
        message_kernel,
        out_shape=jax.ShapeDtypeStruct((CHUNKS, SENT_ROWS, TILE), jnp.bfloat16),
        in_specs=[VMEM] * 2,
        out_specs=VMEM,
        compiler_params=PARAMS,
        name="message",
    )(chunk, passed)
    chunks = lax.all_to_all(copies, "z", 0, 0, tiled=True)
    packed_normal = pl.pallas_call(
        lambda *refs: normal_kernel(total_rows, lax.axis_size("m") * BPL, *refs),
        out_shape=jax.ShapeDtypeStruct((PACKED_ROWS, TILE), jnp.bfloat16),
        in_specs=[VMEM],
        out_specs=VMEM,
        compiler_params=PARAMS,
        name="normal",
    )(chunks)
    swap = [(0, 1), (1, 0)]
    packed_across = lax.ppermute(packed_normal, "x", swap)
    block_rows = (row_count, block_width)
    factor, own_rows = pl.pallas_call(
        own_root_kernel,
        out_shape=(
            jax.ShapeDtypeStruct((block_width, block_width), jnp.bfloat16),
            jax.ShapeDtypeStruct(block_rows, jnp.bfloat16),
        ),
        in_specs=[VMEM] * 2,
        out_specs=(VMEM, VMEM),
        scratch_shapes=[pltpu.VMEM((block_width, block_width), jnp.bfloat16)],
        compiler_params=PARAMS,
        cost_estimate=pl.CostEstimate(flops=16 * block_width**3, bytes_accessed=2**20, transcendentals=0),
        name="own_root",
    )(packed_normal, grads)
    beside = lax.ppermute(factor, "c", swap)
    across = root(packed_across, block_width)
    both = lax.ppermute(across, "c", swap)
    rows = pl.pallas_call(
        rows_kernel,
        out_shape=jax.ShapeDtypeStruct((2,) + block_rows, jnp.bfloat16),
        in_specs=[VMEM] * 3,
        out_specs=VMEM,
        compiler_params=PARAMS,
        cost_estimate=pl.CostEstimate(flops=10**9, bytes_accessed=2**20, transcendentals=0),
        name="rows",
    )(grads, beside, across)
    preconditioned, owned = pl.pallas_call(
        apply_kernel,
        out_shape=(
            jax.ShapeDtypeStruct((block_count, row_count, block_width), jnp.bfloat16),
            slots,
        ),
        in_specs=[SMEM, SMEM] + [VMEM] * 7 + [HBM],
        out_specs=(HBM, HBM),
        scratch_shapes=[
            pltpu.VMEM(block_rows, jnp.bfloat16),
            pltpu.SemaphoreType.DMA((block_count,)),
            pltpu.SemaphoreType.DMA((CAP,)),
        ],
        input_output_aliases={9: 1},
        compiler_params=PARAMS,
        name="apply",
    )(block_owner, owner_counts, grads, own_rows, rows, factor, beside, across, both, empty)
    return preconditioned, owned


def solution(mesh):
    fine = Mesh(mesh.devices.reshape(2, 16, 2, 8), ("x", "z", "c", "m"))
    dp = ("x", "z", "c")
    return jax.shard_map(
        per_device,
        mesh=fine,
        in_specs=(P("m", dp, None), P("m", None), P("m", dp)),
        out_specs=(P("m", dp, None), P("m", dp, None, None)),
        check_vma=False,
    )
```
